32 devices in a mesh: sx: 8 (over z, y), sy: 4 (over x, core).
Axes of the slice: x: 2, y: 2, z: 4, core: 2. Of those that a mesh axis runs over, the one named last changes fastest.
Arguments:
- obs_values: bfloat16 [8192, 64], P(('sx', 'sy')), may hold values from -6 to 6
- obs_dest: int32 [8192, 1], P(('sx', 'sy')), may hold values from 0 to 31; in each aligned block of 256 rows (0 to 255, 256 to 511, ...) at most 16 rows name the same one
- obs_node: int32 [8192], P(('sx', 'sy')), may hold values from 0 to 2047
- schur: bfloat16 [8, 4, 2048, 2048], P('sx', 'sy'), as said below
- local_inverse: bfloat16 [8, 4, 2048, 2048], P('sx', 'sy'), as said below
- coarse_inverse: float32 [256, 256], P(('sx', 'sy')), as said below
Outputs:
- solution_field: float32 [8, 4, 64, 2048], P('sx', 'sy')
- residual: float32 [8, 4, 64, 2048], P('sx', 'sy')
The draws below stay inside these ranges and needn't reach their ends.
Inputs may be any that keep to these rules, and one draw needn't show every extreme that they name: `obs_dest`: at most 16 observations of one device go to one subdomain. `schur`: symmetric positive definite. `local_inverse`: symmetric positive definite. `coarse_inverse`: symmetric positive definite.
All inputs are finite; a program needn't handle non-finite values.
Results may differ from the reference program's by a relative error of at most 0.04.
Values may be sent and summed in bfloat16 or wider, within the bound.
No kernel may reach another device: no remote copies, remote signals or barrier semaphores. Data moves between devices by JAX's collectives and lax.ppermute only.
A program may use at most 128 MiB of HBM per device.

```python
import math
import jax
import jax.numpy as jnp
import numpy as np
from jax import lax

SI = 2048
REAL = 64
NC = 8
ITERS = 6
OBS_DEV = 256
COLS = 8
ROWS = 4
CAP = 16
OBS_ALL = 8192
NCG = 256
DEVICES = 32


def spd_matrix(key, lead, order, low, high, off_scale):
    first = jax.random.fold_in(key, 11)
    second = jax.random.fold_in(key, 23)
    base = jax.random.normal(first, lead + (order, order), jnp.float32)
    sym = (base + jnp.swapaxes(base, -1, -2)) * (off_scale / jnp.sqrt(2.0 * order))
    diag = jax.random.uniform(second, lead + (order,), jnp.float32, low, high)
    eye_mat = jnp.eye(order, dtype=jnp.float32)
    return sym + eye_mat * diag[..., :, None]


def draw_schur(key, part):
    return spd_matrix(key, (COLS, ROWS), SI, 1.0, 2.0, 0.3).astype(jnp.bfloat16)


def draw_local_inverse(key, part):
    return spd_matrix(key, (COLS, ROWS), SI, 0.5, 1.0, 0.15).astype(jnp.bfloat16)


def draw_coarse_inverse(key, part):
    return spd_matrix(key, (), NCG, 4.0, 8.0, 1.0)


def set_ends(result, stream_key, low, largest):
    longest = result.shape.index(max(result.shape))
    spots = []
    for shift in (0, 1):
        where = [jax.random.randint(jax.random.fold_in(stream_key, axis), (), 0, length) for axis, length in enumerate(result.shape)]
        where[longest] = (where[longest] + shift) % result.shape[longest]
        spots.append(tuple(where))
    return result.at[spots[0]].set(low).at[spots[1]].set(largest)


def steps_of(rng, shape, cuts, smallest, largest):
    level = 1.0
    for position, parts in cuts:
        heights = jax.random.uniform(jax.random.fold_in(jax.random.fold_in(rng, 6), position), (parts,), jnp.float32, smallest / len(cuts), largest / len(cuts))
        level = level * jnp.repeat(jnp.exp(heights), shape[position] // parts).reshape((-1,) + (1,) * (len(shape) - 1 - position))
    return level


def shared_out(own_key, own, number, rows, number_of, top, reach, slope):
    ranking = jax.random.permutation(own_key, number_of)
    crowded, usual = portions_of(number_of, rows * top, reach, slope, True), portions_of(number_of, rows * top, reach, slope, False)
    places = jnp.arange(number_of)

    def named(sizes, turn):
        used = int((sizes > 0).sum())
        fixed = max(1, used // 4)
        passed = fixed + (places - fixed + turn * (used - fixed)) % max(1, number_of - fixed)
        return jnp.zeros((number_of,), jnp.int32).at[ranking[jnp.where(places < fixed, places, passed)]].set(jnp.asarray(sizes, jnp.int32))

    sizes = jnp.where(number % 4 == 0, named(crowded, number // 4), named(usual, number - number // 4 - 1))
    mixed = jax.random.permutation(jax.random.fold_in(own, 3), number_of)
    donor, taker = mixed[0:number_of // 2 * 2:2], mixed[1:number_of // 2 * 2:2]
    room = jnp.minimum(sizes[donor] - 1, reach - sizes[taker]) // 2
    room = jnp.where((donor == ranking[0]) | (taker == ranking[0]) | (sizes[taker] == 0), 0, jnp.maximum(room, 0))
    passed = jax.random.randint(jax.random.fold_in(own, 4), (number_of // 2,), 0, 1 << 20) % (room + 1)
    sizes = sizes.at[donor].add(-passed).at[taker].add(passed)
    items = jnp.searchsorted(jnp.cumsum(sizes), jnp.arange(rows * top), side="right").astype(jnp.int32)
    grid = items.reshape(top, rows).T
    grid = grid[jax.random.permutation(jax.random.fold_in(own, 1), rows)]
    turn = jax.random.randint(jax.random.fold_in(own, 2), (rows, 1), 0, top)
    return jnp.take_along_axis(grid, (jnp.arange(top)[None, :] + turn) % top, axis=1)


def portions_of(count, total, limit, skew, full):
    weights = [(1 << 20) // math.isqrt(rank ** skew) + 1 for rank in range(1, count + 1)]
    largest = limit if full else min(limit, max(-(-total // count), total * weights[0] // sum(weights)))
    least = 1 if total - largest >= count - 1 else 0
    holding, rest = [largest] + [least] * (count - 1), total - largest - least * (count - 1)
    while rest > 0:
        candidates = [i for i in range(1, count) if holding[i] < largest] or [i for i in range(1, count) if holding[i] < limit]
        pool, budget = sum([weights[i] for i in candidates]), rest
        for i in candidates:
            extra = min(limit - holding[i], max(1, budget * weights[i] // pool), rest)
            holding[i] = holding[i] + extra
            rest = rest - extra
    return np.array(holding)


def normal_values(key, shape, deviation, bound, cuts=(), held_as=jnp.bfloat16):
    level = steps_of(key, shape, cuts, -0.22, 0.18) if cuts else 1.0
    array = jax.random.normal(key, shape, jnp.float32) * deviation * level
    return jnp.minimum(jnp.maximum(array, -bound), bound).astype(held_as)


def setup_inputs(seed: int = 0) -> dict:
    key_list = jax.random.split(jax.random.key(seed), 7)
    obs_values = normal_values(key_list[0], (OBS_ALL, REAL), 1.0, 6.0, ((0, 32),))
    obs_dest_keys = jax.random.split(jax.random.fold_in(key_list[1], 1), OBS_ALL // OBS_DEV)
    obs_dest_turns = jax.random.permutation(jax.random.fold_in(key_list[1], 3), OBS_ALL // OBS_DEV)
    obs_dest = jax.vmap(lambda own, number: shared_out(jax.random.fold_in(key_list[1], 2), own, number, OBS_DEV, DEVICES, 1, CAP, 2))(obs_dest_keys, obs_dest_turns).reshape((OBS_ALL, 1))
    obs_node = set_ends(jax.random.randint(key_list[2], (OBS_ALL,), 0, SI), jax.random.fold_in(key_list[2], 1), 0, SI - 1).astype(jnp.int32)
    schur = draw_schur(jax.random.fold_in(key_list[6], 71), 0)
    local_inverse = draw_local_inverse(jax.random.fold_in(key_list[6], 71), 0)
    coarse_inverse = draw_coarse_inverse(jax.random.fold_in(key_list[6], 71), 0)
    return {"obs_values": obs_values, "obs_dest": obs_dest, "obs_node": obs_node, "schur": schur, "local_inverse": local_inverse, "coarse_inverse": coarse_inverse}


def assemble(local):
    edge_len = SI // 4
    padded = jnp.pad(local, ((1, 1), (1, 1), (0, 0), (0, 0)))
    west = local[..., 0:edge_len] + padded[:-2, 1:-1, :, edge_len:2 * edge_len]
    east = local[..., edge_len:2 * edge_len] + padded[2:, 1:-1, :, 0:edge_len]
    south = local[..., 2 * edge_len:3 * edge_len] + padded[1:-1, :-2, :, 3 * edge_len:]
    north = local[..., 3 * edge_len:] + padded[1:-1, 2:, :, 2 * edge_len:3 * edge_len]
    return jnp.concatenate([west, east, south, north], axis=3)

def edge_weights():
    edge_len = SI // 4
    col = jnp.arange(COLS)[:, None, None, None]
    row = jnp.arange(ROWS)[None, :, None, None]
    side = (jnp.arange(SI) // edge_len)[None, None, None, :]
    shared = (side == 0) & (col > 0) | (side == 1) & (col < COLS - 1) | (side == 2) & (row > 0) | (side == 3) & (row < ROWS - 1)
    return jnp.where(shared, 0.5, 1.0).astype(jnp.float32)

def coarse_basis():
    edge_len = SI // 4
    node = jnp.arange(SI)
    side = node // edge_len
    offset = (node % edge_len).astype(jnp.float32) - (edge_len - 1) / 2.0
    norm_ramp = jnp.sqrt(jnp.float32(edge_len * (edge_len * edge_len - 1) / 12.0))
    column = jnp.arange(NC)
    on_edge = side[:, None] == (column // 2)[None, :]
    value = jnp.where((column % 2 == 0)[None, :], 1.0 / jnp.sqrt(jnp.float32(edge_len)), offset[:, None] / norm_ramp)
    return jnp.where(on_edge, value, 0.0).astype(jnp.float32)

def local_apply(mats, vec):
    flat_mats = mats.reshape(-1, SI, SI)
    flat_vec = vec.reshape(-1, REAL, SI).astype(jnp.bfloat16)
    out = lax.map(lambda pair: jnp.dot(pair[1], pair[0], preferred_element_type=jnp.float32), (flat_mats, flat_vec))
    return out.reshape(COLS, ROWS, REAL, SI)

def reference(obs_values, obs_dest, obs_node, schur, local_inverse, coarse_inverse):
    hp = lax.Precision.HIGHEST
    target = obs_dest[:, 0].astype(jnp.int32) * SI + obs_node.astype(jnp.int32)
    load = jax.ops.segment_sum(obs_values.astype(jnp.float32), target, num_segments=COLS * ROWS * SI)
    load = jnp.transpose(load.reshape(COLS, ROWS, SI, REAL), (0, 1, 3, 2))
    rhs = assemble(load)
    weight = edge_weights()
    basis = coarse_basis()

    def precond(vec):
        scaled = weight * vec
        part = local_apply(local_inverse, scaled)
        coarse = jnp.einsum('abrs,sk->abkr', scaled, basis, precision=hp).reshape(NCG, REAL)
        solved = jnp.dot(coarse_inverse, coarse, precision=hp).reshape(COLS, ROWS, NC, REAL)
        correction = jnp.einsum('abkr,sk->abrs', solved, basis, precision=hp)
        return assemble(weight * (part + correction))

    def inner(left, right):
        return lax.optimization_barrier(jnp.sum(weight * left * right, axis=(0, 1, 3)))
    solution_field = jnp.zeros_like(rhs)
    residual = rhs
    precon = precond(residual)
    direction = precon
    rz_now = inner(residual, precon)
    for step in range(ITERS):
        image = assemble(local_apply(schur, direction))
        alpha = rz_now / inner(direction, image)
        solution_field = solution_field + alpha[:, None] * direction
        residual = residual - alpha[:, None] * image
        if step < ITERS - 1:
            precon = precond(residual)
            rz_next = inner(residual, precon)
            direction = precon + (rz_next / rz_now)[:, None] * direction
            rz_now = rz_next
    return (solution_field, residual)
```

```python
import functools

import jax
import jax.numpy as jnp
from jax import lax
from jax.experimental import pallas as pl
from jax.experimental.pallas import tpu as pltpu
from jax.sharding import PartitionSpec as P

ITERS = 6
LANES = 128
CHUNK = 256
HP = lax.Precision.HIGHEST
F32 = jnp.float32
BF16 = jnp.bfloat16
VM = pl.BlockSpec(memory_space=pltpu.VMEM)


def call(kernel, outs, args, scratch=(), flops=0):
    size = sum(a.size * a.dtype.itemsize for a in args)
    return pl.pallas_call(
        kernel,
        out_shape=outs,
        in_specs=[VM] * len(args),
        out_specs=jax.tree.map(lambda _: VM, outs),
        scratch_shapes=list(scratch),
        compiler_params=pltpu.CompilerParams(vmem_limit_bytes=8 << 20),
        cost_estimate=pl.CostEstimate(flops=flops, bytes_accessed=size, transcendentals=0),
    )(*args)


def shape(rows, columns, dtype=F32):
    return jax.ShapeDtypeStruct((rows, columns), dtype)


class Place:
    def __init__(self):
        col, row = lax.axis_index("sx"), lax.axis_index("sy")
        cols, rows = lax.axis_size("sx"), lax.axis_size("sy")
        odd_col, odd_row = lax.rem(col, 2), lax.rem(row, 2)
        self.edges = (1 - odd_col, odd_col, 3 - odd_row, 2 + odd_row)
        has = (col > 0, col < cols - 1, row > 0, row < rows - 1)
        self.weights = [jnp.where(there, F32(0.5), F32(1.0)) for there in has]
        far_col = jnp.where(odd_col == 1, col < cols - 1, col > 0)
        far_row = jnp.where(odd_row == 1, row < rows - 1, row > 0)
        self.valid = (None, far_col, None, far_row)


def swaps():
    cols, rows = lax.axis_size("sx"), lax.axis_size("sy")

    def near(count):
        return [(i, i ^ 1) for i in range(count)]

    far_sx = [(0, 0), (cols - 1, cols - 1)]
    for i in range(1, cols - 1, 2):
        far_sx += [(i, i + 1), (i + 1, i)]
    far_sy = []
    for i in range(1, rows, 2):
        far_sy += [(i, (i + 1) % rows), ((i + 1) % rows, i)]
    return (("sx", near(cols)), ("sx", far_sx), ("sy", near(rows)), ("sy", far_sy))


def exchange(edges):
    far_sx, far_sy, near_sx, near_sy = 1, 3, 0, 2
    plan = swaps()
    got = [None] * 4
    for i in (far_sx, far_sy, near_sx, near_sy):
        got[i] = lax.ppermute(edges[i], plan[i][0], plan[i][1])
    return got


def send_edges(value_ref, edge_refs):
    place, edge_len = Place(), value_ref.shape[1] // 4
    for edge, ref in zip(place.edges, edge_refs, strict=True):
        start = pl.multiple_of(edge * edge_len, edge_len)
        ref[...] = value_ref[:, pl.ds(start, edge_len)].astype(BF16)


def add_edges(value_ref, edge_refs):
    place, edge_len = Place(), value_ref.shape[1] // 4
    for edge, valid, ref in zip(place.edges, place.valid, edge_refs, strict=True):
        start = pl.multiple_of(edge * edge_len, edge_len)
        got = ref[...].astype(F32)
        if valid is not None:
            got = jnp.where(valid, got, 0.0)
        value_ref[:, pl.ds(start, edge_len)] += got


def basis_parts(edge_len, start, width):
    node = lax.broadcasted_iota(jnp.int32, (1, width), 1) + start
    offset = node.astype(F32) - (edge_len - 1) / 2.0
    level = 1.0 / jnp.sqrt(F32(edge_len))
    norm = jnp.sqrt(F32(edge_len * (edge_len * edge_len - 1) / 12.0))
    return level, offset / norm


def lane_parts(value):
    return sum(value[:, i : i + LANES] for i in range(LANES, value.shape[1], LANES)) + value[:, :LANES]


def project(value_ref):
    edge_len = value_ref.shape[1] // 4
    columns = []
    for edge in range(4):
        flat = ramped = None
        for start in range(0, edge_len, CHUNK):
            at = edge * edge_len + start
            part = value_ref[:, at : at + CHUNK]
            ramp = basis_parts(edge_len, start, CHUNK)[1]
            one, two = lane_parts(part), lane_parts(part * ramp)
            flat = one if flat is None else flat + one
            ramped = two if ramped is None else ramped + two
        level = basis_parts(edge_len, 0, LANES)[0]
        columns.append(jnp.sum(flat, axis=1, keepdims=True) * level)
        columns.append(jnp.sum(ramped, axis=1, keepdims=True))
    return columns


def write_message(message_ref, columns, gamma, delta):
    rows = gamma.shape[0]
    lane = lax.broadcasted_iota(jnp.int32, (rows, LANES), 1)
    table = jnp.zeros((rows, LANES), F32)
    for i, column in enumerate(columns):
        table = jnp.where(lane == i, column, table)
    table = jnp.where(lane == 8, gamma, table)
    table = jnp.where(lane == 9, delta, table)
    turned = table.T
    lower, upper = turned[0:8], turned[8:16]
    block = jnp.concatenate([lower, upper], axis=1)
    message_ref[...] = jnp.broadcast_to(block[None], message_ref.shape)


def pack_kernel(capacity, values_ref, dest_ref, node_ref, out_ref):
    count = values_ref.shape[0]
    slots = out_ref.shape[0]
    dest = dest_ref[...]
    devices = slots // capacity
    wide = max(LANES, devices)
    lane = lax.broadcasted_iota(jnp.int32, (count, wide), 1)
    hit = (dest == lane).astype(F32)
    before = lax.broadcasted_iota(jnp.int32, (count, count), 0) > lax.broadcasted_iota(jnp.int32, (count, count), 1)
    earlier = jnp.dot(before.astype(BF16), hit.astype(BF16), preferred_element_type=F32)
    rank = jnp.sum(hit * earlier, axis=1, keepdims=True).astype(jnp.int32)
    slot = dest * capacity + rank
    node = node_ref[...]
    realiz = values_ref.shape[1]
    high, low = (node // 64).astype(F32), lax.rem(node, 64).astype(F32)
    side = lax.broadcasted_iota(jnp.int32, (count, LANES - realiz), 1)
    codes = jnp.where(side == 0, high, jnp.where(side == 1, low, 0.0)).astype(BF16)
    full = jnp.concatenate([values_ref[...], codes], axis=1)
    choose = (slot == lax.broadcasted_iota(jnp.int32, (count, slots), 1)).astype(F32).astype(BF16)
    out = lax.dot_general(choose, full, (((0,), (0,)), ((), ())), preferred_element_type=F32)
    out_ref[...] = out.astype(BF16)


def coarse_kernel(row_count, inverse_ref, out_ref):
    size = inverse_ref.shape[1]
    i = lax.broadcasted_iota(jnp.int32, (size, size), 0)
    j = lax.broadcasted_iota(jnp.int32, (size, size), 1)
    kind = (j % 8) // 2
    place = j // 8
    col, row = place // row_count, place % row_count
    cols = size // 8 // row_count
    has = (kind == 0) & (col > 0) | (kind == 1) & (col < cols - 1) | (kind == 2) & (row > 0) | (kind == 3) & (row < row_count - 1)
    step = jnp.where(kind == 0, 2 - 8 * row_count, jnp.where(kind == 1, 8 * row_count - 2, jnp.where(kind == 2, 2 - 8, 8 - 2)))
    pair = has & (i == j + step)
    table = jnp.where(pair, 0.5, jnp.where(i == j, jnp.where(has, 0.5, 1.0), 0.0))
    out_ref[...] = jnp.dot(inverse_ref[...], table, precision=HP, preferred_element_type=F32)


def load_kernel(realiz, got_ref, load_ref, e0, e1, e2, e3, message_ref):
    slots, size = got_ref.shape[0], load_ref.shape[1]
    got = got_ref[...]
    node = got[:, realiz : realiz + 1].astype(F32) * 64.0 + got[:, realiz + 1 : realiz + 2].astype(F32)
    node = node.astype(jnp.int32)
    for start in range(0, size, CHUNK):
        here = (node == lax.broadcasted_iota(jnp.int32, (slots, CHUNK), 1) + start).astype(F32).astype(BF16)
        load = lax.dot_general(got, here, (((0,), (0,)), ((), ())), preferred_element_type=F32)
        load_ref[:, start : start + CHUNK] = load[:realiz]
    send_edges(load_ref, (e0, e1, e2, e3))
    zero = jnp.zeros((realiz, 1), F32)
    write_message(message_ref, project(load_ref), zero, zero)


def local_solve(coarse, inverse_ref, coarse_inverse_ref, resid_ref, columns_of, scaled, part_ref, gamma_ref):
    place = Place()
    size = resid_ref.shape[1]
    edge_len = size // 4
    weight_at = [place.weights[i // edge_len] for i in range(0, size, CHUNK)]
    for start in range(0, size, CHUNK):
        at = pl.ds(start, CHUNK)
        scaled[:, at] = (weight_at[start // CHUNK] * resid_ref[:, at]).astype(BF16)
    solved = jnp.dot(coarse_inverse_ref[...], coarse, precision=HP, preferred_element_type=F32)
    turned = columns_of(solved)
    vec = scaled[...]
    gamma = None
    for start in range(0, size, CHUNK):
        at = pl.ds(start, CHUNK)
        edge, weight = start // edge_len, weight_at[start // CHUNK]
        level, ramp = basis_parts(edge_len, start % edge_len, CHUNK)
        part = jnp.dot(vec, inverse_ref[:, at], preferred_element_type=F32)
        part = part + (turned[2 * edge] * level + turned[2 * edge + 1] * ramp)
        part = weight * part
        part_ref[:, at] = part
        here = lane_parts(resid_ref[:, at] * part)
        gamma = here if gamma is None else gamma + here
    gamma_ref[...] = gamma


def turn(rows, realiz):
    count = rows.shape[0]
    full = jnp.concatenate([rows, jnp.zeros((LANES - count, LANES), F32)], axis=0) if count < LANES else rows
    turned = full.T
    return [turned[:realiz, i : i + 1] for i in range(count)]


def first_kernel(load_ref, g0, g1, g2, g3, gathered_ref, inverse_ref, coarse_inverse_ref,
                 resid_ref, coarse_ref, part_ref, gamma_ref, e0, e1, e2, e3, scaled):
    realiz = load_ref.shape[0]
    resid_ref[...] = load_ref[...]
    add_edges(resid_ref, (g0, g1, g2, g3))
    coarse = gathered_ref[...].reshape(coarse_ref.shape)
    coarse_ref[...] = coarse
    local_solve(coarse, inverse_ref, coarse_inverse_ref, resid_ref, lambda rows: turn(rows, realiz), scaled, part_ref, gamma_ref)
    send_edges(part_ref, (e0, e1, e2, e3))


def image_kernel(part_ref, g0, g1, g2, g3, gamma_ref, schur_ref,
                 precon_ref, image_ref, e0, e1, e2, e3, message_ref, rounded):
    size = part_ref.shape[1]
    precon_ref[...] = part_ref[...]
    add_edges(precon_ref, (g0, g1, g2, g3))
    rounded[...] = precon_ref[...].astype(BF16)
    vec = rounded[...]
    delta = None
    for start in range(0, size, CHUNK):
        at = pl.ds(start, CHUNK)
        image = jnp.dot(vec, schur_ref[:, at], preferred_element_type=F32)
        image_ref[:, at] = image
        here = lane_parts(precon_ref[:, at] * image)
        delta = here if delta is None else delta + here
    send_edges(image_ref, (e0, e1, e2, e3))
    gamma = jnp.sum(gamma_ref[...], axis=1, keepdims=True)
    delta = jnp.sum(delta, axis=1, keepdims=True)
    write_message(message_ref, project(image_ref), gamma, delta)


def step_kernel(mode, last, *refs):
    refs = list(refs)
    take = lambda n: [refs.pop(0) for _ in range(n)]
    image_ref, *edges = take(5)
    gathered_ref, precon_ref, resid_in = take(3)
    if mode != "init":
        direction_in, applied_in, field_in, state_in = take(4)
    if not last:
        coarse_in, = take(1)
        if mode != "init":
            coarse_applied_in, = take(1)
        inverse_ref, coarse_inverse_ref = take(2)
    field_ref, resid_ref = take(2)
    if not last:
        direction_ref, applied_ref, state_ref, coarse_ref, coarse_applied_ref, part_ref, gamma_ref = take(7)
        out_edges = take(4)
    work, = take(1)
    realiz, size = image_ref.shape
    work[...] = image_ref[...]
    add_edges(work, edges)
    total = pltpu.roll(jnp.sum(gathered_ref[...], axis=0), LANES // 2, 1)
    gamma, delta = total[0:1], total[1:2]
    if mode == "init":
        alpha = gamma / delta
        beta = jnp.zeros_like(alpha)
    else:
        beta = gamma / state_in[0:1]
        alpha = gamma / (delta - beta * gamma / state_in[1:2])
    lane = lax.broadcasted_iota(jnp.int32, (1, LANES), 1)
    alpha, beta = (jnp.where(lane < realiz, row, 0.0) for row in (alpha, beta))
    if not last:
        scaled, = take(1)
        state_ref[0:1] = gamma
        state_ref[1:2] = alpha
        applied = gathered_ref[...].reshape(coarse_ref.shape)
        if mode != "init":
            applied = applied + beta * coarse_applied_in[...]
        coarse_applied_ref[...] = applied
        coarse = coarse_in[...] - alpha * applied
        coarse_ref[...] = coarse
    alpha_col, beta_col = turn(jnp.concatenate([alpha, beta, jnp.zeros((6, LANES), F32)], axis=0), realiz)[:2]
    for start in range(0, size, CHUNK):
        at = pl.ds(start, CHUNK)
        direction, applied = precon_ref[:, at], work[:, at]
        if mode == "init":
            field_ref[:, at] = alpha_col * direction
        else:
            direction = direction + beta_col * direction_in[:, at]
            applied = applied + beta_col * applied_in[:, at]
            field_ref[:, at] = field_in[:, at] + alpha_col * direction
        resid_ref[:, at] = resid_in[:, at] - alpha_col * applied
        if not last:
            direction_ref[:, at] = direction
            applied_ref[:, at] = applied
    if not last:
        local_solve(coarse, inverse_ref, coarse_inverse_ref, resid_ref, lambda rows: turn(rows, realiz), scaled, part_ref, gamma_ref)
        send_edges(part_ref, out_edges)


def gather(message):
    return lax.all_to_all(message, ("sx", "sy"), split_axis=0, concat_axis=0, tiled=True)


def body(obs_values, obs_dest, obs_node, schur, local_inverse, coarse_inverse):
    size = schur.shape[-1]
    obs_count, realiz = obs_values.shape
    row_count = lax.axis_size("sy")
    devices = lax.axis_size("sx") * row_count
    capacity = max(2, 2 * obs_count // devices)
    coarse_size = coarse_inverse.shape[1]
    edge = shape(realiz, size // 4, BF16)
    edges = [edge] * 4
    whole = shape(realiz, size)
    message = jax.ShapeDtypeStruct((devices, 8, LANES), F32)
    narrow = shape(realiz, LANES)
    coarse_state = shape(coarse_size, LANES)
    scratch_half, scratch_full = pltpu.VMEM((realiz, size), BF16), pltpu.VMEM((realiz, size), F32)
    flops = 2 * realiz * size * size
    schur_mat, inverse_mat = schur[0, 0], local_inverse[0, 0]

    packed = call(
        functools.partial(pack_kernel, capacity),
        shape(devices * capacity, LANES, BF16),
        (obs_values, obs_dest, obs_node[:, None]),
    )
    got = lax.all_to_all(
        packed.reshape(devices, capacity, LANES), ("sx", "sy"), split_axis=0, concat_axis=0, tiled=True
    ).reshape(devices * capacity, LANES)
    coarse_mat = call(functools.partial(coarse_kernel, row_count), shape(*coarse_inverse.shape), (coarse_inverse,))
    load, *out = call(functools.partial(load_kernel, realiz), [whole, *edges, message], (got,))
    gathered, edges_got = gather(out[4]), exchange(out[:4])
    resid, coarse, part, gamma, *out = call(
        first_kernel,
        [whole, coarse_state, whole, narrow, *edges],
        (load, *edges_got, gathered, inverse_mat, coarse_mat),
        [scratch_half],
        flops,
    )
    field = direction = applied = state = coarse_applied = None
    for step in range(ITERS):
        edges_got = exchange(out)
        precon, image, *out = call(
            image_kernel,
            [whole, whole, *edges, message],
            (part, *edges_got, gamma, schur_mat),
            [scratch_half],
            flops,
        )
        gathered, edges_got = gather(out[4]), exchange(out[:4])
        last = step == ITERS - 1
        mode = "init" if step == 0 else "next"
        args = [image, *edges_got, gathered, precon, resid]
        args += [] if step == 0 else [direction, applied, field, state]
        if last:
            field, resid = call(
                functools.partial(step_kernel, mode, True), [whole, whole], args, [scratch_full]
            )
            break
        args += [coarse] if step == 0 else [coarse, coarse_applied]
        args += [inverse_mat, coarse_mat]
        field, resid, direction, applied, state, coarse, coarse_applied, part, gamma, *out = call(
            functools.partial(step_kernel, mode, False),
            [whole, whole, whole, whole, shape(8, LANES), coarse_state, coarse_state, whole, narrow, *edges],
            args,
            [scratch_full, scratch_half],
            flops,
        )
    return field[None, None], resid[None, None]


def solution(mesh):
    placed = (
        P(("sx", "sy"), None),
        P(("sx", "sy"), None),
        P(("sx", "sy")),
        P("sx", "sy", None, None),
        P("sx", "sy", None, None),
        P(("sx", "sy"), None),
    )
    return jax.shard_map(
        body,
        mesh=mesh,
        in_specs=placed,
        out_specs=(P("sx", "sy", None, None), P("sx", "sy", None, None)),
        check_vma=False,
    )
```

```python
import functools

import jax
import jax.numpy as jnp
from jax import lax
from jax.experimental import pallas as pl
from jax.experimental.pallas import tpu as pltpu
from jax.sharding import PartitionSpec as P

ITERS = 6
EXACT = 2
LANES = 128
CHUNK = 256
HP = lax.Precision.HIGHEST
F32 = jnp.float32
BF16 = jnp.bfloat16
VM = pl.BlockSpec(memory_space=pltpu.VMEM)


def call(kernel, outs, args, scratch=(), flops=0):
    size = sum(a.size * a.dtype.itemsize for a in args)
    return pl.pallas_call(
        kernel,
        out_shape=outs,
        in_specs=[VM] * len(args),
        out_specs=jax.tree.map(lambda _: VM, outs),
        scratch_shapes=list(scratch),
        compiler_params=pltpu.CompilerParams(vmem_limit_bytes=8 << 20),
        cost_estimate=pl.CostEstimate(flops=flops, bytes_accessed=size, transcendentals=0),
    )(*args)


def shape(rows, columns, dtype=F32):
    return jax.ShapeDtypeStruct((rows, columns), dtype)


class Place:
    def __init__(self):
        col, row = lax.axis_index("sx"), lax.axis_index("sy")
        cols, rows = lax.axis_size("sx"), lax.axis_size("sy")
        odd_col, odd_row = lax.rem(col, 2), lax.rem(row, 2)
        self.edges = (1 - odd_col, odd_col, 3 - odd_row, 2 + odd_row)
        has = (col > 0, col < cols - 1, row > 0, row < rows - 1)
        self.weights = [jnp.where(there, F32(0.5), F32(1.0)) for there in has]
        far_col = jnp.where(odd_col == 1, col < cols - 1, col > 0)
        far_row = jnp.where(odd_row == 1, row < rows - 1, row > 0)
        self.valid = (None, far_col, None, far_row)


def swaps():
    cols, rows = lax.axis_size("sx"), lax.axis_size("sy")
    plans = [], [], [], []
    for col in range(cols):
        for row in range(rows):
            across = col + (1 if col % 2 else -1)
            beyond = row + (1 if row % 2 else -1)
            far_sx = (across, row) if 0 <= across < cols else (col, row ^ 1)
            partners = (col ^ 1, row), far_sx, (col, row ^ 1), (col, beyond % rows)
            for plan, (to_col, to_row) in zip(plans, partners, strict=True):
                plan.append((col * rows + row, to_col * rows + to_row))
    return plans


def exchange(edges):
    plans = swaps()
    got = [None] * 4
    for i in (1, 0, 3, 2):
        got[i] = lax.ppermute(edges[i], ("sx", "sy"), plans[i])
    return got


def send_edges(value_ref, edge_refs):
    place, edge_len = Place(), value_ref.shape[1] // 4
    for edge, ref in zip(place.edges, edge_refs, strict=True):
        start = pl.multiple_of(edge * edge_len, edge_len)
        ref[...] = value_ref[:, pl.ds(start, edge_len)].astype(ref.dtype)


def add_edges(value_ref, edge_refs):
    place, edge_len = Place(), value_ref.shape[1] // 4
    for edge, valid, ref in zip(place.edges, place.valid, edge_refs, strict=True):
        start = pl.multiple_of(edge * edge_len, edge_len)
        got = ref[...].astype(F32)
        if valid is not None:
            got = jnp.where(valid, got, 0.0)
        value_ref[:, pl.ds(start, edge_len)] += got


def basis_parts(edge_len, start, width):
    node = lax.broadcasted_iota(jnp.int32, (1, width), 1) + start
    offset = node.astype(F32) - (edge_len - 1) / 2.0
    level = 1.0 / jnp.sqrt(F32(edge_len))
    norm = jnp.sqrt(F32(edge_len * (edge_len * edge_len - 1) / 12.0))
    return level, offset / norm


def lane_parts(value):
    return sum(value[:, i : i + LANES] for i in range(LANES, value.shape[1], LANES)) + value[:, :LANES]


def project(value_ref):
    edge_len = value_ref.shape[1] // 4
    columns = []
    for edge in range(4):
        flat = ramped = None
        for start in range(0, edge_len, CHUNK):
            at = edge * edge_len + start
            part = value_ref[:, at : at + CHUNK]
            ramp = basis_parts(edge_len, start, CHUNK)[1]
            one, two = lane_parts(part), lane_parts(part * ramp)
            flat = one if flat is None else flat + one
            ramped = two if ramped is None else ramped + two
        level = basis_parts(edge_len, 0, LANES)[0]
        columns.append(jnp.sum(flat, axis=1, keepdims=True) * level)
        columns.append(jnp.sum(ramped, axis=1, keepdims=True))
    return columns


def write_message(message_ref, columns, gamma, delta):
    rows = gamma.shape[0]
    lane = lax.broadcasted_iota(jnp.int32, (rows, LANES), 1)
    table = jnp.zeros((rows, LANES), F32)
    for i, column in enumerate(columns):
        table = jnp.where(lane == i, column, table)
    table = jnp.where(lane == 8, gamma, table)
    table = jnp.where(lane == 9, delta, table)
    turned = table.T
    lower, upper = turned[0:8], turned[8:16]
    block = jnp.concatenate([lower, upper], axis=1)
    message_ref[...] = jnp.broadcast_to(block[None], message_ref.shape)


def pack_kernel(capacity, values_ref, dest_ref, node_ref, out_ref):
    count = values_ref.shape[0]
    slots = out_ref.shape[0]
    dest = dest_ref[...]
    devices = slots // capacity
    wide = max(LANES, devices)
    lane = lax.broadcasted_iota(jnp.int32, (count, wide), 1)
    hit = (dest == lane).astype(F32)
    before = lax.broadcasted_iota(jnp.int32, (count, count), 0) > lax.broadcasted_iota(jnp.int32, (count, count), 1)
    earlier = jnp.dot(before.astype(BF16), hit.astype(BF16), preferred_element_type=F32)
    rank = jnp.sum(hit * earlier, axis=1, keepdims=True).astype(jnp.int32)
    slot = dest * capacity + rank
    node = node_ref[...]
    realiz = values_ref.shape[1]
    high, low = (node // 64).astype(F32), lax.rem(node, 64).astype(F32)
    side = lax.broadcasted_iota(jnp.int32, (count, LANES - realiz), 1)
    codes = jnp.where(side == 0, high, jnp.where(side == 1, low, 0.0)).astype(BF16)
    full = jnp.concatenate([values_ref[...], codes], axis=1)
    choose = (slot == lax.broadcasted_iota(jnp.int32, (count, slots), 1)).astype(F32).astype(BF16)
    out = lax.dot_general(choose, full, (((0,), (0,)), ((), ())), preferred_element_type=F32)
    out_ref[...] = out.astype(BF16)


def coarse_kernel(row_count, inverse_ref, out_ref):
    size = inverse_ref.shape[1]
    i = lax.broadcasted_iota(jnp.int32, (size, size), 0)
    j = lax.broadcasted_iota(jnp.int32, (size, size), 1)
    kind = (j % 8) // 2
    place = j // 8
    col, row = place // row_count, place % row_count
    cols = size // 8 // row_count
    has = (kind == 0) & (col > 0) | (kind == 1) & (col < cols - 1) | (kind == 2) & (row > 0) | (kind == 3) & (row < row_count - 1)
    step = jnp.where(kind == 0, 2 - 8 * row_count, jnp.where(kind == 1, 8 * row_count - 2, jnp.where(kind == 2, 2 - 8, 8 - 2)))
    pair = has & (i == j + step)
    table = jnp.where(pair, 0.5, jnp.where(i == j, jnp.where(has, 0.5, 1.0), 0.0))
    out_ref[...] = jnp.dot(inverse_ref[...], table, precision=HP, preferred_element_type=F32)


def load_kernel(realiz, got_ref, load_ref, e0, e1, e2, e3, message_ref):
    slots, size = got_ref.shape[0], load_ref.shape[1]
    got = got_ref[...]
    node = got[:, realiz : realiz + 1].astype(F32) * 64.0 + got[:, realiz + 1 : realiz + 2].astype(F32)
    node = node.astype(jnp.int32)
    for start in range(0, size, CHUNK):
        here = (node == lax.broadcasted_iota(jnp.int32, (slots, CHUNK), 1) + start).astype(F32).astype(BF16)
        load = lax.dot_general(got, here, (((0,), (0,)), ((), ())), preferred_element_type=F32)
        load_ref[:, start : start + CHUNK] = load[:realiz]
    send_edges(load_ref, (e0, e1, e2, e3))
    zero = jnp.zeros((realiz, 1), F32)
    write_message(message_ref, project(load_ref), zero, zero)


def local_solve(coarse, inverse_ref, coarse_inverse_ref, resid_ref, columns_of, scaled, part_ref, gamma_ref):
    place = Place()
    size = resid_ref.shape[1]
    edge_len = size // 4
    weight_at = [place.weights[i // edge_len] for i in range(0, size, CHUNK)]
    for start in range(0, size, CHUNK):
        at = pl.ds(start, CHUNK)
        scaled[:, at] = (weight_at[start // CHUNK] * resid_ref[:, at]).astype(BF16)
    solved = jnp.dot(coarse_inverse_ref[...], coarse, precision=HP, preferred_element_type=F32)
    turned = columns_of(solved)
    vec = scaled[...]
    gamma = None
    for start in range(0, size, CHUNK):
        at = pl.ds(start, CHUNK)
        edge, weight = start // edge_len, weight_at[start // CHUNK]
        level, ramp = basis_parts(edge_len, start % edge_len, CHUNK)
        part = jnp.dot(vec, inverse_ref[:, at], preferred_element_type=F32)
        part = part + (turned[2 * edge] * level + turned[2 * edge + 1] * ramp)
        part = weight * part
        part_ref[:, at] = part
        here = lane_parts(resid_ref[:, at] * part)
        gamma = here if gamma is None else gamma + here
    gamma_ref[...] = gamma


def turn(rows, realiz):
    count = rows.shape[0]
    full = jnp.concatenate([rows, jnp.zeros((LANES - count, LANES), F32)], axis=0) if count < LANES else rows
    turned = full.T
    return [turned[:realiz, i : i + 1] for i in range(count)]


def first_kernel(load_ref, g0, g1, g2, g3, gathered_ref, inverse_ref, coarse_inverse_ref,
                 resid_ref, coarse_ref, part_ref, gamma_ref, e0, e1, e2, e3, scaled):
    realiz = load_ref.shape[0]
    resid_ref[...] = load_ref[...]
    add_edges(resid_ref, (g0, g1, g2, g3))
    coarse = gathered_ref[...].reshape(coarse_ref.shape)
    coarse_ref[...] = coarse
    local_solve(coarse, inverse_ref, coarse_inverse_ref, resid_ref, lambda rows: turn(rows, realiz), scaled, part_ref, gamma_ref)
    send_edges(part_ref, (e0, e1, e2, e3))


def image_kernel(part_ref, g0, g1, g2, g3, gamma_ref, schur_ref,
                 precon_ref, image_ref, e0, e1, e2, e3, message_ref, rounded):
    size = part_ref.shape[1]
    precon_ref[...] = part_ref[...]
    add_edges(precon_ref, (g0, g1, g2, g3))
    rounded[...] = precon_ref[...].astype(BF16)
    vec = rounded[...]
    delta = None
    for start in range(0, size, CHUNK):
        at = pl.ds(start, CHUNK)
        image = jnp.dot(vec, schur_ref[:, at], preferred_element_type=F32)
        image_ref[:, at] = image
        here = lane_parts(precon_ref[:, at] * image)
        delta = here if delta is None else delta + here
    send_edges(image_ref, (e0, e1, e2, e3))
    gamma = jnp.sum(gamma_ref[...], axis=1, keepdims=True)
    delta = jnp.sum(delta, axis=1, keepdims=True)
    write_message(message_ref, project(image_ref), gamma, delta)


def step_kernel(mode, last, *refs):
    refs = list(refs)
    take = lambda n: [refs.pop(0) for _ in range(n)]
    image_ref, *edges = take(5)
    gathered_ref, precon_ref, resid_in = take(3)
    if mode != "init":
        direction_in, applied_in, field_in, state_in = take(4)
    if not last:
        coarse_in, = take(1)
        if mode != "init":
            coarse_applied_in, = take(1)
        inverse_ref, coarse_inverse_ref = take(2)
    field_ref, resid_ref = take(2)
    if not last:
        direction_ref, applied_ref, state_ref, coarse_ref, coarse_applied_ref, part_ref, gamma_ref = take(7)
        out_edges = take(4)
    work, = take(1)
    realiz, size = image_ref.shape
    work[...] = image_ref[...]
    add_edges(work, edges)
    total = pltpu.roll(jnp.sum(gathered_ref[...], axis=0), LANES // 2, 1)
    gamma, delta = total[0:1], total[1:2]
    if mode == "init":
        alpha = gamma / delta
        beta = jnp.zeros_like(alpha)
    else:
        beta = gamma / state_in[0:1]
        alpha = gamma / (delta - beta * gamma / state_in[1:2])
    lane = lax.broadcasted_iota(jnp.int32, (1, LANES), 1)
    alpha, beta = (jnp.where(lane < realiz, row, 0.0) for row in (alpha, beta))
    if not last:
        scaled, = take(1)
        state_ref[0:1] = gamma
        state_ref[1:2] = alpha
        applied = gathered_ref[...].reshape(coarse_ref.shape)
        if mode != "init":
            applied = applied + beta * coarse_applied_in[...]
        coarse_applied_ref[...] = applied
        coarse = coarse_in[...] - alpha * applied
        coarse_ref[...] = coarse
    alpha_col, beta_col = turn(jnp.concatenate([alpha, beta, jnp.zeros((6, LANES), F32)], axis=0), realiz)[:2]
    for start in range(0, size, CHUNK):
        at = pl.ds(start, CHUNK)
        direction, applied = precon_ref[:, at], work[:, at]
        if mode == "init":
            field_ref[:, at] = alpha_col * direction
        else:
            direction = direction + beta_col * direction_in[:, at]
            applied = applied + beta_col * applied_in[:, at]
            field_ref[:, at] = field_in[:, at] + alpha_col * direction
        resid_ref[:, at] = resid_in[:, at] - alpha_col * applied
        if not last:
            direction_ref[:, at] = direction
            applied_ref[:, at] = applied
    if not last:
        local_solve(coarse, inverse_ref, coarse_inverse_ref, resid_ref, lambda rows: turn(rows, realiz), scaled, part_ref, gamma_ref)
        send_edges(part_ref, out_edges)


def gather(message):
    return lax.all_to_all(message, ("sx", "sy"), split_axis=0, concat_axis=0, tiled=True)


def gather_then_exchange(out):
    *edges, message = out
    gathered = gather(message)
    gathered, *edges = lax.optimization_barrier((gathered, *edges))
    return gathered, exchange(edges)


def body(obs_values, obs_dest, obs_node, schur, local_inverse, coarse_inverse):
    size = schur.shape[-1]
    obs_count, realiz = obs_values.shape
    row_count = lax.axis_size("sy")
    devices = lax.axis_size("sx") * row_count
    capacity = max(2, 2 * obs_count // devices)
    coarse_size = coarse_inverse.shape[1]
    edge = shape(realiz, size // 4, BF16)
    edges = [edge] * 4
    exact = shape(realiz, size // 4)
    whole = shape(realiz, size)
    message = jax.ShapeDtypeStruct((devices, 8, LANES), F32)
    narrow = shape(realiz, LANES)
    coarse_state = shape(coarse_size, LANES)
    scratch_half, scratch_full = pltpu.VMEM((realiz, size), BF16), pltpu.VMEM((realiz, size), F32)
    flops = 2 * realiz * size * size
    schur_mat, inverse_mat = schur[0, 0], local_inverse[0, 0]

    packed = call(
        functools.partial(pack_kernel, capacity),
        shape(devices * capacity, LANES, BF16),
        (obs_values, obs_dest, obs_node[:, None]),
    )
    got = lax.all_to_all(
        packed.reshape(devices, capacity, LANES), ("sx", "sy"), split_axis=0, concat_axis=0, tiled=True
    ).reshape(devices * capacity, LANES)
    coarse_mat = call(functools.partial(coarse_kernel, row_count), shape(*coarse_inverse.shape), (coarse_inverse,))
    load, *out = call(functools.partial(load_kernel, realiz), [whole, *edges, message], (got,))
    gathered, edges_got = gather_then_exchange(out)
    resid, coarse, part, gamma, *out = call(
        first_kernel,
        [whole, coarse_state, whole, narrow, *edges],
        (load, *edges_got, gathered, inverse_mat, coarse_mat),
        [scratch_half],
        flops,
    )
    field = direction = applied = state = coarse_applied = None
    for step in range(ITERS):
        edges_got = exchange(out)
        precon, image, *out = call(
            image_kernel,
            [whole, whole, *([exact] * 4 if step < EXACT else edges), message],
            (part, *edges_got, gamma, schur_mat),
            [scratch_half],
            flops,
        )
        gathered, edges_got = gather_then_exchange(out)
        last = step == ITERS - 1
        mode = "init" if step == 0 else "next"
        args = [image, *edges_got, gathered, precon, resid]
        args += [] if step == 0 else [direction, applied, field, state]
        if last:
            field, resid = call(
                functools.partial(step_kernel, mode, True), [whole, whole], args, [scratch_full]
            )
            break
        args += [coarse] if step == 0 else [coarse, coarse_applied]
        args += [inverse_mat, coarse_mat]
        field, resid, direction, applied, state, coarse, coarse_applied, part, gamma, *out = call(
            functools.partial(step_kernel, mode, False),
            [whole, whole, whole, whole, shape(8, LANES), coarse_state, coarse_state, whole, narrow, *edges],
            args,
            [scratch_full, scratch_half],
            flops,
        )
    return field[None, None], resid[None, None]


def solution(mesh):
    placed = (
        P(("sx", "sy"), None),
        P(("sx", "sy"), None),
        P(("sx", "sy")),
        P("sx", "sy", None, None),
        P("sx", "sy", None, None),
        P(("sx", "sy"), None),
    )
    return jax.shard_map(
        body,
        mesh=mesh,
        in_specs=placed,
        out_specs=(P("sx", "sy", None, None), P("sx", "sy", None, None)),
        check_vma=False,
    )
```

```python
import functools

import jax
import jax.numpy as jnp
from jax import lax
from jax.experimental import pallas as pl
from jax.experimental.pallas import tpu as pltpu
from jax.sharding import PartitionSpec as P

ITERS = 6
PAD = 16
COVER = 8e9
LANES = 128
CHUNK = 256
HP = lax.Precision.HIGHEST
F32 = jnp.float32
BF16 = jnp.bfloat16
VM = pl.BlockSpec(memory_space=pltpu.VMEM)
AXES = ("sx", "sy")


def call(kernel, outs, args, scratch=(), flops=0):
    size = sum(a.size * a.dtype.itemsize for a in args)
    return pl.pallas_call(
        kernel,
        out_shape=outs,
        in_specs=[VM] * len(args),
        out_specs=jax.tree.map(lambda _: VM, outs),
        scratch_shapes=list(scratch),
        compiler_params=pltpu.CompilerParams(vmem_limit_bytes=8 << 20),
        cost_estimate=pl.CostEstimate(flops=int(flops), bytes_accessed=size, transcendentals=0),
    )(*args)


def shape(rows, columns, dtype=F32):
    return jax.ShapeDtypeStruct((rows, columns), dtype)


def edge_of(slot, odd_col, odd_row):
    return (1 - odd_col, 3 - odd_row, odd_col, 2 + odd_row)[slot]


class Place:
    def __init__(self):
        col, row = lax.axis_index("sx"), lax.axis_index("sy")
        cols, rows = lax.axis_size("sx"), lax.axis_size("sy")
        odd_col, odd_row = lax.rem(col, 2), lax.rem(row, 2)
        self.edges = [edge_of(slot, odd_col, odd_row) for slot in range(4)]
        far_col = jnp.where(odd_col == 1, col < cols - 1, col > 0)
        far_row = jnp.where(odd_row == 1, row < rows - 1, row > 0)
        self.shared = (None, None, far_col, far_row)

    def weight(self, slot):
        shared = self.shared[slot]
        return F32(0.5) if shared is None else jnp.where(shared, F32(0.5), F32(1.0))


def swaps():
    cols, rows = lax.axis_size("sx"), lax.axis_size("sy")
    plans = [], [], [], []
    for col in range(cols):
        for row in range(rows):
            across = col + (1 if col % 2 else -1)
            beyond = row + (1 if row % 2 else -1)
            far_sx = (across, row) if 0 <= across < cols else (col, row ^ 1)
            partners = (col ^ 1, row), (col, row ^ 1), far_sx, (col, beyond % rows)
            for plan, (to_col, to_row) in zip(plans, partners, strict=True):
                plan.append((col * rows + row, to_col * rows + to_row))
    return plans


def exchange(edges):
    plans = swaps()
    got = [None] * 4
    for slot in (2, 0, 3, 1):
        got[slot] = lax.ppermute(edges[slot], AXES, plans[slot])
    return got


def received(place, slot, ref):
    got = ref[...].astype(F32)
    shared = place.shared[slot]
    return got if shared is None else jnp.where(shared, got, 0.0)


def basis_parts(edge_len, start, width):
    node = lax.broadcasted_iota(jnp.int32, (1, width), 1) + start
    offset = node.astype(F32) - (edge_len - 1) / 2.0
    level = 1.0 / jnp.sqrt(F32(edge_len))
    norm = jnp.sqrt(F32(edge_len * (edge_len * edge_len - 1) / 12.0))
    return level, offset / norm


def lane_parts(value):
    return sum(value[:, i : i + LANES] for i in range(LANES, value.shape[1], LANES)) + value[:, :LANES]


def project(halves):
    edge_len = halves[0].shape[1] // 2
    columns = []
    for slot in range(4):
        flat = ramped = None
        for start in range(0, edge_len, CHUNK):
            at = slot % 2 * edge_len + start
            part = halves[slot // 2][:, at : at + CHUNK]
            ramp = basis_parts(edge_len, start, CHUNK)[1]
            one, two = lane_parts(part), lane_parts(part * ramp)
            flat = one if flat is None else flat + one
            ramped = two if ramped is None else ramped + two
        level = basis_parts(edge_len, 0, LANES)[0]
        columns.append(jnp.sum(flat, axis=1, keepdims=True) * level)
        columns.append(jnp.sum(ramped, axis=1, keepdims=True))
    return columns


def write_message(message_ref, columns, gamma, delta):
    rows = gamma.shape[0]
    lane = lax.broadcasted_iota(jnp.int32, (rows, LANES), 1)
    table = jnp.zeros((rows, LANES), F32)
    order = [*columns[0::2], gamma, *columns[1::2], delta]
    for i, column in enumerate(order):
        table = jnp.where(lane == (i if i < 5 else i + 3), column, table)
    turned = table.T
    block = jnp.concatenate([turned[0:8], turned[8:16]], axis=1)
    for i in range(5):
        row = jnp.broadcast_to(block[i : i + 1][None], (message_ref.shape[0], 1, LANES))
        message_ref[:, :, i * LANES : (i + 1) * LANES] = row


def pack_kernel(capacity, values_ref, dest_ref, node_ref, out_ref):
    realiz, count = values_ref.shape
    slots = out_ref.shape[0]
    dest, node = dest_ref[...], node_ref[...]
    hit = lax.broadcasted_iota(jnp.int32, (slots // capacity, count), 0) == dest
    before = lax.broadcasted_iota(jnp.int32, (count, count), 0) < lax.broadcasted_iota(jnp.int32, (count, count), 1)
    hit = hit.astype(F32)
    earlier = jnp.dot(hit.astype(BF16), before.astype(F32).astype(BF16), preferred_element_type=F32)
    rank = jnp.sum(hit * earlier, axis=0, keepdims=True).astype(jnp.int32)
    slot = dest * capacity + rank
    high, low = (node // 64).astype(F32), lax.rem(node, 64).astype(F32)
    side = lax.broadcasted_iota(jnp.int32, (LANES - realiz, count), 0)
    codes = jnp.where(side == 0, high, jnp.where(side == 1, low, 0.0)).astype(BF16)
    full = jnp.concatenate([values_ref[...], codes], axis=0)
    choose = (lax.broadcasted_iota(jnp.int32, (slots, count), 0) == slot).astype(F32).astype(BF16)
    out = lax.dot_general(choose, full, (((1,), (1,)), ((), ())), preferred_element_type=F32)
    out_ref[...] = out.astype(BF16)


def coarse_kernel(cols, rows, inverse_ref, *out_refs):
    devices = cols * rows
    i = lax.broadcasted_iota(jnp.int32, (8 * devices, 4 * devices), 0)
    j = lax.broadcasted_iota(jnp.int32, (8 * devices, 4 * devices), 1)
    slot, device = j // devices, j % devices
    col, row = device // rows, device % rows
    along_x = (slot == 0) | (slot == 2)
    near = slot < 2
    step_col = jnp.where(near, 1, -1) * (1 - 2 * (col % 2))
    step_row = jnp.where(near, 1, -1) * (1 - 2 * (row % 2))
    to_col = jnp.where(along_x, col + step_col, col)
    to_row = jnp.where(along_x, row, row + step_row)
    shared = (to_col >= 0) & (to_col < cols) & (to_row >= 0) & (to_row < rows)

    def index(col, row):
        odd_col, odd_row = col % 2, row % 2
        edge = jnp.where(slot == 0, 1 - odd_col, jnp.where(slot == 1, 3 - odd_row, jnp.where(slot == 2, odd_col, 2 + odd_row)))
        return (col * rows + row) * 8 + edge * 2

    own, other = index(col, row), index(to_col, to_row)
    place = Place()
    k = lax.broadcasted_iota(jnp.int32, (8, 8), 0)
    from_row = lax.broadcasted_iota(jnp.int32, (8, 8), 1)
    edge = place.edges[3]
    for s in range(3):
        edge = jnp.where(k // 2 == s, place.edges[s], edge)
    pick = (from_row == 2 * edge + k % 2).astype(F32)
    mine = jnp.dot(pick, inverse_ref[...], precision=HP, preferred_element_type=F32)
    for part, out_ref in enumerate(out_refs):
        table = jnp.where(shared & (i == other + part), 0.5, jnp.where(i == own + part, jnp.where(shared, 0.5, 1.0), 0.0))
        out_ref[...] = jnp.dot(mine, table, precision=HP, preferred_element_type=F32)


def load_kernel(realiz, got_ref, near_ref, far_ref, e0, e1, e2, e3, message_ref):
    place, slots, edge_len = Place(), got_ref.shape[0], e0.shape[1]
    got = got_ref[...]
    node = got[:, realiz : realiz + 1].astype(F32) * 64.0 + got[:, realiz + 1 : realiz + 2].astype(F32)
    node = node.astype(jnp.int32)
    halves = near_ref, far_ref
    for slot, edge_ref in enumerate((e0, e1, e2, e3)):
        for start in range(0, edge_len, CHUNK):
            first = place.edges[slot] * edge_len + start
            here = lax.broadcasted_iota(jnp.int32, (slots, CHUNK), 1) + first == node
            load = lax.dot_general(got, here.astype(F32).astype(BF16), (((0,), (0,)), ((), ())), preferred_element_type=F32)
            at = slot % 2 * edge_len + start
            halves[slot // 2][:, at : at + CHUNK] = load[:realiz]
            edge_ref[:realiz, start : start + CHUNK] = load[:realiz]
    zero = jnp.zeros((realiz, 1), F32)
    write_message(message_ref, project(halves), zero, zero)


def half_product(place, half, vec_ref, matrix_ref, slot, start):
    edge_len = vec_ref.shape[1] // 2
    column = pl.multiple_of(place.edges[slot] * edge_len + start, CHUNK)
    total = None
    for i in range(2):
        row = pl.multiple_of(place.edges[2 * half + i] * edge_len, edge_len)
        block = matrix_ref[pl.ds(row, edge_len), pl.ds(column, CHUNK)]
        part = jnp.dot(vec_ref[:, i * edge_len : (i + 1) * edge_len], block, preferred_element_type=F32)
        total = part if total is None else total + part
    return total


def image_near_kernel(part_ref, g0, g1, schur_ref, precon_ref, sum_ref, rounded):
    place, edge_len = Place(), g0.shape[1]
    for i, got in enumerate((g0, g1)):
        at = pl.ds(i * edge_len, edge_len)
        value = part_ref[:, at] + received(place, i, got)
        precon_ref[:, at] = value
        rounded[:, at] = value.astype(BF16)
    for slot in range(4):
        for start in range(0, edge_len, CHUNK):
            sum_ref[:, pl.ds(slot * edge_len + start, CHUNK)] = half_product(place, 0, rounded, schur_ref, slot, start)


def image_far_kernel(part_ref, g2, g3, near_ref, sum_ref, gamma_ref, schur_ref,
                     precon_ref, image_near_ref, image_far_ref, e0, e1, e2, e3, message_ref, rounded):
    place, edge_len = Place(), g2.shape[1]
    for i, got in enumerate((g2, g3)):
        at = pl.ds(i * edge_len, edge_len)
        value = part_ref[:, at] + received(place, 2 + i, got)
        precon_ref[:, at] = value
        rounded[:, at] = value.astype(BF16)
    halves, vectors = (image_near_ref, image_far_ref), (near_ref, precon_ref)
    delta = None
    for slot, edge_ref in enumerate((e0, e1, e2, e3)):
        for start in range(0, edge_len, CHUNK):
            image = sum_ref[:, pl.ds(slot * edge_len + start, CHUNK)] + half_product(place, 1, rounded, schur_ref, slot, start)
            at = pl.ds(slot % 2 * edge_len + start, CHUNK)
            halves[slot // 2][:, at] = image
            edge_ref[: image.shape[0], pl.ds(start, CHUNK)] = image
            here = lane_parts(vectors[slot // 2][:, at] * image)
            delta = here if delta is None else delta + here
    gamma = jnp.sum(gamma_ref[...], axis=1, keepdims=True)
    delta = jnp.sum(delta, axis=1, keepdims=True)
    write_message(message_ref, project(halves), gamma, delta)


def coarse_table(gathered_ref, full):
    devices = gathered_ref.shape[0]
    for slot in range(4):
        full[slot * devices : (slot + 1) * devices] = gathered_ref[:, 0, slot * LANES : (slot + 1) * LANES]


def scalars(mode, gathered_ref, state_in, state_ref, realiz):
    total = jnp.sum(gathered_ref[:, 0, 4 * LANES : 5 * LANES], axis=0, keepdims=True)
    lane = lax.broadcasted_iota(jnp.int32, (1, LANES), 1)
    swapped = pltpu.roll(total, LANES // 2, 1)
    gamma = jnp.where(lane < realiz, total, swapped)
    delta = jnp.where(lane < realiz, swapped, total)
    if mode == "init":
        alpha, beta = gamma / delta, jnp.zeros_like(gamma)
    else:
        beta = gamma / state_in[0:1]
        alpha = gamma / (delta - beta * gamma / state_in[1:2])
    if state_ref is not None:
        state_ref[0:1] = gamma
        state_ref[1:2] = alpha
    return alpha, beta


def turn(rows, realiz):
    count = sum(row.shape[0] for row in rows)
    return jnp.concatenate([*rows, jnp.zeros((LANES - count, LANES), F32)], axis=0).T[:realiz]


def step_half(place, half, mode, image_ref, edges, columns, precon_ref, olds, news, scaled):
    edge_len = edges[0].shape[1]
    resid_in, *olds = olds
    alpha, beta = columns[:, 0:1], columns[:, 1:2]
    for i, got in enumerate(edges):
        slot = 2 * half + i
        for start in range(0, edge_len, CHUNK):
            from_ = pl.ds(start, CHUNK)
            at = pl.ds(i * edge_len + start, CHUNK)
            other = got[: image_ref.shape[0], from_]
            if place.shared[slot] is not None:
                other = jnp.where(place.shared[slot], other, 0.0)
            applied = image_ref[:, at] + other
            if mode == "load":
                resid = applied
            else:
                direction = precon_ref[:, at]
                if mode == "next":
                    direction_in, applied_in, field_in = olds
                    direction = direction + beta * direction_in[:, at]
                    applied = applied + beta * applied_in[:, at]
                    news[1][:, at] = field_in[:, at] + alpha * direction
                else:
                    news[1][:, at] = alpha * direction
                resid = resid_in[:, at] - alpha * applied
                if len(news) > 2:
                    news[2][:, at] = direction
                    news[3][:, at] = applied
            news[0][:, at] = resid
            if scaled is not None:
                scaled[:, pl.ds(slot * edge_len + start, CHUNK)] = (place.weight(slot) * resid).astype(BF16)


def whole_product(place, vec_ref, matrix_ref, slot, start):
    edge_len = vec_ref.shape[1] // 4
    column = pl.multiple_of(place.edges[slot] * edge_len + start, CHUNK)
    total = None
    for i in range(4):
        row = pl.multiple_of(place.edges[i] * edge_len, edge_len)
        block = matrix_ref[pl.ds(row, edge_len), pl.ds(column, CHUNK)]
        part = jnp.dot(vec_ref[:, i * edge_len : (i + 1) * edge_len], block, preferred_element_type=F32)
        total = part if total is None else total + part
    return total


OLD = {"load": 0, "init": 2, "next": 5}


def scalar_kernel(mode, last, gathered_ref, *refs):
    refs = list(refs)
    state_in, coarse_in, applied_in, state_ref = None, None, None, None
    if mode == "next":
        state_in = refs.pop(0)
    if not last:
        if mode != "load":
            coarse_in = refs.pop(0)
        if mode == "next":
            applied_in = refs.pop(0)
        level_mat_ref, ramp_mat_ref = refs.pop(0), refs.pop(0)
    columns_ref = refs.pop(0)
    rows = []
    if mode == "load":
        coarse_ref, = refs
        coarse_table(gathered_ref, coarse_ref)
        coarse = coarse_ref[...]
        rows.append(jnp.zeros((8, LANES), F32))
    else:
        if not last:
            state_ref, coarse_ref, applied_ref = refs
        alpha, beta = scalars(mode, gathered_ref, state_in, state_ref, columns_ref.shape[0])
        rows += [alpha, beta, jnp.zeros((6, LANES), F32)]
        if not last:
            coarse_table(gathered_ref, applied_ref)
            if mode == "next":
                applied_ref[...] = applied_ref[...] + beta * applied_in[...]
            coarse = coarse_in[...] - alpha * applied_ref[...]
            coarse_ref[...] = coarse
    if not last:
        solved = jnp.dot(level_mat_ref[...], coarse, precision=HP, preferred_element_type=F32)
        ramped = jnp.dot(ramp_mat_ref[...], coarse, precision=HP, preferred_element_type=F32)
        rows.append(solved + pltpu.roll(ramped, LANES // 2, 1))
    columns_ref[...] = turn(rows, columns_ref.shape[0])


def step_kernel(mode, *refs):
    refs = list(refs)
    take = lambda n: [refs.pop(0) for _ in range(n)]
    place = Place()
    images, edges, (columns_ref,) = take(2), take(4), take(1)
    olds = [take(OLD[mode]) for _ in range(2)]
    inverse_ref, = take(1)
    news = [take(1 if mode == "load" else 4) for _ in range(2)]
    halves, (gamma_ref,), edge_refs, (scaled,) = take(2), take(1), take(4), take(1)
    edge_len = edges[0].shape[1]
    columns = columns_ref[...]
    for half in range(2):
        precon_ref, *old = olds[half] or [None, None]
        step_half(place, half, mode, images[half], edges[2 * half : 2 * half + 2], columns, precon_ref, old, news[half], scaled)
    gamma = None
    for slot, edge_ref in enumerate(edge_refs):
        flat, ramp_by = (columns[:, 8 + 2 * slot + i : 9 + 2 * slot + i] for i in range(2))
        for start in range(0, edge_len, CHUNK):
            level, ramp = basis_parts(edge_len, start, CHUNK)
            part = whole_product(place, scaled, inverse_ref, slot, start)
            part = place.weight(slot) * (part + (flat * level + ramp_by * ramp))
            at = pl.ds(slot % 2 * edge_len + start, CHUNK)
            halves[slot // 2][:, at] = part
            edge_ref[:, pl.ds(start, CHUNK)] = part.astype(edge_ref.dtype)
            here = lane_parts(news[slot // 2][0][:, at] * part)
            gamma = here if gamma is None else gamma + here
    gamma_ref[...] = gamma


def last_kernel(mode, *refs):
    refs = list(refs)
    take = lambda n: [refs.pop(0) for _ in range(n)]
    place = Place()
    images, edges, (columns_ref,) = take(2), take(4), take(1)
    olds = [take(OLD[mode]) for _ in range(2)]
    field_ref, resid_ref = take(2)
    news = [take(2) for _ in range(2)]
    edge_len = edges[0].shape[1]
    columns = columns_ref[...]
    for half in range(2):
        precon_ref, *old = olds[half]
        step_half(place, half, mode, images[half], edges[2 * half : 2 * half + 2], columns, precon_ref, old, news[half], None)
        for i in range(2):
            to = pl.ds(pl.multiple_of(place.edges[2 * half + i] * edge_len, edge_len), edge_len)
            at = pl.ds(i * edge_len, edge_len)
            resid_ref[:, to] = news[half][0][:, at]
            field_ref[:, to] = news[half][1][:, at]


def gather(message):
    return lax.all_to_all(message, AXES, split_axis=0, concat_axis=0, tiled=True)


def body(obs_values, obs_dest, obs_node, schur, local_inverse, coarse_inverse):
    size = schur.shape[-1]
    obs_count, realiz = obs_values.shape
    cols, rows = lax.axis_size("sx"), lax.axis_size("sy")
    devices = cols * rows
    capacity = max(2, 2 * obs_count // devices)
    edges = [shape(realiz, size // 4, BF16)] * 4
    exact = [shape(realiz + PAD, size // 4)] * 4
    half, whole = shape(realiz, size // 2), shape(realiz, size)
    message = jax.ShapeDtypeStruct((devices, 1, 5 * LANES), F32)
    narrow, state_shape = shape(realiz, LANES), shape(8, LANES)
    coarse_state = shape(4 * devices, LANES)
    scratch_half, scratch_whole = pltpu.VMEM((realiz, size // 2), BF16), pltpu.VMEM((realiz, size), BF16)
    flops = 2 * realiz * size * size
    schur_mat, inverse_mat = schur[0, 0], local_inverse[0, 0]

    packed = call(
        functools.partial(pack_kernel, capacity),
        shape(devices * capacity, LANES, BF16),
        (obs_values.T, obs_dest.reshape(1, obs_count), obs_node.reshape(1, obs_count)),
        flops=COVER,
    )
    coarse_mats = call(
        functools.partial(coarse_kernel, cols, rows), [shape(8, 4 * devices)] * 2, (coarse_inverse,)
    )
    packed, *coarse_mats = lax.optimization_barrier((packed, *coarse_mats))
    got = lax.all_to_all(packed.reshape(devices, capacity, LANES), AXES, split_axis=0, concat_axis=0, tiled=True)
    *image, e0, e1, e2, e3, sent = call(
        functools.partial(load_kernel, realiz),
        [half, half, *exact, message],
        (got.reshape(devices * capacity, LANES),),
        flops=COVER,
    )
    mode, olds, states = "load", ([], []), []
    for step in range(ITERS + 1):
        last = step == ITERS
        g, gathered = exchange((e0, e1, e2, e3)), gather(sent)
        new_states = [] if last else [state_shape, coarse_state, coarse_state][1 if mode == "load" else 0 :]
        new_states = new_states[:1] if mode == "load" else new_states
        columns, *states = call(
            functools.partial(scalar_kernel, mode, last),
            [narrow, *new_states],
            (gathered, *states[:1]) if last else (gathered, *states, *coarse_mats),
        )
        ins = [*image, *g, columns, *olds[0], *olds[1]]
        if last:
            scratch = [pltpu.VMEM((realiz, size // 2), F32)] * 4
            field, resid = call(functools.partial(last_kernel, mode), [whole, whole], ins, scratch)
            return field[None, None], resid[None, None]
        count = 1 if mode == "load" else 4
        outs = call(
            functools.partial(step_kernel, mode),
            [*[half] * (2 * count), half, half, narrow, *edges],
            [*ins, inverse_mat],
            [scratch_whole],
            flops,
        )
        near, far, outs = outs[:count], outs[count : 2 * count], outs[2 * count :]
        part_near, part_far, gamma, e0, e1, e2, e3 = outs
        g = exchange((e0, e1, e2, e3))
        z_near, partial = call(
            image_near_kernel, [half, whole], (part_near, g[0], g[1], schur_mat), [scratch_half], flops // 2
        )
        z_far, *image, e0, e1, e2, e3, sent = call(
            image_far_kernel,
            [half, half, half, *exact, message],
            (part_far, g[2], g[3], z_near, partial, gamma, schur_mat),
            [scratch_half],
            flops // 2,
        )
        mode = "init" if step == 0 else "next"
        olds = [[z, new[0]] + ([] if step == 0 else [new[2], new[3], new[1]]) for z, new in ((z_near, near), (z_far, far))]


def solution(mesh):
    placed = (
        P(AXES, None),
        P(AXES, None),
        P(AXES),
        P("sx", "sy", None, None),
        P("sx", "sy", None, None),
        P(AXES, None),
    )
    return jax.shard_map(
        body,
        mesh=mesh,
        in_specs=placed,
        out_specs=(P("sx", "sy", None, None), P("sx", "sy", None, None)),
        check_vma=False,
    )
```

```python
import functools

import jax
import jax.numpy as jnp
from jax import lax
from jax.experimental import pallas as pl
from jax.experimental.pallas import tpu as pltpu
from jax.sharding import PartitionSpec as P

ITERS = 6
PAD = 16
COVER = 8e9
LANES = 128
CHUNK = 256
HP = lax.Precision.HIGHEST
F32 = jnp.float32
BF16 = jnp.bfloat16
VM = pl.BlockSpec(memory_space=pltpu.VMEM)
AXES = ("sx", "sy")


def call(kernel, outs, args, scratch=(), flops=0, spec=VM):
    size = sum(a.size * a.dtype.itemsize for a in args)
    return pl.pallas_call(
        kernel,
        out_shape=outs,
        in_specs=[spec] * len(args),
        out_specs=jax.tree.map(lambda _: VM, outs),
        scratch_shapes=list(scratch),
        compiler_params=pltpu.CompilerParams(vmem_limit_bytes=(8 if spec is VM else 56) << 20),
        cost_estimate=pl.CostEstimate(flops=int(flops), bytes_accessed=size, transcendentals=0),
    )(*args)


def shape(rows, columns, dtype=F32):
    return jax.ShapeDtypeStruct((rows, columns), dtype)


def edge_of(slot, odd_col, odd_row):
    return (1 - odd_col, 3 - odd_row, odd_col, 2 + odd_row)[slot]


class Place:
    def __init__(self):
        col, row = lax.axis_index("sx"), lax.axis_index("sy")
        cols, rows = lax.axis_size("sx"), lax.axis_size("sy")
        odd_col, odd_row = lax.rem(col, 2), lax.rem(row, 2)
        self.edges = [edge_of(slot, odd_col, odd_row) for slot in range(4)]
        far_col = jnp.where(odd_col == 1, col < cols - 1, col > 0)
        far_row = jnp.where(odd_row == 1, row < rows - 1, row > 0)
        self.shared = (None, None, far_col, far_row)

    def weight(self, slot):
        shared = self.shared[slot]
        return F32(0.5) if shared is None else jnp.where(shared, F32(0.5), F32(1.0))


def swaps():
    cols, rows = lax.axis_size("sx"), lax.axis_size("sy")
    plans = [], [], [], []
    for col in range(cols):
        for row in range(rows):
            across = col + (1 if col % 2 else -1)
            beyond = row + (1 if row % 2 else -1)
            far_sx = (across, row) if 0 <= across < cols else (col, row ^ 1)
            partners = (col ^ 1, row), (col, row ^ 1), far_sx, (col, beyond % rows)
            for plan, (to_col, to_row) in zip(plans, partners, strict=True):
                plan.append((col * rows + row, to_col * rows + to_row))
    return plans


def exchange(edges):
    plans = swaps()
    got = [None] * 4
    for slot in (2, 0, 3, 1):
        got[slot] = lax.ppermute(edges[slot], AXES, plans[slot])
    return got


def basis_parts(edge_len, start, width):
    node = lax.broadcasted_iota(jnp.int32, (1, width), 1) + start
    offset = node.astype(F32) - (edge_len - 1) / 2.0
    level = 1.0 / jnp.sqrt(F32(edge_len))
    norm = jnp.sqrt(F32(edge_len * (edge_len * edge_len - 1) / 12.0))
    return level, offset / norm


def lane_parts(value):
    return sum(value[:, i : i + LANES] for i in range(LANES, value.shape[1], LANES)) + value[:, :LANES]


def project(halves):
    edge_len = halves[0].shape[1] // 2
    columns = []
    for slot in range(4):
        flat = ramped = None
        for start in range(0, edge_len, CHUNK):
            at = slot % 2 * edge_len + start
            part = halves[slot // 2][:, at : at + CHUNK]
            ramp = basis_parts(edge_len, start, CHUNK)[1]
            one, two = lane_parts(part), lane_parts(part * ramp)
            flat = one if flat is None else flat + one
            ramped = two if ramped is None else ramped + two
        level = basis_parts(edge_len, 0, LANES)[0]
        columns.append(jnp.sum(flat, axis=1, keepdims=True) * level)
        columns.append(jnp.sum(ramped, axis=1, keepdims=True))
    return columns


def write_message(message_ref, columns, gamma, delta):
    rows = gamma.shape[0]
    lane = lax.broadcasted_iota(jnp.int32, (rows, LANES), 1)
    table = jnp.zeros((rows, LANES), F32)
    order = [*columns[0::2], gamma, *columns[1::2], delta]
    for i, column in enumerate(order):
        table = jnp.where(lane == (i if i < 5 else i + 3), column, table)
    turned = table.T
    block = jnp.concatenate([turned[0:8], turned[8:16]], axis=1)
    for i in range(5):
        row = jnp.broadcast_to(block[i : i + 1][None], (message_ref.shape[0], 1, LANES))
        message_ref[:, :, i * LANES : (i + 1) * LANES] = row


def first_kernel(capacity, cols, rows, values_in, dest_in, node_in, inverse_in, out_ref, level_mat_ref, ramp_mat_ref,
                 values_ref, dest_ref, node_ref, inverse_ref, sems):
    pairs = ((values_in, values_ref), (dest_in, dest_ref), (node_in, node_ref), (inverse_in, inverse_ref))
    copies = [pltpu.make_async_copy(source, to, sems.at[i]) for i, (source, to) in enumerate(pairs)]
    for copy in copies:
        copy.start()
    for copy in copies:
        copy.wait()
    pack(capacity, values_ref, dest_ref, node_ref, out_ref)
    coarse_matrices(cols, rows, inverse_ref, (level_mat_ref, ramp_mat_ref))


def pack(capacity, values_ref, dest_ref, node_ref, out_ref):
    realiz, count = values_ref.shape
    slots = out_ref.shape[0]
    dest, node = dest_ref[...], node_ref[...]
    hit = lax.broadcasted_iota(jnp.int32, (slots // capacity, count), 0) == dest
    before = lax.broadcasted_iota(jnp.int32, (count, count), 0) < lax.broadcasted_iota(jnp.int32, (count, count), 1)
    hit = hit.astype(F32)
    earlier = jnp.dot(hit.astype(BF16), before.astype(F32).astype(BF16), preferred_element_type=F32)
    rank = jnp.sum(hit * earlier, axis=0, keepdims=True).astype(jnp.int32)
    slot = dest * capacity + rank
    high, low = (node // 64).astype(F32), lax.rem(node, 64).astype(F32)
    side = lax.broadcasted_iota(jnp.int32, (LANES - realiz, count), 0)
    codes = jnp.where(side == 0, high, jnp.where(side == 1, low, 0.0)).astype(BF16)
    full = jnp.concatenate([values_ref[...], codes], axis=0)
    choose = (lax.broadcasted_iota(jnp.int32, (slots, count), 0) == slot).astype(F32).astype(BF16)
    out = lax.dot_general(choose, full, (((1,), (1,)), ((), ())), preferred_element_type=F32)
    out_ref[...] = out.astype(BF16)


def coarse_matrices(cols, rows, inverse_ref, out_refs):
    devices = cols * rows
    i = lax.broadcasted_iota(jnp.int32, (8 * devices, 4 * devices), 0)
    j = lax.broadcasted_iota(jnp.int32, (8 * devices, 4 * devices), 1)
    slot, device = j // devices, j % devices
    col, row = device // rows, device % rows
    along_x = (slot == 0) | (slot == 2)
    near = slot < 2
    step_col = jnp.where(near, 1, -1) * (1 - 2 * (col % 2))
    step_row = jnp.where(near, 1, -1) * (1 - 2 * (row % 2))
    to_col = jnp.where(along_x, col + step_col, col)
    to_row = jnp.where(along_x, row, row + step_row)
    shared = (to_col >= 0) & (to_col < cols) & (to_row >= 0) & (to_row < rows)

    def index(col, row):
        odd_col, odd_row = col % 2, row % 2
        edge = jnp.where(slot == 0, 1 - odd_col, jnp.where(slot == 1, 3 - odd_row, jnp.where(slot == 2, odd_col, 2 + odd_row)))
        return (col * rows + row) * 8 + edge * 2

    own, other = index(col, row), index(to_col, to_row)
    place = Place()
    k = lax.broadcasted_iota(jnp.int32, (8, 8), 0)
    from_row = lax.broadcasted_iota(jnp.int32, (8, 8), 1)
    edge = place.edges[3]
    for s in range(3):
        edge = jnp.where(k // 2 == s, place.edges[s], edge)
    pick = (from_row == 2 * edge + k % 2).astype(F32)
    mine = jnp.dot(pick, inverse_ref[...], precision=HP, preferred_element_type=F32)
    for part, out_ref in enumerate(out_refs):
        table = jnp.where(shared & (i == other + part), 0.5, jnp.where(i == own + part, jnp.where(shared, 0.5, 1.0), 0.0))
        out_ref[...] = jnp.dot(mine, table, precision=HP, preferred_element_type=F32)


def load_kernel(realiz, got_ref, near_ref, far_ref, e0, e1, e2, e3, message_ref):
    place, slots, edge_len = Place(), got_ref.shape[0], e0.shape[1]
    got = got_ref[...]
    node = got[:, realiz : realiz + 1].astype(F32) * 64.0 + got[:, realiz + 1 : realiz + 2].astype(F32)
    node = node.astype(jnp.int32)
    halves = near_ref, far_ref
    for slot, edge_ref in enumerate((e0, e1, e2, e3)):
        for start in range(0, edge_len, CHUNK):
            first = place.edges[slot] * edge_len + start
            here = lax.broadcasted_iota(jnp.int32, (slots, CHUNK), 1) + first == node
            load = lax.dot_general(got, here.astype(F32).astype(BF16), (((0,), (0,)), ((), ())), preferred_element_type=F32)
            at = slot % 2 * edge_len + start
            halves[slot // 2][:, at : at + CHUNK] = load[:realiz]
            edge_ref[:realiz, start : start + CHUNK] = load[:realiz]
    zero = jnp.zeros((realiz, 1), F32)
    write_message(message_ref, project(halves), zero, zero)


def product(place, slots, vec_ref, matrix_ref, slot, start):
    edge_len = vec_ref.shape[1] // len(slots)
    column = pl.multiple_of(place.edges[slot] * edge_len + start, CHUNK)
    total = None
    for i, source in enumerate(slots):
        row = pl.multiple_of(place.edges[source] * edge_len, edge_len)
        block = matrix_ref[pl.ds(row, edge_len), pl.ds(column, CHUNK)]
        part = jnp.dot(vec_ref[:, i * edge_len : (i + 1) * edge_len], block, preferred_element_type=F32)
        total = part if total is None else total + part
    return total


def image_near_kernel(part_ref, g0, g1, schur_ref, precon_ref, sum_ref, rounded):
    place, edge_len = Place(), g0.shape[1]
    for i, got in enumerate((g0, g1)):
        at = pl.ds(i * edge_len, edge_len)
        value = part_ref[:, at] + got[...].astype(F32)
        precon_ref[:, at] = value
        rounded[:, at] = value.astype(BF16)
    for slot in range(4):
        for start in range(0, edge_len, CHUNK):
            sum_ref[:, pl.ds(slot * edge_len + start, CHUNK)] = product(place, (0, 1), rounded, schur_ref, slot, start)


def image_far_kernel(part_ref, g2, g3, near_ref, sum_ref, gamma_ref, schur_ref, *refs):
    precon_ref, image_near_ref, image_far_ref, e0, e1, e2, e3, message_ref, rounded = refs[-9:]
    place, edge_len = Place(), g2.shape[1]
    for i, got in enumerate((g2, g3)):
        at = pl.ds(i * edge_len, edge_len)
        value = part_ref[:, at] + jnp.where(place.shared[2 + i], got[...].astype(F32), 0.0)
        precon_ref[:, at] = value
        rounded[:, at] = value.astype(BF16)
    halves, vectors = (image_near_ref, image_far_ref), (near_ref, precon_ref)
    delta = None
    for slot, edge_ref in enumerate((e0, e1, e2, e3)):
        for start in range(0, edge_len, CHUNK):
            image = sum_ref[:, pl.ds(slot * edge_len + start, CHUNK)] + product(place, (2, 3), rounded, schur_ref, slot, start)
            at = pl.ds(slot % 2 * edge_len + start, CHUNK)
            halves[slot // 2][:, at] = image
            edge_ref[: image.shape[0], pl.ds(start, CHUNK)] = image
            here = lane_parts(vectors[slot // 2][:, at] * image)
            delta = here if delta is None else delta + here
    gamma = jnp.sum(gamma_ref[...], axis=1, keepdims=True)
    delta = jnp.sum(delta, axis=1, keepdims=True)
    write_message(message_ref, project(halves), gamma, delta)


def coarse_table(gathered_ref, full):
    devices = gathered_ref.shape[0]
    for slot in range(4):
        full[slot * devices : (slot + 1) * devices] = gathered_ref[:, 0, slot * LANES : (slot + 1) * LANES]


def scalars(mode, gathered_ref, state_in, state_ref, realiz):
    total = jnp.sum(gathered_ref[:, 0, 4 * LANES : 5 * LANES], axis=0, keepdims=True)
    lane = lax.broadcasted_iota(jnp.int32, (1, LANES), 1)
    swapped = pltpu.roll(total, LANES // 2, 1)
    gamma = jnp.where(lane < realiz, total, swapped)
    delta = jnp.where(lane < realiz, swapped, total)
    if mode == "init":
        alpha, beta = gamma / delta, jnp.zeros_like(gamma)
    else:
        beta = gamma / state_in[0:1]
        alpha = gamma / (delta - beta * gamma / state_in[1:2])
    if state_ref is not None:
        state_ref[0:1] = gamma
        state_ref[1:2] = alpha
    return alpha, beta


def turn(rows, realiz):
    count = sum(row.shape[0] for row in rows)
    return jnp.concatenate([*rows, jnp.zeros((LANES - count, LANES), F32)], axis=0).T[:realiz]


def new_residual(place, slot, mode, columns, image_ref, got_ref, old, at, start):
    got = got_ref[: image_ref.shape[0], pl.ds(start, CHUNK)]
    shared = place.shared[slot]
    applied = image_ref[:, at] + (got if shared is None else jnp.where(shared, got, 0.0))
    if mode == "load":
        return None, applied
    if mode == "next":
        applied = applied + columns[:, 1:2] * old[1][:, at]
    return applied, old[0][:, at] - columns[:, 0:1] * applied


def new_field(mode, columns, precon_ref, old, at):
    direction = precon_ref[:, at]
    if mode == "init":
        return direction, columns[:, 0:1] * direction
    direction = direction + columns[:, 1:2] * old[0][:, at]
    return direction, old[1][:, at] + columns[:, 0:1] * direction


OLD = {"load": 0, "init": 1, "next": 2}


def step_kernel(mode, *refs):
    refs = list(refs)
    take = lambda n: [refs.pop(0) for _ in range(n)]
    place = Place()
    images, edges, (gathered_ref,) = take(2), take(4), take(1)
    olds = [take(OLD[mode]) for _ in range(2)]
    state_in, = take(1) if mode == "next" else (None,)
    coarse_in, = take(1) if mode != "load" else (None,)
    applied_in, = take(1) if mode == "next" else (None,)
    level_mat_ref, ramp_mat_ref, inverse_ref = take(3)
    news = [take(1 if mode == "load" else 2) for _ in range(2)]
    columns_ref, coarse_ref = take(2)
    state_ref, applied_ref = take(2) if mode != "load" else (None, None)
    halves, (gamma_ref,), edge_refs, (scaled,) = take(2), take(1), take(4), take(1)
    realiz, edge_len = images[0].shape[0], edges[0].shape[1]
    if mode == "load":
        coarse_table(gathered_ref, coarse_ref)
        coarse = coarse_ref[...]
        rows, columns = [jnp.zeros((8, LANES), F32)], None
    else:
        alpha, beta = scalars(mode, gathered_ref, state_in, state_ref, realiz)
        columns = turn([alpha, beta], realiz)
        coarse_table(gathered_ref, applied_ref)
        if mode == "next":
            applied_ref[...] = applied_ref[...] + beta * applied_in[...]
        coarse = coarse_in[...] - alpha * applied_ref[...]
        coarse_ref[...] = coarse
        rows = [alpha, beta, jnp.zeros((6, LANES), F32)]
    for slot in range(4):
        half = slot // 2
        for start in range(0, edge_len, CHUNK):
            at = pl.ds(slot % 2 * edge_len + start, CHUNK)
            applied, resid = new_residual(place, slot, mode, columns, images[half], edges[slot], olds[half], at, start)
            news[half][0][:, at] = resid
            if applied is not None:
                news[half][1][:, at] = applied
            scaled[:, pl.ds(slot * edge_len + start, CHUNK)] = (place.weight(slot) * resid).astype(BF16)
    level = jnp.dot(level_mat_ref[...], coarse, precision=HP, preferred_element_type=F32)
    ramp = jnp.dot(ramp_mat_ref[...], coarse, precision=HP, preferred_element_type=F32)
    rows.append(level + pltpu.roll(ramp, LANES // 2, 1))
    columns = turn(rows, realiz)
    columns_ref[...] = columns
    gamma = None
    for slot, edge_ref in enumerate(edge_refs):
        flat, ramp_by = (columns[:, 8 + 2 * slot + i : 9 + 2 * slot + i] for i in range(2))
        for start in range(0, edge_len, CHUNK):
            level, ramp = basis_parts(edge_len, start, CHUNK)
            part = product(place, (0, 1, 2, 3), scaled, inverse_ref, slot, start)
            part = place.weight(slot) * (part + (flat * level + ramp_by * ramp))
            at = pl.ds(slot % 2 * edge_len + start, CHUNK)
            halves[slot // 2][:, at] = part
            edge_ref[:, pl.ds(start, CHUNK)] = part.astype(BF16)
            here = lane_parts(news[slot // 2][0][:, at] * part)
            gamma = here if gamma is None else gamma + here
    gamma_ref[...] = gamma


def field_kernel(mode, columns_ref, *refs):
    old = 0 if mode == "init" else 2
    columns = columns_ref[...]
    for half in range(2):
        precon_ref, *olds = refs[half * (1 + old) : (half + 1) * (1 + old)]
        direction_ref, field_ref = refs[2 * (1 + old) + 2 * half : 2 * (1 + old) + 2 * half + 2]
        for start in range(0, precon_ref.shape[1], CHUNK):
            at = pl.ds(start, CHUNK)
            direction_ref[:, at], field_ref[:, at] = new_field(mode, columns, precon_ref, olds, at)


def last_kernel(*refs):
    refs = list(refs)
    take = lambda n: [refs.pop(0) for _ in range(n)]
    place = Place()
    images, edges, (gathered_ref,) = take(2), take(4), take(1)
    olds, (state_in,), tracks = [take(2) for _ in range(2)], take(1), [take(3) for _ in range(2)]
    field_ref, resid_ref = refs
    realiz, edge_len = images[0].shape[0], edges[0].shape[1]
    columns = turn(scalars("next", gathered_ref, state_in, None, realiz), realiz)
    for slot in range(4):
        half = slot // 2
        for start in range(0, edge_len, CHUNK):
            at = pl.ds(slot % 2 * edge_len + start, CHUNK)
            to = pl.ds(pl.multiple_of(place.edges[slot] * edge_len + start, CHUNK), CHUNK)
            _, resid_ref[:, to] = new_residual(place, slot, "next", columns, images[half], edges[slot], olds[half], at, start)
            _, field_ref[:, to] = new_field("next", columns, tracks[half][0], tracks[half][1:], at)


def gather(message):
    return lax.all_to_all(message, AXES, split_axis=0, concat_axis=0, tiled=True)


def body(obs_values, obs_dest, obs_node, schur, local_inverse, coarse_inverse):
    size = schur.shape[-1]
    obs_count, realiz = obs_values.shape
    cols, rows = lax.axis_size("sx"), lax.axis_size("sy")
    devices = cols * rows
    capacity = max(2, 2 * obs_count // devices)
    edge = shape(realiz, size // 4, BF16)
    exact = [shape(realiz + PAD, size // 4)] * 4
    half, whole = shape(realiz, size // 2), shape(realiz, size)
    message = jax.ShapeDtypeStruct((devices, 1, 5 * LANES), F32)
    narrow, state_shape = shape(realiz, LANES), shape(8, LANES)
    coarse_state = shape(4 * devices, LANES)
    scratch_half = pltpu.VMEM((realiz, size // 2), BF16)
    flops = 2 * realiz * size * size
    schur_mat, inverse_mat = schur[0, 0], local_inverse[0, 0]

    packed, *coarse_mats = call(
        functools.partial(first_kernel, capacity, cols, rows),
        [shape(devices * capacity, LANES, BF16), *[shape(8, 4 * devices)] * 2],
        (obs_values.T, obs_dest.reshape(1, obs_count), obs_node.reshape(1, obs_count), coarse_inverse),
        [
            pltpu.VMEM((realiz, obs_count), BF16),
            *[pltpu.VMEM((1, obs_count), jnp.int32)] * 2,
            pltpu.VMEM(coarse_inverse.shape, F32),
            pltpu.SemaphoreType.DMA((4,)),
        ],
        COVER,
        pl.BlockSpec(memory_space=pltpu.HBM),
    )
    got = lax.all_to_all(packed.reshape(devices, capacity, LANES), AXES, split_axis=0, concat_axis=0, tiled=True)
    *image, e0, e1, e2, e3, sent = call(
        functools.partial(load_kernel, realiz),
        [half, half, *exact, message],
        (got.reshape(devices * capacity, LANES),),
        flops=COVER,
    )
    mode, olds, states = "load", ([], []), []
    for step in range(ITERS + 1):
        g, gathered = exchange((e0, e1, e2, e3)), gather(sent)
        ins = [*image, *g, gathered, *olds[0], *olds[1]]
        if step == ITERS:
            field, resid = call(last_kernel, [whole, whole], [*ins, states[0], z[0], *track[0], z[1], *track[1]])
            return field[None, None], resid[None, None]
        count, state_count = (1, 1) if mode == "load" else (2, 3)
        outs = call(
            functools.partial(step_kernel, mode),
            [*[half] * (2 * count), narrow, *[coarse_state, state_shape, coarse_state][:state_count], half, half, narrow, *[edge] * 4],
            [*ins, *states, *coarse_mats, inverse_mat],
            [pltpu.VMEM((realiz, size), BF16)],
            flops,
        )
        olds, (columns, coarse), outs = (outs[:count], outs[count : 2 * count]), outs[2 * count : 2 * count + 2], outs[2 * count + 2 :]
        states, outs = [*outs[:1], coarse, *outs[1:2]] if mode != "load" else [coarse], outs[state_count - 1 :]
        part_near, part_far, gamma, e0, e1, e2, e3 = outs
        g = exchange((e0, e1, e2, e3))
        if step == 0:
            track = (), ()
        else:
            outs = call(
                functools.partial(field_kernel, mode), [half] * 4, (columns, z[0], *track[0], z[1], *track[1]), flops=1
            )
            track = outs[:2], outs[2:]
        z_near, partial = call(
            image_near_kernel, [half, whole], (part_near, g[0], g[1], schur_mat), [scratch_half], flops // 2
        )
        z_far, *image, e0, e1, e2, e3, sent = call(
            image_far_kernel,
            [half, half, half, *exact, message],
            (part_far, g[2], g[3], z_near, partial, gamma, schur_mat, *track[0][:1]),
            [scratch_half],
            flops // 2,
        )
        z = z_near, z_far
        mode = "init" if step == 0 else "next"


def solution(mesh):
    placed = (
        P(AXES, None),
        P(AXES, None),
        P(AXES),
        P("sx", "sy", None, None),
        P("sx", "sy", None, None),
        P(AXES, None),
    )
    return jax.shard_map(
        body,
        mesh=mesh,
        in_specs=placed,
        out_specs=(P("sx", "sy", None, None), P("sx", "sy", None, None)),
        check_vma=False,
    )
```

```python
import functools

import jax
import jax.numpy as jnp
from jax import lax
from jax.experimental import pallas as pl
from jax.experimental.pallas import tpu as pltpu
from jax.sharding import PartitionSpec as P

ITERS = 6
ORDER = (1, 0, 2, 3)
PAD = 16
COVER = 8e9
LANES = 128
CHUNK = 256
HP = lax.Precision.HIGHEST
F32 = jnp.float32
BF16 = jnp.bfloat16
VM = pl.BlockSpec(memory_space=pltpu.VMEM)
AXES = ("sx", "sy")


def call(kernel, outs, args, scratch=(), flops=0, spec=VM):
    size = sum(a.size * a.dtype.itemsize for a in args)
    return pl.pallas_call(
        kernel,
        out_shape=outs,
        in_specs=[spec] * len(args),
        out_specs=jax.tree.map(lambda _: VM, outs),
        scratch_shapes=list(scratch),
        compiler_params=pltpu.CompilerParams(vmem_limit_bytes=(8 if spec is VM else 56) << 20),
        cost_estimate=pl.CostEstimate(flops=int(flops), bytes_accessed=size, transcendentals=0),
    )(*args)


def shape(rows, columns, dtype=F32):
    return jax.ShapeDtypeStruct((rows, columns), dtype)


def edge_of(slot, odd_col, odd_row):
    return (1 - odd_col, 3 - odd_row, odd_col, 2 + odd_row)[slot]


class Place:
    def __init__(self):
        col, row = lax.axis_index("sx"), lax.axis_index("sy")
        cols, rows = lax.axis_size("sx"), lax.axis_size("sy")
        odd_col, odd_row = lax.rem(col, 2), lax.rem(row, 2)
        self.edges = [edge_of(slot, odd_col, odd_row) for slot in range(4)]
        far_col = jnp.where(odd_col == 1, col < cols - 1, col > 0)
        far_row = jnp.where(odd_row == 1, row < rows - 1, row > 0)
        self.shared = (None, None, far_col, far_row)

    def weight(self, slot):
        shared = self.shared[slot]
        return F32(0.5) if shared is None else jnp.where(shared, F32(0.5), F32(1.0))


def swaps():
    cols, rows = lax.axis_size("sx"), lax.axis_size("sy")
    plans = [], [], [], []
    for col in range(cols):
        for row in range(rows):
            across = col + (1 if col % 2 else -1)
            beyond = row + (1 if row % 2 else -1)
            far_sx = (across, row) if 0 <= across < cols else (col, row ^ 1)
            partners = (col ^ 1, row), (col, row ^ 1), far_sx, (col, beyond % rows)
            for plan, (to_col, to_row) in zip(plans, partners, strict=True):
                plan.append((col * rows + row, to_col * rows + to_row))
    return plans


def exchange(edges):
    plans = swaps()
    got = [None] * 4
    for slot in (2, 0, 3, 1):
        got[slot] = lax.ppermute(edges[slot], AXES, plans[slot])
    return got


def basis_parts(edge_len, start, width):
    node = lax.broadcasted_iota(jnp.int32, (1, width), 1) + start
    offset = node.astype(F32) - (edge_len - 1) / 2.0
    level = 1.0 / jnp.sqrt(F32(edge_len))
    norm = jnp.sqrt(F32(edge_len * (edge_len * edge_len - 1) / 12.0))
    return level, offset / norm


def lane_parts(value):
    return sum(value[:, i : i + LANES] for i in range(LANES, value.shape[1], LANES)) + value[:, :LANES]


def project(halves):
    edge_len = halves[0].shape[1] // 2
    columns = []
    for slot in range(4):
        flat = ramped = None
        for start in range(0, edge_len, CHUNK):
            at = slot % 2 * edge_len + start
            part = halves[slot // 2][:, at : at + CHUNK]
            ramp = basis_parts(edge_len, start, CHUNK)[1]
            one, two = lane_parts(part), lane_parts(part * ramp)
            flat = one if flat is None else flat + one
            ramped = two if ramped is None else ramped + two
        level = basis_parts(edge_len, 0, LANES)[0]
        columns.append(jnp.sum(flat, axis=1, keepdims=True) * level)
        columns.append(jnp.sum(ramped, axis=1, keepdims=True))
    return columns


def write_message(message_ref, columns, gamma, delta):
    rows = gamma.shape[0]
    lane = lax.broadcasted_iota(jnp.int32, (rows, LANES), 1)
    table = jnp.zeros((rows, LANES), F32)
    order = [*columns[0::2], gamma, *columns[1::2], delta]
    for i, column in enumerate(order):
        table = jnp.where(lane == (i if i < 5 else i + 3), column, table)
    turned = table.T
    block = jnp.concatenate([turned[0:8], turned[8:16]], axis=1)
    for i in range(5):
        row = jnp.broadcast_to(block[i : i + 1][None], (message_ref.shape[0], 1, LANES))
        message_ref[:, :, i * LANES : (i + 1) * LANES] = row


def first_kernel(capacity, cols, rows, values_in, dest_in, node_in, inverse_in, out_ref, level_mat_ref, ramp_mat_ref,
                 values_ref, dest_ref, node_ref, inverse_ref, sems):
    pairs = ((values_in, values_ref), (dest_in, dest_ref), (node_in, node_ref), (inverse_in, inverse_ref))
    copies = [pltpu.make_async_copy(source, to, sems.at[i]) for i, (source, to) in enumerate(pairs)]
    for copy in copies:
        copy.start()
    for copy in copies:
        copy.wait()
    pack(capacity, values_ref, dest_ref, node_ref, out_ref)
    coarse_matrices(cols, rows, inverse_ref, (level_mat_ref, ramp_mat_ref))


def pack(capacity, values_ref, dest_ref, node_ref, out_ref):
    realiz, count = values_ref.shape
    slots = out_ref.shape[0]
    dest, node = dest_ref[...], node_ref[...]
    hit = lax.broadcasted_iota(jnp.int32, (slots // capacity, count), 0) == dest
    before = lax.broadcasted_iota(jnp.int32, (count, count), 0) < lax.broadcasted_iota(jnp.int32, (count, count), 1)
    hit = hit.astype(F32)
    earlier = jnp.dot(hit.astype(BF16), before.astype(F32).astype(BF16), preferred_element_type=F32)
    rank = jnp.sum(hit * earlier, axis=0, keepdims=True).astype(jnp.int32)
    slot = dest * capacity + rank
    high, low = (node // 64).astype(F32), lax.rem(node, 64).astype(F32)
    side = lax.broadcasted_iota(jnp.int32, (LANES - realiz, count), 0)
    codes = jnp.where(side == 0, high, jnp.where(side == 1, low, 0.0)).astype(BF16)
    full = jnp.concatenate([values_ref[...], codes], axis=0)
    choose = (lax.broadcasted_iota(jnp.int32, (slots, count), 0) == slot).astype(F32).astype(BF16)
    out = lax.dot_general(choose, full, (((1,), (1,)), ((), ())), preferred_element_type=F32)
    out_ref[...] = out.astype(BF16)


def coarse_matrices(cols, rows, inverse_ref, out_refs):
    devices = cols * rows
    i = lax.broadcasted_iota(jnp.int32, (8 * devices, 4 * devices), 0)
    j = lax.broadcasted_iota(jnp.int32, (8 * devices, 4 * devices), 1)
    slot, device = j // devices, j % devices
    col, row = device // rows, device % rows
    along_x = (slot == 0) | (slot == 2)
    near = slot < 2
    step_col = jnp.where(near, 1, -1) * (1 - 2 * (col % 2))
    step_row = jnp.where(near, 1, -1) * (1 - 2 * (row % 2))
    to_col = jnp.where(along_x, col + step_col, col)
    to_row = jnp.where(along_x, row, row + step_row)
    shared = (to_col >= 0) & (to_col < cols) & (to_row >= 0) & (to_row < rows)

    def index(col, row):
        odd_col, odd_row = col % 2, row % 2
        edge = jnp.where(slot == 0, 1 - odd_col, jnp.where(slot == 1, 3 - odd_row, jnp.where(slot == 2, odd_col, 2 + odd_row)))
        return (col * rows + row) * 8 + edge * 2

    own, other = index(col, row), index(to_col, to_row)
    place = Place()
    k = lax.broadcasted_iota(jnp.int32, (8, 8), 0)
    from_row = lax.broadcasted_iota(jnp.int32, (8, 8), 1)
    edge = place.edges[3]
    for s in range(3):
        edge = jnp.where(k // 2 == s, place.edges[s], edge)
    pick = (from_row == 2 * edge + k % 2).astype(F32)
    mine = jnp.dot(pick, inverse_ref[...], precision=HP, preferred_element_type=F32)
    for part, out_ref in enumerate(out_refs):
        table = jnp.where(shared & (i == other + part), 0.5, jnp.where(i == own + part, jnp.where(shared, 0.5, 1.0), 0.0))
        out_ref[...] = jnp.dot(mine, table, precision=HP, preferred_element_type=F32)


def load_kernel(realiz, got_ref, near_ref, far_ref, e0, e1, e2, e3, message_ref):
    place, slots, edge_len = Place(), got_ref.shape[0], e0.shape[1]
    got = got_ref[...]
    node = got[:, realiz : realiz + 1].astype(F32) * 64.0 + got[:, realiz + 1 : realiz + 2].astype(F32)
    node = node.astype(jnp.int32)
    halves = near_ref, far_ref
    for slot, edge_ref in enumerate((e0, e1, e2, e3)):
        for start in range(0, edge_len, CHUNK):
            first = place.edges[slot] * edge_len + start
            here = lax.broadcasted_iota(jnp.int32, (slots, CHUNK), 1) + first == node
            load = lax.dot_general(got, here.astype(F32).astype(BF16), (((0,), (0,)), ((), ())), preferred_element_type=F32)
            at = slot % 2 * edge_len + start
            halves[slot // 2][:, at : at + CHUNK] = load[:realiz]
            edge_ref[:realiz, start : start + CHUNK] = load[:realiz]
    zero = jnp.zeros((realiz, 1), F32)
    write_message(message_ref, project(halves), zero, zero)


def product(place, slots, vec_ref, matrix_ref, slot, start):
    edge_len = vec_ref.shape[1] // len(slots)
    column = pl.multiple_of(place.edges[slot] * edge_len + start, CHUNK)
    total = None
    for i, source in enumerate(slots):
        row = pl.multiple_of(place.edges[source] * edge_len, edge_len)
        block = matrix_ref[pl.ds(row, edge_len), pl.ds(column, CHUNK)]
        part = jnp.dot(vec_ref[:, i * edge_len : (i + 1) * edge_len], block, preferred_element_type=F32)
        total = part if total is None else total + part
    return total


def image_first_kernel(part_ref, got_ref, schur_ref, precon_ref, sum_ref, rounded):
    place, edge_len = Place(), got_ref.shape[1]
    value = part_ref[...] + jnp.where(place.shared[2], got_ref[...].astype(F32), 0.0)
    precon_ref[...] = value
    rounded[...] = value.astype(BF16)
    for slot in range(4):
        for start in range(0, edge_len, CHUNK):
            sum_ref[:, pl.ds(slot * edge_len + start, CHUNK)] = product(place, (2,), rounded, schur_ref, slot, start)


def image_near_kernel(part_ref, g0, g1, sum_in, schur_ref, precon_ref, sum_ref, rounded):
    place, edge_len = Place(), g0.shape[1]
    for i, got in enumerate((g0, g1)):
        at = pl.ds(i * edge_len, edge_len)
        value = part_ref[:, at] + got[...].astype(F32)
        precon_ref[:, at] = value
        rounded[:, at] = value.astype(BF16)
    for slot in range(4):
        for start in range(0, edge_len, CHUNK):
            at = pl.ds(slot * edge_len + start, CHUNK)
            sum_ref[:, at] = sum_in[:, at] + product(place, (0, 1), rounded, schur_ref, slot, start)


def image_last_kernel(part_ref, g3, first_ref, near_ref, sum_ref, gamma_ref, schur_ref, *refs):
    precon_ref, image_near_ref, image_far_ref, e0, e1, e2, e3, message_ref, rounded = refs[-9:]
    place, edge_len = Place(), g3.shape[1]
    value = part_ref[...] + jnp.where(place.shared[3], g3[...].astype(F32), 0.0)
    precon_ref[:, pl.ds(0, edge_len)] = first_ref[...]
    precon_ref[:, pl.ds(edge_len, edge_len)] = value
    rounded[...] = value.astype(BF16)
    halves, vectors = (image_near_ref, image_far_ref), (near_ref, precon_ref)
    delta = None
    for slot, edge_ref in enumerate((e0, e1, e2, e3)):
        for start in range(0, edge_len, CHUNK):
            image = sum_ref[:, pl.ds(slot * edge_len + start, CHUNK)] + product(place, (3,), rounded, schur_ref, slot, start)
            at = pl.ds(slot % 2 * edge_len + start, CHUNK)
            halves[slot // 2][:, at] = image
            edge_ref[: image.shape[0], pl.ds(start, CHUNK)] = image
            here = lane_parts(vectors[slot // 2][:, at] * image)
            delta = here if delta is None else delta + here
    gamma = jnp.sum(gamma_ref[...], axis=1, keepdims=True)
    delta = jnp.sum(delta, axis=1, keepdims=True)
    write_message(message_ref, project(halves), gamma, delta)


def coarse_table(gathered_ref, full):
    devices = gathered_ref.shape[0]
    for slot in range(4):
        full[slot * devices : (slot + 1) * devices] = gathered_ref[:, 0, slot * LANES : (slot + 1) * LANES]


def scalars(mode, gathered_ref, state_in, state_ref, realiz):
    total = jnp.sum(gathered_ref[:, 0, 4 * LANES : 5 * LANES], axis=0, keepdims=True)
    lane = lax.broadcasted_iota(jnp.int32, (1, LANES), 1)
    swapped = pltpu.roll(total, LANES // 2, 1)
    gamma = jnp.where(lane < realiz, total, swapped)
    delta = jnp.where(lane < realiz, swapped, total)
    if mode == "init":
        alpha, beta = gamma / delta, jnp.zeros_like(gamma)
    else:
        beta = gamma / state_in[0:1]
        alpha = gamma / (delta - beta * gamma / state_in[1:2])
    if state_ref is not None:
        state_ref[0:1] = gamma
        state_ref[1:2] = alpha
    return alpha, beta


def turn(rows, realiz):
    count = sum(row.shape[0] for row in rows)
    return jnp.concatenate([*rows, jnp.zeros((LANES - count, LANES), F32)], axis=0).T[:realiz]


def in_slots(refs):
    return [refs[ORDER.index(slot)] for slot in range(4)]


def new_residual(place, slot, mode, columns, image_ref, got_ref, old, at, start):
    got = got_ref[: image_ref.shape[0], pl.ds(start, CHUNK)]
    shared = place.shared[slot]
    applied = image_ref[:, at] + (got if shared is None else jnp.where(shared, got, 0.0))
    if mode == "load":
        return None, applied
    if mode == "next":
        applied = applied + columns[:, 1:2] * old[1][:, at]
    return applied, old[0][:, at] - columns[:, 0:1] * applied


def new_field(mode, columns, precon_ref, old, at):
    direction = precon_ref[:, at]
    if mode == "init":
        return direction, columns[:, 0:1] * direction
    direction = direction + columns[:, 1:2] * old[0][:, at]
    return direction, old[1][:, at] + columns[:, 0:1] * direction


def precondition(place, columns, scaled, inverse_ref, slots, resid_refs, part_at, edge_refs, gamma):
    edge_len = scaled.shape[1] // 4
    for slot in slots:
        flat, ramp_by = (columns[:, 8 + 2 * slot + i : 9 + 2 * slot + i] for i in range(2))
        for start in range(0, edge_len, CHUNK):
            level, ramp = basis_parts(edge_len, start, CHUNK)
            part = product(place, (0, 1, 2, 3), scaled, inverse_ref, slot, start)
            part = place.weight(slot) * (part + (flat * level + ramp_by * ramp))
            part_ref, first = part_at[slot]
            part_ref[:, pl.ds(first + start, CHUNK)] = part
            edge_refs[slot][:, pl.ds(start, CHUNK)] = part.astype(BF16)
            here = lane_parts(resid_refs[slot // 2][:, pl.ds(slot % 2 * edge_len + start, CHUNK)] * part)
            gamma = here if gamma is None else gamma + here
    return gamma


OLD = {"load": 0, "init": 1, "next": 2}


def step_kernel(mode, *refs):
    refs = list(refs)
    take = lambda n: [refs.pop(0) for _ in range(n)]
    place = Place()
    images, edges, (gathered_ref,) = take(2), in_slots(take(4)), take(1)
    olds = [take(OLD[mode]) for _ in range(2)]
    state_in, = take(1) if mode == "next" else (None,)
    coarse_in, = take(1) if mode != "load" else (None,)
    applied_in, = take(1) if mode == "next" else (None,)
    level_mat_ref, ramp_mat_ref, inverse_ref = take(3)
    news = [take(1 if mode == "load" else 2) for _ in range(2)]
    columns_ref, coarse_ref = take(2)
    state_ref, applied_ref = take(2) if mode != "load" else (None, None)
    scaled, part_ref, edge_ref, gamma_ref = take(4)
    realiz, edge_len = images[0].shape[0], edges[0].shape[1]
    if mode == "load":
        coarse_table(gathered_ref, coarse_ref)
        coarse = coarse_ref[...]
        rows, columns = [jnp.zeros((8, LANES), F32)], None
    else:
        alpha, beta = scalars(mode, gathered_ref, state_in, state_ref, realiz)
        columns = turn([alpha, beta], realiz)
        coarse_table(gathered_ref, applied_ref)
        if mode == "next":
            applied_ref[...] = applied_ref[...] + beta * applied_in[...]
        coarse = coarse_in[...] - alpha * applied_ref[...]
        coarse_ref[...] = coarse
        rows = [alpha, beta, jnp.zeros((6, LANES), F32)]
    for slot in range(4):
        half = slot // 2
        for start in range(0, edge_len, CHUNK):
            at = pl.ds(slot % 2 * edge_len + start, CHUNK)
            applied, resid = new_residual(place, slot, mode, columns, images[half], edges[slot], olds[half], at, start)
            news[half][0][:, at] = resid
            if applied is not None:
                news[half][1][:, at] = applied
            scaled[:, pl.ds(slot * edge_len + start, CHUNK)] = (place.weight(slot) * resid).astype(BF16)
    level = jnp.dot(level_mat_ref[...], coarse, precision=HP, preferred_element_type=F32)
    ramp = jnp.dot(ramp_mat_ref[...], coarse, precision=HP, preferred_element_type=F32)
    rows.append(level + pltpu.roll(ramp, LANES // 2, 1))
    columns = turn(rows, realiz)
    columns_ref[...] = columns
    resids = [new[0] for new in news]
    gamma_ref[...] = precondition(place, columns, scaled, inverse_ref, (2,), resids, {2: (part_ref, 0)}, {2: edge_ref}, None)


def rest_kernel(columns_ref, scaled, near_ref, far_ref, gamma_in, inverse_ref, part_near_ref, part_ref, gamma_ref, e0, e1, e3):
    edge_len = scaled.shape[1] // 4
    part_at = {0: (part_near_ref, 0), 1: (part_near_ref, edge_len), 3: (part_ref, 0)}
    gamma_ref[...] = precondition(
        Place(), columns_ref[...], scaled, inverse_ref, (0, 3, 1), (near_ref, far_ref), part_at, {0: e0, 1: e1, 3: e3}, gamma_in[...]
    )


def field_kernel(mode, columns_ref, *refs):
    old = 0 if mode == "init" else 2
    columns = columns_ref[...]
    for half in range(2):
        precon_ref, *olds = refs[half * (1 + old) : (half + 1) * (1 + old)]
        direction_ref, field_ref = refs[2 * (1 + old) + 2 * half : 2 * (1 + old) + 2 * half + 2]
        for start in range(0, precon_ref.shape[1], CHUNK):
            at = pl.ds(start, CHUNK)
            direction_ref[:, at], field_ref[:, at] = new_field(mode, columns, precon_ref, olds, at)


def last_kernel(*refs):
    refs = list(refs)
    take = lambda n: [refs.pop(0) for _ in range(n)]
    place = Place()
    images, edges, (gathered_ref,) = take(2), in_slots(take(4)), take(1)
    olds, (state_in,), tracks = [take(2) for _ in range(2)], take(1), [take(3) for _ in range(2)]
    field_ref, resid_ref = refs
    realiz, edge_len = images[0].shape[0], edges[0].shape[1]
    columns = turn(scalars("next", gathered_ref, state_in, None, realiz), realiz)
    for slot in range(4):
        half = slot // 2
        for start in range(0, edge_len, CHUNK):
            at = pl.ds(slot % 2 * edge_len + start, CHUNK)
            to = pl.ds(pl.multiple_of(place.edges[slot] * edge_len + start, CHUNK), CHUNK)
            _, resid_ref[:, to] = new_residual(place, slot, "next", columns, images[half], edges[slot], olds[half], at, start)
            _, field_ref[:, to] = new_field("next", columns, tracks[half][0], tracks[half][1:], at)


def gather(message):
    return lax.all_to_all(message, AXES, split_axis=0, concat_axis=0, tiled=True)


def body(obs_values, obs_dest, obs_node, schur, local_inverse, coarse_inverse):
    size = schur.shape[-1]
    obs_count, realiz = obs_values.shape
    cols, rows = lax.axis_size("sx"), lax.axis_size("sy")
    devices = cols * rows
    capacity = max(2, 2 * obs_count // devices)
    edge, quarter = shape(realiz, size // 4, BF16), shape(realiz, size // 4)
    exact = [shape(realiz + PAD, size // 4)] * 4
    half, whole = shape(realiz, size // 2), shape(realiz, size)
    message = jax.ShapeDtypeStruct((devices, 1, 5 * LANES), F32)
    narrow, state_shape = shape(realiz, LANES), shape(8, LANES)
    coarse_state = shape(4 * devices, LANES)
    scratch_half, scratch_quarter = pltpu.VMEM((realiz, size // 2), BF16), pltpu.VMEM((realiz, size // 4), BF16)
    flops = 2 * realiz * size * size
    schur_mat, inverse_mat = schur[0, 0], local_inverse[0, 0]

    packed, *coarse_mats = call(
        functools.partial(first_kernel, capacity, cols, rows),
        [shape(devices * capacity, LANES, BF16), *[shape(8, 4 * devices)] * 2],
        (obs_values.T, obs_dest.reshape(1, obs_count), obs_node.reshape(1, obs_count), coarse_inverse),
        [
            pltpu.VMEM((realiz, obs_count), BF16),
            *[pltpu.VMEM((1, obs_count), jnp.int32)] * 2,
            pltpu.VMEM(coarse_inverse.shape, F32),
            pltpu.SemaphoreType.DMA((4,)),
        ],
        COVER,
        pl.BlockSpec(memory_space=pltpu.HBM),
    )
    got = lax.all_to_all(packed.reshape(devices, capacity, LANES), AXES, split_axis=0, concat_axis=0, tiled=True)
    *image, e0, e1, e2, e3, sent = call(
        functools.partial(load_kernel, realiz),
        [half, half, *exact, message],
        (got.reshape(devices * capacity, LANES),),
        flops=COVER,
    )
    mode, olds, states = "load", ([], []), []
    for step in range(ITERS + 1):
        g, gathered = exchange((e0, e1, e2, e3)), gather(sent)
        ins = [*image, *[g[slot] for slot in ORDER], gathered, *olds[0], *olds[1]]
        if step == ITERS:
            field, resid = call(last_kernel, [whole, whole], [*ins, states[0], z[0], *track[0], z[1], *track[1]])
            return field[None, None], resid[None, None]
        count, state_count = (1, 1) if mode == "load" else (2, 3)
        outs = call(
            functools.partial(step_kernel, mode),
            [*[half] * (2 * count), narrow, *[coarse_state, state_shape, coarse_state][:state_count], shape(realiz, size, BF16), quarter, edge, narrow],
            [*ins, *states, *coarse_mats, inverse_mat],
            flops=flops // 4,
        )
        olds, (columns, coarse), outs = (outs[:count], outs[count : 2 * count]), outs[2 * count : 2 * count + 2], outs[2 * count + 2 :]
        states, outs = [*outs[:1], coarse, *outs[1:2]] if mode != "load" else [coarse], outs[state_count - 1 :]
        scaled, part_first, e2, gamma = outs
        part_near, part_last, gamma, e0, e1, e3 = call(
            rest_kernel,
            [half, quarter, narrow, edge, edge, edge],
            (columns, scaled, olds[0][0], olds[1][0], gamma, inverse_mat),
            flops=flops * 3 // 4,
        )
        g = exchange((e0, e1, e2, e3))
        if step == 0:
            track = (), ()
        else:
            outs = call(
                functools.partial(field_kernel, mode), [half] * 4, (columns, z[0], *track[0], z[1], *track[1]), flops=1
            )
            track = outs[:2], outs[2:]
        z_first, partial = call(
            image_first_kernel, [quarter, whole], (part_first, g[2], schur_mat), [scratch_quarter], flops // 4
        )
        z_near, partial = call(
            image_near_kernel, [half, whole], (part_near, g[0], g[1], partial, schur_mat), [scratch_half], flops // 2
        )
        z_far, *image, e0, e1, e2, e3, sent = call(
            image_last_kernel,
            [half, half, half, *exact, message],
            (part_last, g[3], z_first, z_near, partial, gamma, schur_mat, *track[0][:1]),
            [scratch_quarter],
            flops // 4,
        )
        z = z_near, z_far
        mode = "init" if step == 0 else "next"


def solution(mesh):
    placed = (
        P(AXES, None),
        P(AXES, None),
        P(AXES),
        P("sx", "sy", None, None),
        P("sx", "sy", None, None),
        P(AXES, None),
    )
    return jax.shard_map(
        body,
        mesh=mesh,
        in_specs=placed,
        out_specs=(P("sx", "sy", None, None), P("sx", "sy", None, None)),
        check_vma=False,
    )
```

```python
import functools

import jax
import jax.numpy as jnp
from jax import lax
from jax.experimental import pallas as pl
from jax.experimental.pallas import tpu as pltpu
from jax.sharding import PartitionSpec as P

ITERS = 6
ORDER = (1, 0, 2, 3)
PAD = 16
COVER = 8e9
LANES = 128
CHUNK = 256
HP = lax.Precision.HIGHEST
F32 = jnp.float32
BF16 = jnp.bfloat16
VM = pl.BlockSpec(memory_space=pltpu.VMEM)
AXES = ("sx", "sy")


def call(kernel, outs, args, scratch=(), flops=0, spec=VM):
    size = sum(a.size * a.dtype.itemsize for a in args)
    return pl.pallas_call(
        kernel,
        out_shape=outs,
        in_specs=[spec] * len(args),
        out_specs=jax.tree.map(lambda _: VM, outs),
        scratch_shapes=list(scratch),
        compiler_params=pltpu.CompilerParams(vmem_limit_bytes=(8 if spec is VM else 56) << 20),
        cost_estimate=pl.CostEstimate(flops=int(flops), bytes_accessed=size, transcendentals=0),
    )(*args)


def shape(rows, columns, dtype=F32):
    return jax.ShapeDtypeStruct((rows, columns), dtype)


def edge_of(slot, odd_col, odd_row):
    return (1 - odd_col, 3 - odd_row, odd_col, 2 + odd_row)[slot]


class Place:
    def __init__(self):
        col, row = lax.axis_index("sx"), lax.axis_index("sy")
        cols, rows = lax.axis_size("sx"), lax.axis_size("sy")
        odd_col, odd_row = lax.rem(col, 2), lax.rem(row, 2)
        self.edges = [edge_of(slot, odd_col, odd_row) for slot in range(4)]
        far_col = jnp.where(odd_col == 1, col < cols - 1, col > 0)
        far_row = jnp.where(odd_row == 1, row < rows - 1, row > 0)
        self.shared = (None, None, far_col, far_row)

    def weight(self, slot):
        shared = self.shared[slot]
        return F32(0.5) if shared is None else jnp.where(shared, F32(0.5), F32(1.0))


def swaps():
    cols, rows = lax.axis_size("sx"), lax.axis_size("sy")
    plans = [], [], [], []
    for col in range(cols):
        for row in range(rows):
            across = col + (1 if col % 2 else -1)
            beyond = row + (1 if row % 2 else -1)
            far_sx = (across, row) if 0 <= across < cols else (col, row ^ 1)
            partners = (col ^ 1, row), (col, row ^ 1), far_sx, (col, beyond % rows)
            for plan, (to_col, to_row) in zip(plans, partners, strict=True):
                plan.append((col * rows + row, to_col * rows + to_row))
    return plans


def exchange(edges):
    plans = swaps()
    got = [None] * 4
    for slot in (2, 0, 3, 1):
        got[slot] = lax.ppermute(edges[slot], AXES, plans[slot])
    return got


def basis_parts(edge_len, start, width):
    node = lax.broadcasted_iota(jnp.int32, (1, width), 1) + start
    offset = node.astype(F32) - (edge_len - 1) / 2.0
    level = 1.0 / jnp.sqrt(F32(edge_len))
    norm = jnp.sqrt(F32(edge_len * (edge_len * edge_len - 1) / 12.0))
    return level, offset / norm


def lane_parts(value):
    return sum(value[:, i : i + LANES] for i in range(LANES, value.shape[1], LANES)) + value[:, :LANES]


def project(halves):
    edge_len = halves[0].shape[1] // 2
    columns = []
    for slot in range(4):
        flat = ramped = None
        for start in range(0, edge_len, CHUNK):
            at = slot % 2 * edge_len + start
            part = halves[slot // 2][:, at : at + CHUNK]
            ramp = basis_parts(edge_len, start, CHUNK)[1]
            one, two = lane_parts(part), lane_parts(part * ramp)
            flat = one if flat is None else flat + one
            ramped = two if ramped is None else ramped + two
        level = basis_parts(edge_len, 0, LANES)[0]
        columns.append(jnp.sum(flat, axis=1, keepdims=True) * level)
        columns.append(jnp.sum(ramped, axis=1, keepdims=True))
    return columns


def write_message(message_ref, columns, gamma, delta):
    rows = gamma.shape[0]
    lane = lax.broadcasted_iota(jnp.int32, (rows, LANES), 1)
    table = jnp.zeros((rows, LANES), F32)
    order = [*columns[0::2], gamma, *columns[1::2], delta]
    for i, column in enumerate(order):
        table = jnp.where(lane == (i if i < 5 else i + 3), column, table)
    turned = table.T
    block = jnp.concatenate([turned[0:8], turned[8:16]], axis=1)
    for i in range(5):
        row = jnp.broadcast_to(block[i : i + 1][None], (message_ref.shape[0], 1, LANES))
        message_ref[:, :, i * LANES : (i + 1) * LANES] = row


def first_kernel(capacity, cols, rows, values_in, dest_in, node_in, inverse_in, out_ref, level_mat_ref, ramp_mat_ref,
                 values_ref, dest_ref, node_ref, inverse_ref, sems):
    pairs = ((values_in, values_ref), (dest_in, dest_ref), (node_in, node_ref), (inverse_in, inverse_ref))
    copies = [pltpu.make_async_copy(source, to, sems.at[i]) for i, (source, to) in enumerate(pairs)]
    for copy in copies:
        copy.start()
    for copy in copies:
        copy.wait()
    pack(capacity, values_ref, dest_ref, node_ref, out_ref)
    coarse_matrices(cols, rows, inverse_ref, (level_mat_ref, ramp_mat_ref))


def pack(capacity, values_ref, dest_ref, node_ref, out_ref):
    realiz, count = values_ref.shape
    slots = out_ref.shape[0]
    dest, node = dest_ref[...], node_ref[...]
    hit = lax.broadcasted_iota(jnp.int32, (slots // capacity, count), 0) == dest
    before = lax.broadcasted_iota(jnp.int32, (count, count), 0) < lax.broadcasted_iota(jnp.int32, (count, count), 1)
    hit = hit.astype(F32)
    earlier = jnp.dot(hit.astype(BF16), before.astype(F32).astype(BF16), preferred_element_type=F32)
    rank = jnp.sum(hit * earlier, axis=0, keepdims=True).astype(jnp.int32)
    slot = dest * capacity + rank
    high, low = (node // 64).astype(F32), lax.rem(node, 64).astype(F32)
    side = lax.broadcasted_iota(jnp.int32, (LANES - realiz, count), 0)
    codes = jnp.where(side == 0, high, jnp.where(side == 1, low, 0.0)).astype(BF16)
    full = jnp.concatenate([values_ref[...], codes], axis=0)
    choose = (lax.broadcasted_iota(jnp.int32, (slots, count), 0) == slot).astype(F32).astype(BF16)
    out = lax.dot_general(choose, full, (((1,), (1,)), ((), ())), preferred_element_type=F32)
    out_ref[...] = out.astype(BF16)


def coarse_matrices(cols, rows, inverse_ref, out_refs):
    devices = cols * rows
    i = lax.broadcasted_iota(jnp.int32, (8 * devices, 4 * devices), 0)
    j = lax.broadcasted_iota(jnp.int32, (8 * devices, 4 * devices), 1)
    slot, device = j // devices, j % devices
    col, row = device // rows, device % rows
    along_x = (slot == 0) | (slot == 2)
    near = slot < 2
    step_col = jnp.where(near, 1, -1) * (1 - 2 * (col % 2))
    step_row = jnp.where(near, 1, -1) * (1 - 2 * (row % 2))
    to_col = jnp.where(along_x, col + step_col, col)
    to_row = jnp.where(along_x, row, row + step_row)
    shared = (to_col >= 0) & (to_col < cols) & (to_row >= 0) & (to_row < rows)

    def index(col, row):
        odd_col, odd_row = col % 2, row % 2
        edge = jnp.where(slot == 0, 1 - odd_col, jnp.where(slot == 1, 3 - odd_row, jnp.where(slot == 2, odd_col, 2 + odd_row)))
        return (col * rows + row) * 8 + edge * 2

    own, other = index(col, row), index(to_col, to_row)
    place = Place()
    k = lax.broadcasted_iota(jnp.int32, (8, 8), 0)
    from_row = lax.broadcasted_iota(jnp.int32, (8, 8), 1)
    edge = place.edges[3]
    for s in range(3):
        edge = jnp.where(k // 2 == s, place.edges[s], edge)
    pick = (from_row == 2 * edge + k % 2).astype(F32)
    mine = jnp.dot(pick, inverse_ref[...], precision=HP, preferred_element_type=F32)
    for part, out_ref in enumerate(out_refs):
        table = jnp.where(shared & (i == other + part), 0.5, jnp.where(i == own + part, jnp.where(shared, 0.5, 1.0), 0.0))
        out_ref[...] = jnp.dot(mine, table, precision=HP, preferred_element_type=F32)


def load_kernel(realiz, got_ref, near_ref, far_ref, e0, e1, e2, e3, message_ref):
    place, slots, edge_len = Place(), got_ref.shape[0], e0.shape[1]
    got = got_ref[...]
    node = got[:, realiz : realiz + 1].astype(F32) * 64.0 + got[:, realiz + 1 : realiz + 2].astype(F32)
    node = node.astype(jnp.int32)
    halves = near_ref, far_ref
    for slot, edge_ref in enumerate((e0, e1, e2, e3)):
        for start in range(0, edge_len, CHUNK):
            first = place.edges[slot] * edge_len + start
            here = lax.broadcasted_iota(jnp.int32, (slots, CHUNK), 1) + first == node
            load = lax.dot_general(got, here.astype(F32).astype(BF16), (((0,), (0,)), ((), ())), preferred_element_type=F32)
            at = slot % 2 * edge_len + start
            halves[slot // 2][:, at : at + CHUNK] = load[:realiz]
            edge_ref[:realiz, start : start + CHUNK] = load[:realiz]
    zero = jnp.zeros((realiz, 1), F32)
    write_message(message_ref, project(halves), zero, zero)


def product(place, slots, vec_ref, matrix_ref, slot, start):
    edge_len = vec_ref.shape[1] // len(slots)
    column = pl.multiple_of(place.edges[slot] * edge_len + start, CHUNK)
    total = None
    for i, source in enumerate(slots):
        row = pl.multiple_of(place.edges[source] * edge_len, edge_len)
        block = matrix_ref[pl.ds(row, edge_len), pl.ds(column, CHUNK)]
        part = jnp.dot(vec_ref[:, i * edge_len : (i + 1) * edge_len], block, preferred_element_type=F32)
        total = part if total is None else total + part
    return total


def image_far_kernel(part_ref, g3, g2, schur_ref, precon_ref, sum_ref, rounded):
    place, edge_len = Place(), g2.shape[1]
    for i, got in enumerate((g2, g3)):
        at = pl.ds(i * edge_len, edge_len)
        value = part_ref[:, at] + jnp.where(place.shared[2 + i], got[...].astype(F32), 0.0)
        precon_ref[:, at] = value
        rounded[:, at] = value.astype(BF16)
    for slot in range(4):
        for start in range(0, edge_len, CHUNK):
            sum_ref[:, pl.ds(slot * edge_len + start, CHUNK)] = product(place, (2, 3), rounded, schur_ref, slot, start)


def image_near_kernel(part_ref, g0, g1, far_ref, sum_ref, gamma_ref, schur_ref, *refs):
    precon_ref, image_near_ref, image_far_ref, e0, e1, e2, e3, message_ref, rounded = refs[-9:]
    place, edge_len = Place(), g0.shape[1]
    for i, got in enumerate((g0, g1)):
        at = pl.ds(i * edge_len, edge_len)
        value = part_ref[:, at] + got[...].astype(F32)
        precon_ref[:, at] = value
        rounded[:, at] = value.astype(BF16)
    halves, vectors = (image_near_ref, image_far_ref), (precon_ref, far_ref)
    delta = None
    for slot, edge_ref in enumerate((e0, e1, e2, e3)):
        for start in range(0, edge_len, CHUNK):
            image = sum_ref[:, pl.ds(slot * edge_len + start, CHUNK)] + product(place, (0, 1), rounded, schur_ref, slot, start)
            at = pl.ds(slot % 2 * edge_len + start, CHUNK)
            halves[slot // 2][:, at] = image
            edge_ref[: image.shape[0], pl.ds(start, CHUNK)] = image
            here = lane_parts(vectors[slot // 2][:, at] * image)
            delta = here if delta is None else delta + here
    gamma = jnp.sum(gamma_ref[...], axis=1, keepdims=True)
    delta = jnp.sum(delta, axis=1, keepdims=True)
    write_message(message_ref, project(halves), gamma, delta)


def coarse_table(gathered_ref, full):
    devices = gathered_ref.shape[0]
    for slot in range(4):
        full[slot * devices : (slot + 1) * devices] = gathered_ref[:, 0, slot * LANES : (slot + 1) * LANES]


def scalars(mode, gathered_ref, state_in, state_ref, realiz):
    total = jnp.sum(gathered_ref[:, 0, 4 * LANES : 5 * LANES], axis=0, keepdims=True)
    lane = lax.broadcasted_iota(jnp.int32, (1, LANES), 1)
    swapped = pltpu.roll(total, LANES // 2, 1)
    gamma = jnp.where(lane < realiz, total, swapped)
    delta = jnp.where(lane < realiz, swapped, total)
    if mode == "init":
        alpha, beta = gamma / delta, jnp.zeros_like(gamma)
    else:
        beta = gamma / state_in[0:1]
        alpha = gamma / (delta - beta * gamma / state_in[1:2])
    if state_ref is not None:
        state_ref[0:1] = gamma
        state_ref[1:2] = alpha
    return alpha, beta


def turn(rows, realiz):
    count = sum(row.shape[0] for row in rows)
    return jnp.concatenate([*rows, jnp.zeros((LANES - count, LANES), F32)], axis=0).T[:realiz]


def in_slots(refs):
    return [refs[ORDER.index(slot)] for slot in range(4)]


def new_residual(place, slot, mode, columns, image_ref, got_ref, old, at, start):
    got = got_ref[: image_ref.shape[0], pl.ds(start, CHUNK)]
    shared = place.shared[slot]
    applied = image_ref[:, at] + (got if shared is None else jnp.where(shared, got, 0.0))
    if mode == "load":
        return None, applied
    if mode == "next":
        applied = applied + columns[:, 1:2] * old[1][:, at]
    return applied, old[0][:, at] - columns[:, 0:1] * applied


def new_field(mode, columns, precon_ref, old, at):
    direction = precon_ref[:, at]
    if mode == "init":
        return direction, columns[:, 0:1] * direction
    direction = direction + columns[:, 1:2] * old[0][:, at]
    return direction, old[1][:, at] + columns[:, 0:1] * direction


def precondition(place, columns, scaled, inverse_ref, part_at, resid_refs, edge_refs, gamma):
    edge_len = scaled.shape[1] // 4
    for slot in part_at:
        flat, ramp_by = (columns[:, 8 + 2 * slot + i : 9 + 2 * slot + i] for i in range(2))
        for start in range(0, edge_len, CHUNK):
            level, ramp = basis_parts(edge_len, start, CHUNK)
            part = product(place, (0, 1, 2, 3), scaled, inverse_ref, slot, start)
            part = place.weight(slot) * (part + (flat * level + ramp_by * ramp))
            part_ref, first = part_at[slot]
            part_ref[:, pl.ds(first + start, CHUNK)] = part
            edge_refs[slot][:, pl.ds(start, CHUNK)] = part.astype(BF16)
            here = lane_parts(resid_refs[slot // 2][:, pl.ds(slot % 2 * edge_len + start, CHUNK)] * part)
            gamma = here if gamma is None else gamma + here
    return gamma


OLD = {"load": 0, "init": 1, "next": 2}


def step_kernel(mode, *refs):
    refs = list(refs)
    take = lambda n: [refs.pop(0) for _ in range(n)]
    place = Place()
    images, edges, (gathered_ref,) = take(2), in_slots(take(4)), take(1)
    olds = [take(OLD[mode]) for _ in range(2)]
    state_in, = take(1) if mode == "next" else (None,)
    coarse_in, = take(1) if mode != "load" else (None,)
    applied_in, = take(1) if mode == "next" else (None,)
    level_mat_ref, ramp_mat_ref, inverse_ref = take(3)
    news = [take(1 if mode == "load" else 2) for _ in range(2)]
    columns_ref, coarse_ref = take(2)
    state_ref, applied_ref = take(2) if mode != "load" else (None, None)
    scaled, part_ref, e2, e3, gamma_ref = take(5)
    realiz, edge_len = images[0].shape[0], edges[0].shape[1]
    if mode == "load":
        coarse_table(gathered_ref, coarse_ref)
        coarse = coarse_ref[...]
        rows, columns = [jnp.zeros((8, LANES), F32)], None
    else:
        alpha, beta = scalars(mode, gathered_ref, state_in, state_ref, realiz)
        columns = turn([alpha, beta], realiz)
        coarse_table(gathered_ref, applied_ref)
        if mode == "next":
            applied_ref[...] = applied_ref[...] + beta * applied_in[...]
        coarse = coarse_in[...] - alpha * applied_ref[...]
        coarse_ref[...] = coarse
        rows = [alpha, beta, jnp.zeros((6, LANES), F32)]
    for slot in range(4):
        half = slot // 2
        for start in range(0, edge_len, CHUNK):
            at = pl.ds(slot % 2 * edge_len + start, CHUNK)
            applied, resid = new_residual(place, slot, mode, columns, images[half], edges[slot], olds[half], at, start)
            news[half][0][:, at] = resid
            if applied is not None:
                news[half][1][:, at] = applied
            scaled[:, pl.ds(slot * edge_len + start, CHUNK)] = (place.weight(slot) * resid).astype(BF16)
    level = jnp.dot(level_mat_ref[...], coarse, precision=HP, preferred_element_type=F32)
    ramp = jnp.dot(ramp_mat_ref[...], coarse, precision=HP, preferred_element_type=F32)
    rows.append(level + pltpu.roll(ramp, LANES // 2, 1))
    columns = turn(rows, realiz)
    columns_ref[...] = columns
    resids = [new[0] for new in news]
    part_at = {2: (part_ref, 0), 3: (part_ref, edge_len)}
    gamma_ref[...] = precondition(place, columns, scaled, inverse_ref, part_at, resids, {2: e2, 3: e3}, None)


def rest_kernel(columns_ref, scaled, near_ref, far_ref, gamma_in, inverse_ref, part_ref, e0, e1, gamma_ref):
    part_at = {0: (part_ref, 0), 1: (part_ref, scaled.shape[1] // 4)}
    gamma_ref[...] = precondition(
        Place(), columns_ref[...], scaled, inverse_ref, part_at, (near_ref, far_ref), {0: e0, 1: e1}, gamma_in[...]
    )


def field_kernel(mode, columns_ref, *refs):
    old = 0 if mode == "init" else 2
    columns = columns_ref[...]
    for half in range(2):
        precon_ref, *olds = refs[half * (1 + old) : (half + 1) * (1 + old)]
        direction_ref, field_ref = refs[2 * (1 + old) + 2 * half : 2 * (1 + old) + 2 * half + 2]
        for start in range(0, precon_ref.shape[1], CHUNK):
            at = pl.ds(start, CHUNK)
            direction_ref[:, at], field_ref[:, at] = new_field(mode, columns, precon_ref, olds, at)


def last_kernel(*refs):
    refs = list(refs)
    take = lambda n: [refs.pop(0) for _ in range(n)]
    place = Place()
    images, edges, (gathered_ref,) = take(2), in_slots(take(4)), take(1)
    olds, (state_in,), tracks = [take(2) for _ in range(2)], take(1), [take(3) for _ in range(2)]
    field_ref, resid_ref = refs
    realiz, edge_len = images[0].shape[0], edges[0].shape[1]
    columns = turn(scalars("next", gathered_ref, state_in, None, realiz), realiz)
    for slot in range(4):
        half = slot // 2
        for start in range(0, edge_len, CHUNK):
            at = pl.ds(slot % 2 * edge_len + start, CHUNK)
            to = pl.ds(pl.multiple_of(place.edges[slot] * edge_len + start, CHUNK), CHUNK)
            _, resid_ref[:, to] = new_residual(place, slot, "next", columns, images[half], edges[slot], olds[half], at, start)
            _, field_ref[:, to] = new_field("next", columns, tracks[half][0], tracks[half][1:], at)


def gather(message):
    return lax.all_to_all(message, AXES, split_axis=0, concat_axis=0, tiled=True)


def body(obs_values, obs_dest, obs_node, schur, local_inverse, coarse_inverse):
    size = schur.shape[-1]
    obs_count, realiz = obs_values.shape
    cols, rows = lax.axis_size("sx"), lax.axis_size("sy")
    devices = cols * rows
    capacity = max(2, 2 * obs_count // devices)
    edge = shape(realiz, size // 4, BF16)
    exact = [shape(realiz + PAD, size // 4)] * 4
    half, whole = shape(realiz, size // 2), shape(realiz, size)
    message = jax.ShapeDtypeStruct((devices, 1, 5 * LANES), F32)
    narrow, state_shape = shape(realiz, LANES), shape(8, LANES)
    coarse_state = shape(4 * devices, LANES)
    scratch_half = pltpu.VMEM((realiz, size // 2), BF16)
    flops = 2 * realiz * size * size
    schur_mat, inverse_mat = schur[0, 0], local_inverse[0, 0]

    packed, *coarse_mats = call(
        functools.partial(first_kernel, capacity, cols, rows),
        [shape(devices * capacity, LANES, BF16), *[shape(8, 4 * devices)] * 2],
        (obs_values.T, obs_dest.reshape(1, obs_count), obs_node.reshape(1, obs_count), coarse_inverse),
        [
            pltpu.VMEM((realiz, obs_count), BF16),
            *[pltpu.VMEM((1, obs_count), jnp.int32)] * 2,
            pltpu.VMEM(coarse_inverse.shape, F32),
            pltpu.SemaphoreType.DMA((4,)),
        ],
        COVER,
        pl.BlockSpec(memory_space=pltpu.HBM),
    )
    got = lax.all_to_all(packed.reshape(devices, capacity, LANES), AXES, split_axis=0, concat_axis=0, tiled=True)
    *image, e0, e1, e2, e3, sent = call(
        functools.partial(load_kernel, realiz),
        [half, half, *exact, message],
        (got.reshape(devices * capacity, LANES),),
        flops=COVER,
    )
    mode, olds, states = "load", ([], []), []
    for step in range(ITERS + 1):
        g, gathered = exchange((e0, e1, e2, e3)), gather(sent)
        ins = [*image, *[g[slot] for slot in ORDER], gathered, *olds[0], *olds[1]]
        if step == ITERS:
            field, resid = call(last_kernel, [whole, whole], [*ins, states[0], z[0], *track[0], z[1], *track[1]])
            return field[None, None], resid[None, None]
        count, state_count = (1, 1) if mode == "load" else (2, 3)
        outs = call(
            functools.partial(step_kernel, mode),
            [*[half] * (2 * count), narrow, *[coarse_state, state_shape, coarse_state][:state_count], shape(realiz, size, BF16), half, edge, edge, narrow],
            [*ins, *states, *coarse_mats, inverse_mat],
            flops=flops // 2,
        )
        olds, (columns, coarse), outs = (outs[:count], outs[count : 2 * count]), outs[2 * count : 2 * count + 2], outs[2 * count + 2 :]
        states, outs = [*outs[:1], coarse, *outs[1:2]] if mode != "load" else [coarse], outs[state_count - 1 :]
        scaled, part_far, e2, e3, gamma = outs
        part_near, e0, e1, gamma = call(
            rest_kernel,
            [half, edge, edge, narrow],
            (columns, scaled, olds[0][0], olds[1][0], gamma, inverse_mat),
            flops=flops // 2,
        )
        g = exchange((e0, e1, e2, e3))
        if step == 0:
            track = (), ()
        else:
            outs = call(
                functools.partial(field_kernel, mode), [half] * 4, (columns, z[0], *track[0], z[1], *track[1]), flops=1
            )
            track = outs[:2], outs[2:]
        z_far, partial = call(
            image_far_kernel, [half, whole], (part_far, g[3], g[2], schur_mat), [scratch_half], flops // 2
        )
        z_near, *image, e0, e1, e2, e3, sent = call(
            image_near_kernel,
            [half, half, half, *exact, message],
            (part_near, g[0], g[1], z_far, partial, gamma, schur_mat, *track[0][:1]),
            [scratch_half],
            flops // 2,
        )
        z = z_near, z_far
        mode = "init" if step == 0 else "next"


def solution(mesh):
    placed = (
        P(AXES, None),
        P(AXES, None),
        P(AXES),
        P("sx", "sy", None, None),
        P("sx", "sy", None, None),
        P(AXES, None),
    )
    return jax.shard_map(
        body,
        mesh=mesh,
        in_specs=placed,
        out_specs=(P("sx", "sy", None, None), P("sx", "sy", None, None)),
        check_vma=False,
    )
```

```python
import functools

import jax
import jax.numpy as jnp
from jax import lax
from jax.experimental import pallas as pl
from jax.experimental.pallas import tpu as pltpu
from jax.sharding import PartitionSpec as P

ITERS = 6
ORDER = (1, 0, 2, 3)
PAD = 16
COVER = 8e9
LANES = 128
CHUNK = 512
HP = lax.Precision.HIGHEST
F32 = jnp.float32
BF16 = jnp.bfloat16
VM = pl.BlockSpec(memory_space=pltpu.VMEM)
AXES = ("sx", "sy")


def call(kernel, outs, args, scratch=(), flops=0, spec=VM):
    size = sum(a.size * a.dtype.itemsize for a in args)
    return pl.pallas_call(
        kernel,
        out_shape=outs,
        in_specs=[spec] * len(args),
        out_specs=jax.tree.map(lambda _: VM, outs),
        scratch_shapes=list(scratch),
        compiler_params=pltpu.CompilerParams(vmem_limit_bytes=(8 if spec is VM else 56) << 20),
        cost_estimate=pl.CostEstimate(flops=int(flops), bytes_accessed=size, transcendentals=0),
    )(*args)


def shape(rows, columns, dtype=F32):
    return jax.ShapeDtypeStruct((rows, columns), dtype)


def edge_of(slot, odd_col, odd_row):
    return (1 - odd_col, 3 - odd_row, odd_col, 2 + odd_row)[slot]


class Place:
    def __init__(self):
        col, row = lax.axis_index("sx"), lax.axis_index("sy")
        cols, rows = lax.axis_size("sx"), lax.axis_size("sy")
        odd_col, odd_row = lax.rem(col, 2), lax.rem(row, 2)
        self.edges = [edge_of(slot, odd_col, odd_row) for slot in range(4)]
        far_col = jnp.where(odd_col == 1, col < cols - 1, col > 0)
        far_row = jnp.where(odd_row == 1, row < rows - 1, row > 0)
        self.shared = (None, None, far_col, far_row)

    def weight(self, slot):
        shared = self.shared[slot]
        return F32(0.5) if shared is None else jnp.where(shared, F32(0.5), F32(1.0))


def swaps():
    cols, rows = lax.axis_size("sx"), lax.axis_size("sy")
    plans = [], [], [], []
    for col in range(cols):
        for row in range(rows):
            across = col + (1 if col % 2 else -1)
            beyond = row + (1 if row % 2 else -1)
            far_sx = (across, row) if 0 <= across < cols else (col, row ^ 1)
            partners = (col ^ 1, row), (col, row ^ 1), far_sx, (col, beyond % rows)
            for plan, (to_col, to_row) in zip(plans, partners, strict=True):
                plan.append((col * rows + row, to_col * rows + to_row))
    return plans


def exchange(edges):
    plans = swaps()
    got = [None] * 4
    for slot in (2, 0, 3, 1):
        got[slot] = lax.ppermute(edges[slot], AXES, plans[slot])
    return got


def basis_parts(edge_len, start, width):
    node = lax.broadcasted_iota(jnp.int32, (1, width), 1) + start
    offset = node.astype(F32) - (edge_len - 1) / 2.0
    level = 1.0 / jnp.sqrt(F32(edge_len))
    norm = jnp.sqrt(F32(edge_len * (edge_len * edge_len - 1) / 12.0))
    return level, offset / norm


def lane_parts(value):
    return sum(value[:, i : i + LANES] for i in range(LANES, value.shape[1], LANES)) + value[:, :LANES]


def project(halves):
    edge_len = halves[0].shape[1] // 2
    columns = []
    for slot in range(4):
        flat = ramped = None
        for start in range(0, edge_len, CHUNK):
            at = slot % 2 * edge_len + start
            part = halves[slot // 2][:, at : at + CHUNK]
            ramp = basis_parts(edge_len, start, CHUNK)[1]
            one, two = lane_parts(part), lane_parts(part * ramp)
            flat = one if flat is None else flat + one
            ramped = two if ramped is None else ramped + two
        level = basis_parts(edge_len, 0, LANES)[0]
        columns.append(jnp.sum(flat, axis=1, keepdims=True) * level)
        columns.append(jnp.sum(ramped, axis=1, keepdims=True))
    return columns


def write_message(message_ref, columns, gamma, delta):
    rows = gamma.shape[0]
    lane = lax.broadcasted_iota(jnp.int32, (rows, LANES), 1)
    table = jnp.zeros((rows, LANES), F32)
    order = [*columns[0::2], gamma, *columns[1::2], delta]
    for i, column in enumerate(order):
        table = jnp.where(lane == (i if i < 5 else i + 3), column, table)
    turned = table.T
    block = jnp.concatenate([turned[0:8], turned[8:16]], axis=1)
    for i in range(5):
        row = jnp.broadcast_to(block[i : i + 1][None], (message_ref.shape[0], 1, LANES))
        message_ref[:, :, i * LANES : (i + 1) * LANES] = row


def first_kernel(capacity, cols, rows, values_in, dest_in, node_in, inverse_in, out_ref, level_mat_ref, ramp_mat_ref,
                 values_ref, dest_ref, node_ref, inverse_ref, sems):
    pairs = ((values_in, values_ref), (dest_in, dest_ref), (node_in, node_ref), (inverse_in, inverse_ref))
    copies = [pltpu.make_async_copy(source, to, sems.at[i]) for i, (source, to) in enumerate(pairs)]
    for copy in copies:
        copy.start()
    for copy in copies:
        copy.wait()
    pack(capacity, values_ref, dest_ref, node_ref, out_ref)
    coarse_matrices(cols, rows, inverse_ref, (level_mat_ref, ramp_mat_ref))


def pack(capacity, values_ref, dest_ref, node_ref, out_ref):
    realiz, count = values_ref.shape
    slots = out_ref.shape[0]
    dest, node = dest_ref[...], node_ref[...]
    hit = lax.broadcasted_iota(jnp.int32, (slots // capacity, count), 0) == dest
    before = lax.broadcasted_iota(jnp.int32, (count, count), 0) < lax.broadcasted_iota(jnp.int32, (count, count), 1)
    hit = hit.astype(F32)
    earlier = jnp.dot(hit.astype(BF16), before.astype(F32).astype(BF16), preferred_element_type=F32)
    rank = jnp.sum(hit * earlier, axis=0, keepdims=True).astype(jnp.int32)
    slot = dest * capacity + rank
    high, low = (node // 64).astype(F32), lax.rem(node, 64).astype(F32)
    side = lax.broadcasted_iota(jnp.int32, (LANES - realiz, count), 0)
    codes = jnp.where(side == 0, high, jnp.where(side == 1, low, 0.0)).astype(BF16)
    full = jnp.concatenate([values_ref[...], codes], axis=0)
    choose = (lax.broadcasted_iota(jnp.int32, (slots, count), 0) == slot).astype(F32).astype(BF16)
    out = lax.dot_general(choose, full, (((1,), (1,)), ((), ())), preferred_element_type=F32)
    out_ref[...] = out.astype(BF16)


def coarse_matrices(cols, rows, inverse_ref, out_refs):
    devices = cols * rows
    i = lax.broadcasted_iota(jnp.int32, (8 * devices, 4 * devices), 0)
    j = lax.broadcasted_iota(jnp.int32, (8 * devices, 4 * devices), 1)
    slot, device = j // devices, j % devices
    col, row = device // rows, device % rows
    along_x = (slot == 0) | (slot == 2)
    near = slot < 2
    step_col = jnp.where(near, 1, -1) * (1 - 2 * (col % 2))
    step_row = jnp.where(near, 1, -1) * (1 - 2 * (row % 2))
    to_col = jnp.where(along_x, col + step_col, col)
    to_row = jnp.where(along_x, row, row + step_row)
    shared = (to_col >= 0) & (to_col < cols) & (to_row >= 0) & (to_row < rows)

    def index(col, row):
        odd_col, odd_row = col % 2, row % 2
        edge = jnp.where(slot == 0, 1 - odd_col, jnp.where(slot == 1, 3 - odd_row, jnp.where(slot == 2, odd_col, 2 + odd_row)))
        return (col * rows + row) * 8 + edge * 2

    own, other = index(col, row), index(to_col, to_row)
    place = Place()
    k = lax.broadcasted_iota(jnp.int32, (8, 8), 0)
    from_row = lax.broadcasted_iota(jnp.int32, (8, 8), 1)
    edge = place.edges[3]
    for s in range(3):
        edge = jnp.where(k // 2 == s, place.edges[s], edge)
    pick = (from_row == 2 * edge + k % 2).astype(F32)
    mine = jnp.dot(pick, inverse_ref[...], precision=HP, preferred_element_type=F32)
    for part, out_ref in enumerate(out_refs):
        table = jnp.where(shared & (i == other + part), 0.5, jnp.where(i == own + part, jnp.where(shared, 0.5, 1.0), 0.0))
        out_ref[...] = jnp.dot(mine, table, precision=HP, preferred_element_type=F32)


def load_kernel(realiz, got_ref, near_ref, far_ref, e0, e1, e2, e3, message_ref):
    place, slots, edge_len = Place(), got_ref.shape[0], e0.shape[1]
    got = got_ref[...]
    node = got[:, realiz : realiz + 1].astype(F32) * 64.0 + got[:, realiz + 1 : realiz + 2].astype(F32)
    node = node.astype(jnp.int32)
    halves = near_ref, far_ref
    for slot, edge_ref in enumerate((e0, e1, e2, e3)):
        for start in range(0, edge_len, CHUNK):
            first = place.edges[slot] * edge_len + start
            here = lax.broadcasted_iota(jnp.int32, (slots, CHUNK), 1) + first == node
            load = lax.dot_general(got, here.astype(F32).astype(BF16), (((0,), (0,)), ((), ())), preferred_element_type=F32)
            at = slot % 2 * edge_len + start
            halves[slot // 2][:, at : at + CHUNK] = load[:realiz]
            edge_ref[:realiz, start : start + CHUNK] = load[:realiz]
    zero = jnp.zeros((realiz, 1), F32)
    write_message(message_ref, project(halves), zero, zero)


def product(place, slots, vec_ref, matrix_ref, slot, start):
    edge_len = vec_ref.shape[1] // len(slots)
    column = pl.multiple_of(place.edges[slot] * edge_len + start, CHUNK)
    total = None
    for i, source in enumerate(slots):
        row = pl.multiple_of(place.edges[source] * edge_len, edge_len)
        block = matrix_ref[pl.ds(row, edge_len), pl.ds(column, CHUNK)]
        part = jnp.dot(vec_ref[:, i * edge_len : (i + 1) * edge_len], block, preferred_element_type=F32)
        total = part if total is None else total + part
    return total


def image_far_kernel(part_ref, g3, g2, schur_ref, precon_ref, sum_ref, rounded):
    place, edge_len = Place(), g2.shape[1]
    for i, got in enumerate((g2, g3)):
        at = pl.ds(i * edge_len, edge_len)
        value = part_ref[:, at] + jnp.where(place.shared[2 + i], got[...].astype(F32), 0.0)
        precon_ref[:, at] = value
        rounded[:, at] = value.astype(BF16)
    for slot in range(4):
        for start in range(0, edge_len, CHUNK):
            sum_ref[:, pl.ds(slot * edge_len + start, CHUNK)] = product(place, (2, 3), rounded, schur_ref, slot, start)


def image_near_kernel(part_ref, g0, g1, far_ref, sum_ref, gamma_ref, schur_ref, *refs):
    precon_ref, image_near_ref, image_far_ref, e0, e1, e2, e3, message_ref, rounded = refs[-9:]
    place, edge_len = Place(), g0.shape[1]
    for i, got in enumerate((g0, g1)):
        at = pl.ds(i * edge_len, edge_len)
        value = part_ref[:, at] + got[...].astype(F32)
        precon_ref[:, at] = value
        rounded[:, at] = value.astype(BF16)
    halves, vectors = (image_near_ref, image_far_ref), (precon_ref, far_ref)
    delta = None
    for slot, edge_ref in enumerate((e0, e1, e2, e3)):
        for start in range(0, edge_len, CHUNK):
            image = sum_ref[:, pl.ds(slot * edge_len + start, CHUNK)] + product(place, (0, 1), rounded, schur_ref, slot, start)
            at = pl.ds(slot % 2 * edge_len + start, CHUNK)
            halves[slot // 2][:, at] = image
            edge_ref[: image.shape[0], pl.ds(start, CHUNK)] = image
            here = lane_parts(vectors[slot // 2][:, at] * image)
            delta = here if delta is None else delta + here
    gamma = jnp.sum(gamma_ref[...], axis=1, keepdims=True)
    delta = jnp.sum(delta, axis=1, keepdims=True)
    write_message(message_ref, project(halves), gamma, delta)


def coarse_table(gathered_ref, full):
    devices = gathered_ref.shape[0]
    for slot in range(4):
        full[slot * devices : (slot + 1) * devices] = gathered_ref[:, 0, slot * LANES : (slot + 1) * LANES]


def scalars(mode, gathered_ref, state_in, state_ref, realiz):
    total = jnp.sum(gathered_ref[:, 0, 4 * LANES : 5 * LANES], axis=0, keepdims=True)
    lane = lax.broadcasted_iota(jnp.int32, (1, LANES), 1)
    swapped = pltpu.roll(total, LANES // 2, 1)
    gamma = jnp.where(lane < realiz, total, swapped)
    delta = jnp.where(lane < realiz, swapped, total)
    if mode == "init":
        alpha, beta = gamma / delta, jnp.zeros_like(gamma)
    else:
        beta = gamma / state_in[0:1]
        alpha = gamma / (delta - beta * gamma / state_in[1:2])
    if state_ref is not None:
        state_ref[0:1] = gamma
        state_ref[1:2] = alpha
    return alpha, beta


def turn(rows, realiz):
    count = sum(row.shape[0] for row in rows)
    return jnp.concatenate([*rows, jnp.zeros((LANES - count, LANES), F32)], axis=0).T[:realiz]


def in_slots(refs):
    return [refs[ORDER.index(slot)] for slot in range(4)]


def new_residual(place, slot, mode, columns, image_ref, got_ref, old, at, start):
    got = got_ref[: image_ref.shape[0], pl.ds(start, CHUNK)]
    shared = place.shared[slot]
    applied = image_ref[:, at] + (got if shared is None else jnp.where(shared, got, 0.0))
    if mode == "load":
        return None, applied
    if mode == "next":
        applied = applied + columns[:, 1:2] * old[1][:, at]
    return applied, old[0][:, at] - columns[:, 0:1] * applied


def new_field(mode, columns, precon_ref, old, at):
    direction = precon_ref[:, at]
    if mode == "init":
        return direction, columns[:, 0:1] * direction
    direction = direction + columns[:, 1:2] * old[0][:, at]
    return direction, old[1][:, at] + columns[:, 0:1] * direction


def precondition(place, columns, scaled, inverse_ref, part_at, resid_refs, edge_refs, gamma):
    edge_len = scaled.shape[1] // 4
    for slot in part_at:
        flat, ramp_by = (columns[:, 8 + 2 * slot + i : 9 + 2 * slot + i] for i in range(2))
        for start in range(0, edge_len, CHUNK):
            level, ramp = basis_parts(edge_len, start, CHUNK)
            part = product(place, (0, 1, 2, 3), scaled, inverse_ref, slot, start)
            part = place.weight(slot) * (part + (flat * level + ramp_by * ramp))
            part_ref, first = part_at[slot]
            part_ref[:, pl.ds(first + start, CHUNK)] = part
            edge_refs[slot][:, pl.ds(start, CHUNK)] = part.astype(BF16)
            here = lane_parts(resid_refs[slot // 2][:, pl.ds(slot % 2 * edge_len + start, CHUNK)] * part)
            gamma = here if gamma is None else gamma + here
    return gamma


OLD = {"load": 0, "init": 1, "next": 2}


def step_kernel(mode, *refs):
    refs = list(refs)
    take = lambda n: [refs.pop(0) for _ in range(n)]
    place = Place()
    images, edges, (gathered_ref,) = take(2), in_slots(take(4)), take(1)
    olds = [take(OLD[mode]) for _ in range(2)]
    state_in, = take(1) if mode == "next" else (None,)
    coarse_in, = take(1) if mode != "load" else (None,)
    applied_in, = take(1) if mode == "next" else (None,)
    level_mat_ref, ramp_mat_ref, inverse_ref = take(3)
    news = [take(1 if mode == "load" else 2) for _ in range(2)]
    columns_ref, coarse_ref = take(2)
    state_ref, applied_ref = take(2) if mode != "load" else (None, None)
    scaled, part_ref, e2, e3, gamma_ref = take(5)
    realiz, edge_len = images[0].shape[0], edges[0].shape[1]
    if mode == "load":
        coarse_table(gathered_ref, coarse_ref)
        coarse = coarse_ref[...]
        rows, columns = [jnp.zeros((8, LANES), F32)], None
    else:
        alpha, beta = scalars(mode, gathered_ref, state_in, state_ref, realiz)
        columns = turn([alpha, beta], realiz)
        coarse_table(gathered_ref, applied_ref)
        if mode == "next":
            applied_ref[...] = applied_ref[...] + beta * applied_in[...]
        coarse = coarse_in[...] - alpha * applied_ref[...]
        coarse_ref[...] = coarse
        rows = [alpha, beta, jnp.zeros((6, LANES), F32)]
    for slot in range(4):
        half = slot // 2
        for start in range(0, edge_len, CHUNK):
            at = pl.ds(slot % 2 * edge_len + start, CHUNK)
            applied, resid = new_residual(place, slot, mode, columns, images[half], edges[slot], olds[half], at, start)
            news[half][0][:, at] = resid
            if applied is not None:
                news[half][1][:, at] = applied
            scaled[:, pl.ds(slot * edge_len + start, CHUNK)] = (place.weight(slot) * resid).astype(BF16)
    level = jnp.dot(level_mat_ref[...], coarse, precision=HP, preferred_element_type=F32)
    ramp = jnp.dot(ramp_mat_ref[...], coarse, precision=HP, preferred_element_type=F32)
    rows.append(level + pltpu.roll(ramp, LANES // 2, 1))
    columns = turn(rows, realiz)
    columns_ref[...] = columns
    resids = [new[0] for new in news]
    part_at = {2: (part_ref, 0), 3: (part_ref, edge_len)}
    gamma_ref[...] = precondition(place, columns, scaled, inverse_ref, part_at, resids, {2: e2, 3: e3}, None)


def rest_kernel(columns_ref, scaled, near_ref, far_ref, gamma_in, inverse_ref, part_ref, e0, e1, gamma_ref):
    part_at = {0: (part_ref, 0), 1: (part_ref, scaled.shape[1] // 4)}
    gamma_ref[...] = precondition(
        Place(), columns_ref[...], scaled, inverse_ref, part_at, (near_ref, far_ref), {0: e0, 1: e1}, gamma_in[...]
    )


def field_kernel(mode, columns_ref, *refs):
    old = 0 if mode == "init" else 2
    columns = columns_ref[...]
    for half in range(2):
        precon_ref, *olds = refs[half * (1 + old) : (half + 1) * (1 + old)]
        direction_ref, field_ref = refs[2 * (1 + old) + 2 * half : 2 * (1 + old) + 2 * half + 2]
        for start in range(0, precon_ref.shape[1], CHUNK):
            at = pl.ds(start, CHUNK)
            direction_ref[:, at], field_ref[:, at] = new_field(mode, columns, precon_ref, olds, at)


def last_kernel(*refs):
    refs = list(refs)
    take = lambda n: [refs.pop(0) for _ in range(n)]
    place = Place()
    images, edges, (gathered_ref,) = take(2), in_slots(take(4)), take(1)
    olds, (state_in,), tracks = [take(2) for _ in range(2)], take(1), [take(3) for _ in range(2)]
    field_ref, resid_ref = refs
    realiz, edge_len = images[0].shape[0], edges[0].shape[1]
    columns = turn(scalars("next", gathered_ref, state_in, None, realiz), realiz)
    for slot in range(4):
        half = slot // 2
        for start in range(0, edge_len, CHUNK):
            at = pl.ds(slot % 2 * edge_len + start, CHUNK)
            to = pl.ds(pl.multiple_of(place.edges[slot] * edge_len + start, CHUNK), CHUNK)
            _, resid_ref[:, to] = new_residual(place, slot, "next", columns, images[half], edges[slot], olds[half], at, start)
            _, field_ref[:, to] = new_field("next", columns, tracks[half][0], tracks[half][1:], at)


def gather(message):
    return lax.all_to_all(message, AXES, split_axis=0, concat_axis=0, tiled=True)


def body(obs_values, obs_dest, obs_node, schur, local_inverse, coarse_inverse):
    size = schur.shape[-1]
    obs_count, realiz = obs_values.shape
    cols, rows = lax.axis_size("sx"), lax.axis_size("sy")
    devices = cols * rows
    capacity = max(2, 2 * obs_count // devices)
    edge = shape(realiz, size // 4, BF16)
    exact = [shape(realiz + PAD, size // 4)] * 4
    half, whole = shape(realiz, size // 2), shape(realiz, size)
    message = jax.ShapeDtypeStruct((devices, 1, 5 * LANES), F32)
    narrow, state_shape = shape(realiz, LANES), shape(8, LANES)
    coarse_state = shape(4 * devices, LANES)
    scratch_half = pltpu.VMEM((realiz, size // 2), BF16)
    flops = 2 * realiz * size * size
    schur_mat, inverse_mat = schur[0, 0], local_inverse[0, 0]

    packed, *coarse_mats = call(
        functools.partial(first_kernel, capacity, cols, rows),
        [shape(devices * capacity, LANES, BF16), *[shape(8, 4 * devices)] * 2],
        (obs_values.T, obs_dest.reshape(1, obs_count), obs_node.reshape(1, obs_count), coarse_inverse),
        [
            pltpu.VMEM((realiz, obs_count), BF16),
            *[pltpu.VMEM((1, obs_count), jnp.int32)] * 2,
            pltpu.VMEM(coarse_inverse.shape, F32),
            pltpu.SemaphoreType.DMA((4,)),
        ],
        COVER,
        pl.BlockSpec(memory_space=pltpu.HBM),
    )
    got = lax.all_to_all(packed.reshape(devices, capacity, LANES), AXES, split_axis=0, concat_axis=0, tiled=True)
    *image, e0, e1, e2, e3, sent = call(
        functools.partial(load_kernel, realiz),
        [half, half, *exact, message],
        (got.reshape(devices * capacity, LANES),),
        flops=COVER,
    )
    mode, olds, states = "load", ([], []), []
    for step in range(ITERS + 1):
        g, gathered = exchange((e0, e1, e2, e3)), gather(sent)
        ins = [*image, *[g[slot] for slot in ORDER], gathered, *olds[0], *olds[1]]
        if step == ITERS:
            field, resid = call(last_kernel, [whole, whole], [*ins, states[0], z[0], *track[0], z[1], *track[1]])
            return field[None, None], resid[None, None]
        count, state_count = (1, 1) if mode == "load" else (2, 3)
        outs = call(
            functools.partial(step_kernel, mode),
            [*[half] * (2 * count), narrow, *[coarse_state, state_shape, coarse_state][:state_count], shape(realiz, size, BF16), half, edge, edge, narrow],
            [*ins, *states, *coarse_mats, inverse_mat],
            flops=flops // 2,
        )
        olds, (columns, coarse), outs = (outs[:count], outs[count : 2 * count]), outs[2 * count : 2 * count + 2], outs[2 * count + 2 :]
        states, outs = [*outs[:1], coarse, *outs[1:2]] if mode != "load" else [coarse], outs[state_count - 1 :]
        scaled, part_far, e2, e3, gamma = outs
        part_near, e0, e1, gamma = call(
            rest_kernel,
            [half, edge, edge, narrow],
            (columns, scaled, olds[0][0], olds[1][0], gamma, inverse_mat),
            flops=flops // 2,
        )
        g = exchange((e0, e1, e2, e3))
        if step == 0:
            track = (), ()
        else:
            outs = call(
                functools.partial(field_kernel, mode), [half] * 4, (columns, z[0], *track[0], z[1], *track[1]), flops=1
            )
            track = outs[:2], outs[2:]
        z_far, partial = call(
            image_far_kernel, [half, whole], (part_far, g[3], g[2], schur_mat), [scratch_half], flops // 2
        )
        z_near, *image, e0, e1, e2, e3, sent = call(
            image_near_kernel,
            [half, half, half, *exact, message],
            (part_near, g[0], g[1], z_far, partial, gamma, schur_mat, *track[0][:1]),
            [scratch_half],
            flops // 2,
        )
        z = z_near, z_far
        mode = "init" if step == 0 else "next"


def solution(mesh):
    placed = (
        P(AXES, None),
        P(AXES, None),
        P(AXES),
        P("sx", "sy", None, None),
        P("sx", "sy", None, None),
        P(AXES, None),
    )
    return jax.shard_map(
        body,
        mesh=mesh,
        in_specs=placed,
        out_specs=(P("sx", "sy", None, None), P("sx", "sy", None, None)),
        check_vma=False,
    )
```

```python
import functools

import jax
import jax.numpy as jnp
from jax import lax
from jax.experimental import pallas as pl
from jax.experimental.pallas import tpu as pltpu
from jax.sharding import PartitionSpec as P

ITERS = 6
ORDER = (1, 0, 2, 3)
PAD = 16
COVER = 8e9
LANES = 128
CHUNK = 512
HP = lax.Precision.HIGHEST
F32 = jnp.float32
BF16 = jnp.bfloat16
VM = pl.BlockSpec(memory_space=pltpu.VMEM)
AXES = ("sx", "sy")


def call(kernel, outs, args, scratch=(), flops=0, spec=VM):
    size = sum(a.size * a.dtype.itemsize for a in args)
    return pl.pallas_call(
        kernel,
        out_shape=outs,
        in_specs=[spec] * len(args),
        out_specs=jax.tree.map(lambda _: VM, outs),
        scratch_shapes=list(scratch),
        compiler_params=pltpu.CompilerParams(vmem_limit_bytes=(8 if spec is VM else 56) << 20),
        cost_estimate=pl.CostEstimate(flops=int(flops), bytes_accessed=size, transcendentals=0),
    )(*args)


def shape(rows, columns, dtype=F32):
    return jax.ShapeDtypeStruct((rows, columns), dtype)


def edge_of(slot, odd_col, odd_row):
    return (1 - odd_col, 3 - odd_row, odd_col, 2 + odd_row)[slot]


class Place:
    def __init__(self):
        col, row = lax.axis_index("sx"), lax.axis_index("sy")
        cols, rows = lax.axis_size("sx"), lax.axis_size("sy")
        odd_col, odd_row = lax.rem(col, 2), lax.rem(row, 2)
        self.edges = [edge_of(slot, odd_col, odd_row) for slot in range(4)]
        far_col = jnp.where(odd_col == 1, col < cols - 1, col > 0)
        far_row = jnp.where(odd_row == 1, row < rows - 1, row > 0)
        self.shared = (None, None, far_col, far_row)

    def weight(self, slot):
        shared = self.shared[slot]
        return F32(0.5) if shared is None else jnp.where(shared, F32(0.5), F32(1.0))


def swaps():
    cols, rows = lax.axis_size("sx"), lax.axis_size("sy")
    plans = [], [], [], []
    for col in range(cols):
        for row in range(rows):
            across = col + (1 if col % 2 else -1)
            beyond = row + (1 if row % 2 else -1)
            far_sx = (across, row) if 0 <= across < cols else (col, row ^ 1)
            partners = (col ^ 1, row), (col, row ^ 1), far_sx, (col, beyond % rows)
            for plan, (to_col, to_row) in zip(plans, partners, strict=True):
                plan.append((col * rows + row, to_col * rows + to_row))
    return plans


def exchange(edges):
    plans = swaps()
    got = [None] * 4
    for slot in (2, 0, 3, 1):
        got[slot] = lax.ppermute(edges[slot], AXES, plans[slot])
    return got


def basis_parts(edge_len, start, width):
    node = lax.broadcasted_iota(jnp.int32, (1, width), 1) + start
    offset = node.astype(F32) - (edge_len - 1) / 2.0
    level = 1.0 / jnp.sqrt(F32(edge_len))
    norm = jnp.sqrt(F32(edge_len * (edge_len * edge_len - 1) / 12.0))
    return level, offset / norm


def lane_parts(value):
    return sum(value[:, i : i + LANES] for i in range(LANES, value.shape[1], LANES)) + value[:, :LANES]


def project(halves):
    edge_len = halves[0].shape[1] // 2
    columns = []
    for slot in range(4):
        flat = ramped = None
        for start in range(0, edge_len, CHUNK):
            at = slot % 2 * edge_len + start
            part = halves[slot // 2][:, at : at + CHUNK]
            ramp = basis_parts(edge_len, start, CHUNK)[1]
            one, two = lane_parts(part), lane_parts(part * ramp)
            flat = one if flat is None else flat + one
            ramped = two if ramped is None else ramped + two
        level = basis_parts(edge_len, 0, LANES)[0]
        columns.append(jnp.sum(flat, axis=1, keepdims=True) * level)
        columns.append(jnp.sum(ramped, axis=1, keepdims=True))
    return columns


def write_message(message_ref, columns, products):
    found = [*zip((0, 8, 1, 9, 2, 10, 3, 11), columns), *zip((4, 12), products)]
    rows = found[0][1].shape[0]
    lane = lax.broadcasted_iota(jnp.int32, (rows, LANES), 1)
    table = jnp.zeros((rows, LANES), F32)
    for place, column in found:
        table = jnp.where(lane == place, column, table)
    turned = table.T
    block = jnp.concatenate([turned[0:8], turned[8:16]], axis=1)
    sent = [*range(4 if columns else 0), *([4] if products else [])]
    for i, source in enumerate(sent):
        row = jnp.broadcast_to(block[source : source + 1][None], (message_ref.shape[0], 1, LANES))
        message_ref[:, :, i * LANES : (i + 1) * LANES] = row


def first_kernel(capacity, cols, rows, values_in, dest_in, node_in, inverse_in, out_ref, level_mat_ref, ramp_mat_ref,
                 values_ref, dest_ref, node_ref, inverse_ref, sems):
    pairs = ((values_in, values_ref), (dest_in, dest_ref), (node_in, node_ref), (inverse_in, inverse_ref))
    copies = [pltpu.make_async_copy(source, to, sems.at[i]) for i, (source, to) in enumerate(pairs)]
    for copy in copies:
        copy.start()
    for copy in copies:
        copy.wait()
    pack(capacity, values_ref, dest_ref, node_ref, out_ref)
    coarse_matrices(cols, rows, inverse_ref, (level_mat_ref, ramp_mat_ref))


def pack(capacity, values_ref, dest_ref, node_ref, out_ref):
    realiz, count = values_ref.shape
    slots = out_ref.shape[0]
    dest, node = dest_ref[...], node_ref[...]
    hit = lax.broadcasted_iota(jnp.int32, (slots // capacity, count), 0) == dest
    before = lax.broadcasted_iota(jnp.int32, (count, count), 0) < lax.broadcasted_iota(jnp.int32, (count, count), 1)
    hit = hit.astype(F32)
    earlier = jnp.dot(hit.astype(BF16), before.astype(F32).astype(BF16), preferred_element_type=F32)
    rank = jnp.sum(hit * earlier, axis=0, keepdims=True).astype(jnp.int32)
    slot = dest * capacity + rank
    high, low = (node // 64).astype(F32), lax.rem(node, 64).astype(F32)
    side = lax.broadcasted_iota(jnp.int32, (LANES - realiz, count), 0)
    codes = jnp.where(side == 0, high, jnp.where(side == 1, low, 0.0)).astype(BF16)
    full = jnp.concatenate([values_ref[...], codes], axis=0)
    choose = (lax.broadcasted_iota(jnp.int32, (slots, count), 0) == slot).astype(F32).astype(BF16)
    out = lax.dot_general(choose, full, (((1,), (1,)), ((), ())), preferred_element_type=F32)
    out_ref[...] = out.astype(BF16)


def coarse_matrices(cols, rows, inverse_ref, out_refs):
    devices = cols * rows
    i = lax.broadcasted_iota(jnp.int32, (8 * devices, 4 * devices), 0)
    j = lax.broadcasted_iota(jnp.int32, (8 * devices, 4 * devices), 1)
    slot, device = j // devices, j % devices
    col, row = device // rows, device % rows
    along_x = (slot == 0) | (slot == 2)
    near = slot < 2
    step_col = jnp.where(near, 1, -1) * (1 - 2 * (col % 2))
    step_row = jnp.where(near, 1, -1) * (1 - 2 * (row % 2))
    to_col = jnp.where(along_x, col + step_col, col)
    to_row = jnp.where(along_x, row, row + step_row)
    shared = (to_col >= 0) & (to_col < cols) & (to_row >= 0) & (to_row < rows)

    def index(col, row):
        odd_col, odd_row = col % 2, row % 2
        edge = jnp.where(slot == 0, 1 - odd_col, jnp.where(slot == 1, 3 - odd_row, jnp.where(slot == 2, odd_col, 2 + odd_row)))
        return (col * rows + row) * 8 + edge * 2

    own, other = index(col, row), index(to_col, to_row)
    place = Place()
    k = lax.broadcasted_iota(jnp.int32, (8, 8), 0)
    from_row = lax.broadcasted_iota(jnp.int32, (8, 8), 1)
    edge = place.edges[3]
    for s in range(3):
        edge = jnp.where(k // 2 == s, place.edges[s], edge)
    pick = (from_row == 2 * edge + k % 2).astype(F32)
    mine = jnp.dot(pick, inverse_ref[...], precision=HP, preferred_element_type=F32)
    for part, out_ref in enumerate(out_refs):
        table = jnp.where(shared & (i == other + part), 0.5, jnp.where(i == own + part, jnp.where(shared, 0.5, 1.0), 0.0))
        out_ref[...] = jnp.dot(mine, table, precision=HP, preferred_element_type=F32)


def load_kernel(realiz, got_ref, near_ref, far_ref, e0, e1, e2, e3, message_ref):
    place, slots, edge_len = Place(), got_ref.shape[0], e0.shape[1]
    got = got_ref[...]
    node = got[:, realiz : realiz + 1].astype(F32) * 64.0 + got[:, realiz + 1 : realiz + 2].astype(F32)
    node = node.astype(jnp.int32)
    halves = near_ref, far_ref
    for slot, edge_ref in enumerate((e0, e1, e2, e3)):
        for start in range(0, edge_len, CHUNK):
            first = place.edges[slot] * edge_len + start
            here = lax.broadcasted_iota(jnp.int32, (slots, CHUNK), 1) + first == node
            load = lax.dot_general(got, here.astype(F32).astype(BF16), (((0,), (0,)), ((), ())), preferred_element_type=F32)
            at = slot % 2 * edge_len + start
            halves[slot // 2][:, at : at + CHUNK] = load[:realiz]
            edge_ref[:realiz, start : start + CHUNK] = load[:realiz]
    write_message(message_ref, project(halves), ())


def product(place, slots, vec_ref, matrix_ref, slot, start):
    edge_len = vec_ref.shape[1] // len(slots)
    column = pl.multiple_of(place.edges[slot] * edge_len + start, CHUNK)
    total = None
    for i, source in enumerate(slots):
        row = pl.multiple_of(place.edges[source] * edge_len, edge_len)
        block = matrix_ref[pl.ds(row, edge_len), pl.ds(column, CHUNK)]
        part = jnp.dot(vec_ref[:, i * edge_len : (i + 1) * edge_len], block, preferred_element_type=F32)
        total = part if total is None else total + part
    return total


def image_far_kernel(part_ref, g3, g2, schur_ref, precon_ref, sum_ref, rounded):
    place, edge_len = Place(), g2.shape[1]
    for i, got in enumerate((g2, g3)):
        at = pl.ds(i * edge_len, edge_len)
        value = part_ref[:, at] + jnp.where(place.shared[2 + i], got[...].astype(F32), 0.0)
        precon_ref[:, at] = value
        rounded[:, at] = value.astype(BF16)
    for slot in range(4):
        for start in range(0, edge_len, CHUNK):
            sum_ref[:, pl.ds(slot * edge_len + start, CHUNK)] = product(place, (2, 3), rounded, schur_ref, slot, start)


def image_near_kernel(part_ref, g0, g1, far_ref, sum_ref, gamma_ref, schur_ref, *refs):
    precon_ref, image_near_ref, image_far_ref, e0, e1, e2, e3, message_ref, rounded = refs[-9:]
    place, edge_len = Place(), g0.shape[1]
    for i, got in enumerate((g0, g1)):
        at = pl.ds(i * edge_len, edge_len)
        value = part_ref[:, at] + got[...].astype(F32)
        precon_ref[:, at] = value
        rounded[:, at] = value.astype(BF16)
    halves, vectors = (image_near_ref, image_far_ref), (precon_ref, far_ref)
    delta = None
    for slot, edge_ref in enumerate((e0, e1, e2, e3)):
        for start in range(0, edge_len, CHUNK):
            image = sum_ref[:, pl.ds(slot * edge_len + start, CHUNK)] + product(place, (0, 1), rounded, schur_ref, slot, start)
            at = pl.ds(slot % 2 * edge_len + start, CHUNK)
            halves[slot // 2][:, at] = image
            edge_ref[: image.shape[0], pl.ds(start, CHUNK)] = image
            here = lane_parts(vectors[slot // 2][:, at] * image)
            delta = here if delta is None else delta + here
    gamma = jnp.sum(gamma_ref[...], axis=1, keepdims=True)
    delta = jnp.sum(delta, axis=1, keepdims=True)
    columns = project(halves) if message_ref.shape[2] > LANES else ()
    write_message(message_ref, columns, (gamma, delta))


def coarse_table(gathered_ref, full):
    devices = gathered_ref.shape[0]
    for slot in range(4):
        full[slot * devices : (slot + 1) * devices] = gathered_ref[:, 0, slot * LANES : (slot + 1) * LANES]


def scalars(mode, gathered_ref, state_in, state_ref, realiz):
    total = jnp.sum(gathered_ref[:, 0, gathered_ref.shape[2] - LANES :], axis=0, keepdims=True)
    lane = lax.broadcasted_iota(jnp.int32, (1, LANES), 1)
    swapped = pltpu.roll(total, LANES // 2, 1)
    gamma = jnp.where(lane < realiz, total, swapped)
    delta = jnp.where(lane < realiz, swapped, total)
    if mode == "init":
        alpha, beta = gamma / delta, jnp.zeros_like(gamma)
    else:
        beta = gamma / state_in[0:1]
        alpha = gamma / (delta - beta * gamma / state_in[1:2])
    if state_ref is not None:
        state_ref[0:1] = gamma
        state_ref[1:2] = alpha
    return alpha, beta


def turn(rows, realiz):
    count = sum(row.shape[0] for row in rows)
    return jnp.concatenate([*rows, jnp.zeros((LANES - count, LANES), F32)], axis=0).T[:realiz]


def in_slots(refs):
    return [refs[ORDER.index(slot)] for slot in range(4)]


def new_residual(place, slot, mode, columns, image_ref, got_ref, old, at, start):
    got = got_ref[: image_ref.shape[0], pl.ds(start, CHUNK)]
    shared = place.shared[slot]
    applied = image_ref[:, at] + (got if shared is None else jnp.where(shared, got, 0.0))
    if mode == "load":
        return None, applied
    if mode == "next":
        applied = applied + columns[:, 1:2] * old[1][:, at]
    return applied, old[0][:, at] - columns[:, 0:1] * applied


def new_field(mode, columns, precon_ref, old, at):
    direction = precon_ref[:, at]
    if mode == "init":
        return direction, columns[:, 0:1] * direction
    direction = direction + columns[:, 1:2] * old[0][:, at]
    return direction, old[1][:, at] + columns[:, 0:1] * direction


def precondition(place, columns, scaled, inverse_ref, part_at, resid_refs, edge_refs, gamma):
    edge_len = scaled.shape[1] // 4
    for slot in part_at:
        flat, ramp_by = (columns[:, 8 + 2 * slot + i : 9 + 2 * slot + i] for i in range(2))
        for start in range(0, edge_len, CHUNK):
            level, ramp = basis_parts(edge_len, start, CHUNK)
            part = product(place, (0, 1, 2, 3), scaled, inverse_ref, slot, start)
            part = place.weight(slot) * (part + (flat * level + ramp_by * ramp))
            part_ref, first = part_at[slot]
            part_ref[:, pl.ds(first + start, CHUNK)] = part
            edge_refs[slot][:, pl.ds(start, CHUNK)] = part.astype(BF16)
            here = lane_parts(resid_refs[slot // 2][:, pl.ds(slot % 2 * edge_len + start, CHUNK)] * part)
            gamma = here if gamma is None else gamma + here
    return gamma


OLD = {"load": 0, "init": 1, "next": 2}


def step_kernel(mode, *refs):
    refs = list(refs)
    take = lambda n: [refs.pop(0) for _ in range(n)]
    place = Place()
    images, edges, (gathered_ref,) = take(2), in_slots(take(4)), take(1)
    olds = [take(OLD[mode]) for _ in range(2)]
    state_in, = take(1) if mode == "next" else (None,)
    coarse_in, = take(1) if mode != "load" else (None,)
    applied_in, = take(1) if mode == "next" else (None,)
    level_mat_ref, ramp_mat_ref, inverse_ref = take(3)
    news = [take(1 if mode == "load" else 2) for _ in range(2)]
    columns_ref, coarse_ref = take(2)
    state_ref, applied_ref = take(2) if mode != "load" else (None, None)
    scaled, part_ref, e2, e3, gamma_ref = take(5)
    realiz, edge_len = images[0].shape[0], edges[0].shape[1]
    if mode == "load":
        coarse_table(gathered_ref, coarse_ref)
        coarse = coarse_ref[...]
        rows, columns = [jnp.zeros((8, LANES), F32)], None
    else:
        alpha, beta = scalars(mode, gathered_ref, state_in, state_ref, realiz)
        columns = turn([alpha, beta], realiz)
        coarse_table(gathered_ref, applied_ref)
        if mode == "next":
            applied_ref[...] = applied_ref[...] + beta * applied_in[...]
        coarse = coarse_in[...] - alpha * applied_ref[...]
        coarse_ref[...] = coarse
        rows = [alpha, beta, jnp.zeros((6, LANES), F32)]
    for slot in range(4):
        half = slot // 2
        for start in range(0, edge_len, CHUNK):
            at = pl.ds(slot % 2 * edge_len + start, CHUNK)
            applied, resid = new_residual(place, slot, mode, columns, images[half], edges[slot], olds[half], at, start)
            news[half][0][:, at] = resid
            if applied is not None:
                news[half][1][:, at] = applied
            scaled[:, pl.ds(slot * edge_len + start, CHUNK)] = (place.weight(slot) * resid).astype(BF16)
    level = jnp.dot(level_mat_ref[...], coarse, precision=HP, preferred_element_type=F32)
    ramp = jnp.dot(ramp_mat_ref[...], coarse, precision=HP, preferred_element_type=F32)
    rows.append(level + pltpu.roll(ramp, LANES // 2, 1))
    columns = turn(rows, realiz)
    columns_ref[...] = columns
    resids = [new[0] for new in news]
    part_at = {2: (part_ref, 0), 3: (part_ref, edge_len)}
    gamma_ref[...] = precondition(place, columns, scaled, inverse_ref, part_at, resids, {2: e2, 3: e3}, None)


def rest_kernel(columns_ref, scaled, near_ref, far_ref, gamma_in, inverse_ref, part_ref, e0, e1, gamma_ref):
    part_at = {0: (part_ref, 0), 1: (part_ref, scaled.shape[1] // 4)}
    gamma_ref[...] = precondition(
        Place(), columns_ref[...], scaled, inverse_ref, part_at, (near_ref, far_ref), {0: e0, 1: e1}, gamma_in[...]
    )


def field_kernel(mode, columns_ref, *refs):
    old = 0 if mode == "init" else 2
    columns = columns_ref[...]
    for half in range(2):
        precon_ref, *olds = refs[half * (1 + old) : (half + 1) * (1 + old)]
        direction_ref, field_ref = refs[2 * (1 + old) + 2 * half : 2 * (1 + old) + 2 * half + 2]
        for start in range(0, precon_ref.shape[1], CHUNK):
            at = pl.ds(start, CHUNK)
            direction_ref[:, at], field_ref[:, at] = new_field(mode, columns, precon_ref, olds, at)


def last_kernel(*refs):
    refs = list(refs)
    take = lambda n: [refs.pop(0) for _ in range(n)]
    place = Place()
    images, edges, (gathered_ref,) = take(2), in_slots(take(4)), take(1)
    olds, (state_in,), tracks = [take(2) for _ in range(2)], take(1), [take(3) for _ in range(2)]
    field_ref, resid_ref = refs
    realiz, edge_len = images[0].shape[0], edges[0].shape[1]
    columns = turn(scalars("next", gathered_ref, state_in, None, realiz), realiz)
    for slot in range(4):
        half = slot // 2
        for start in range(0, edge_len, CHUNK):
            at = pl.ds(slot % 2 * edge_len + start, CHUNK)
            to = pl.ds(pl.multiple_of(place.edges[slot] * edge_len + start, CHUNK), CHUNK)
            _, resid_ref[:, to] = new_residual(place, slot, "next", columns, images[half], edges[slot], olds[half], at, start)
            _, field_ref[:, to] = new_field("next", columns, tracks[half][0], tracks[half][1:], at)


def gather(message):
    return lax.all_to_all(message, AXES, split_axis=0, concat_axis=0, tiled=True)


def body(obs_values, obs_dest, obs_node, schur, local_inverse, coarse_inverse):
    size = schur.shape[-1]
    obs_count, realiz = obs_values.shape
    cols, rows = lax.axis_size("sx"), lax.axis_size("sy")
    devices = cols * rows
    capacity = max(2, 2 * obs_count // devices)
    edge = shape(realiz, size // 4, BF16)
    exact, padded = [shape(realiz, size // 4)] * 4, [shape(realiz + PAD, size // 4)] * 4
    half, whole = shape(realiz, size // 2), shape(realiz, size)
    first, message, last = (jax.ShapeDtypeStruct((devices, 1, rows_sent * LANES), F32) for rows_sent in (4, 5, 1))
    narrow, state_shape = shape(realiz, LANES), shape(8, LANES)
    coarse_state = shape(4 * devices, LANES)
    scratch_half = pltpu.VMEM((realiz, size // 2), BF16)
    flops = 2 * realiz * size * size
    schur_mat, inverse_mat = schur[0, 0], local_inverse[0, 0]

    packed, *coarse_mats = call(
        functools.partial(first_kernel, capacity, cols, rows),
        [shape(devices * capacity, LANES, BF16), *[shape(8, 4 * devices)] * 2],
        (obs_values.T, obs_dest.reshape(1, obs_count), obs_node.reshape(1, obs_count), coarse_inverse),
        [
            pltpu.VMEM((realiz, obs_count), BF16),
            *[pltpu.VMEM((1, obs_count), jnp.int32)] * 2,
            pltpu.VMEM(coarse_inverse.shape, F32),
            pltpu.SemaphoreType.DMA((4,)),
        ],
        COVER,
        pl.BlockSpec(memory_space=pltpu.HBM),
    )
    got = lax.all_to_all(packed.reshape(devices, capacity, LANES), AXES, split_axis=0, concat_axis=0, tiled=True)
    *image, e0, e1, e2, e3, sent = call(
        functools.partial(load_kernel, realiz),
        [half, half, *exact, first],
        (got.reshape(devices * capacity, LANES),),
        flops=COVER,
    )
    mode, olds, states = "load", ([], []), []
    for step in range(ITERS + 1):
        g, gathered = exchange((e0, e1, e2, e3)), gather(sent)
        ins = [*image, *[g[slot] for slot in ORDER], gathered, *olds[0], *olds[1]]
        if step == ITERS:
            field, resid = call(last_kernel, [whole, whole], [*ins, states[0], z[0], *track[0], z[1], *track[1]])
            return field[None, None], resid[None, None]
        count, state_count = (1, 1) if mode == "load" else (2, 3)
        outs = call(
            functools.partial(step_kernel, mode),
            [*[half] * (2 * count), narrow, *[coarse_state, state_shape, coarse_state][:state_count], shape(realiz, size, BF16), half, edge, edge, narrow],
            [*ins, *states, *coarse_mats, inverse_mat],
            flops=flops // 2,
        )
        olds, (columns, coarse), outs = (outs[:count], outs[count : 2 * count]), outs[2 * count : 2 * count + 2], outs[2 * count + 2 :]
        states, outs = [*outs[:1], coarse, *outs[1:2]] if mode != "load" else [coarse], outs[state_count - 1 :]
        scaled, part_far, e2, e3, gamma = outs
        part_near, e0, e1, gamma = call(
            rest_kernel,
            [half, edge, edge, narrow],
            (columns, scaled, olds[0][0], olds[1][0], gamma, inverse_mat),
            flops=flops // 2,
        )
        g = exchange((e0, e1, e2, e3))
        if step == 0:
            track = (), ()
        else:
            outs = call(
                functools.partial(field_kernel, mode), [half] * 4, (columns, z[0], *track[0], z[1], *track[1]), flops=1
            )
            track = outs[:2], outs[2:]
        z_far, partial = call(
            image_far_kernel, [half, whole], (part_far, g[3], g[2], schur_mat), [scratch_half], flops // 2
        )
        z_near, *image, e0, e1, e2, e3, sent = call(
            image_near_kernel,
            [half, half, half, *([*exact, last] if step == ITERS - 1 else [*padded, message])],
            (part_near, g[0], g[1], z_far, partial, gamma, schur_mat, *track[0][:1]),
            [scratch_half],
            flops // 2,
        )
        z = z_near, z_far
        mode = "init" if step == 0 else "next"


def solution(mesh):
    placed = (
        P(AXES, None),
        P(AXES, None),
        P(AXES),
        P("sx", "sy", None, None),
        P("sx", "sy", None, None),
        P(AXES, None),
    )
    return jax.shard_map(
        body,
        mesh=mesh,
        in_specs=placed,
        out_specs=(P("sx", "sy", None, None), P("sx", "sy", None, None)),
        check_vma=False,
    )
```

```python
import functools

import jax
import jax.numpy as jnp
from jax import lax
from jax.experimental import pallas as pl
from jax.experimental.pallas import tpu as pltpu
from jax.sharding import PartitionSpec as P

ITERS = 6
LOAD_ORDER = (2, 3, 0, 1)
ORDER = (1, 0, 2, 3)
PAD = 16
COVER = 8e9
LANES = 128
CHUNK = 512
STEP = 256
HP = lax.Precision.HIGHEST
F32 = jnp.float32
BF16 = jnp.bfloat16
VM = pl.BlockSpec(memory_space=pltpu.VMEM)
AXES = ("sx", "sy")


def call(kernel, outs, args, scratch=(), flops=0, spec=VM):
    size = sum(a.size * a.dtype.itemsize for a in args)
    return pl.pallas_call(
        kernel,
        out_shape=outs,
        in_specs=[spec] * len(args),
        out_specs=jax.tree.map(lambda _: VM, outs),
        scratch_shapes=list(scratch),
        compiler_params=pltpu.CompilerParams(vmem_limit_bytes=(8 if spec is VM else 56) << 20),
        cost_estimate=pl.CostEstimate(flops=int(flops), bytes_accessed=size, transcendentals=0),
    )(*args)


def shape(rows, columns, dtype=F32):
    return jax.ShapeDtypeStruct((rows, columns), dtype)


def edge_of(slot, odd_col, odd_row):
    return (1 - odd_col, 3 - odd_row, odd_col, 2 + odd_row)[slot]


class Place:
    def __init__(self):
        col, row = lax.axis_index("sx"), lax.axis_index("sy")
        cols, rows = lax.axis_size("sx"), lax.axis_size("sy")
        odd_col, odd_row = lax.rem(col, 2), lax.rem(row, 2)
        self.edges = [edge_of(slot, odd_col, odd_row) for slot in range(4)]
        far_col = jnp.where(odd_col == 1, col < cols - 1, col > 0)
        far_row = jnp.where(odd_row == 1, row < rows - 1, row > 0)
        self.shared = (None, None, far_col, far_row)

    def weight(self, slot):
        shared = self.shared[slot]
        return F32(0.5) if shared is None else jnp.where(shared, F32(0.5), F32(1.0))


def swaps():
    cols, rows = lax.axis_size("sx"), lax.axis_size("sy")
    plans = [], [], [], []
    for col in range(cols):
        for row in range(rows):
            across = col + (1 if col % 2 else -1)
            beyond = row + (1 if row % 2 else -1)
            far_sx = (across, row) if 0 <= across < cols else (col, row ^ 1)
            partners = (col ^ 1, row), (col, row ^ 1), far_sx, (col, beyond % rows)
            for plan, (to_col, to_row) in zip(plans, partners, strict=True):
                plan.append((col * rows + row, to_col * rows + to_row))
    return plans


def exchange(edges):
    plans = swaps()
    got = [None] * 4
    for slot in (2, 0, 3, 1):
        got[slot] = lax.ppermute(edges[slot], AXES, plans[slot])
    return got


def basis_parts(edge_len, start, width):
    node = lax.broadcasted_iota(jnp.int32, (1, width), 1) + start
    offset = node.astype(F32) - (edge_len - 1) / 2.0
    level = 1.0 / jnp.sqrt(F32(edge_len))
    norm = jnp.sqrt(F32(edge_len * (edge_len * edge_len - 1) / 12.0))
    return level, offset / norm


def lane_parts(value):
    return sum(value[:, i : i + LANES] for i in range(LANES, value.shape[1], LANES)) + value[:, :LANES]


def project(halves):
    edge_len = halves[0].shape[1] // 2
    columns = []
    for slot in range(4):
        flat = ramped = None
        for start in range(0, edge_len, CHUNK):
            at = slot % 2 * edge_len + start
            part = halves[slot // 2][:, at : at + CHUNK]
            ramp = basis_parts(edge_len, start, CHUNK)[1]
            one, two = lane_parts(part), lane_parts(part * ramp)
            flat = one if flat is None else flat + one
            ramped = two if ramped is None else ramped + two
        level = basis_parts(edge_len, 0, LANES)[0]
        columns.append(jnp.sum(flat, axis=1, keepdims=True) * level)
        columns.append(jnp.sum(ramped, axis=1, keepdims=True))
    return columns


def write_message(message_ref, columns, products):
    found = [*zip((0, 8, 1, 9, 2, 10, 3, 11), columns), *zip((4, 12), products)]
    rows = found[0][1].shape[0]
    lane = lax.broadcasted_iota(jnp.int32, (rows, LANES), 1)
    table = jnp.zeros((rows, LANES), F32)
    for place, column in found:
        table = jnp.where(lane == place, column, table)
    turned = table.T
    block = jnp.concatenate([turned[0:8], turned[8:16]], axis=1)
    sent = [*range(4 if columns else 0), *([4] if products else [])]
    for i, source in enumerate(sent):
        row = jnp.broadcast_to(block[source : source + 1][None], (message_ref.shape[0], 1, LANES))
        message_ref[:, :, i * LANES : (i + 1) * LANES] = row


def first_kernel(capacity, cols, rows, values_in, dest_in, node_in, inverse_in, out_ref, level_mat_ref, ramp_mat_ref,
                 values_ref, dest_ref, node_ref, inverse_ref, sems):
    pairs = ((values_in, values_ref), (dest_in, dest_ref), (node_in, node_ref), (inverse_in, inverse_ref))
    copies = [pltpu.make_async_copy(source, to, sems.at[i]) for i, (source, to) in enumerate(pairs)]
    for copy in copies:
        copy.start()
    for copy in copies:
        copy.wait()
    pack(capacity, values_ref, dest_ref, node_ref, out_ref)
    coarse_matrices(cols, rows, inverse_ref, (level_mat_ref, ramp_mat_ref))


def pack(capacity, values_ref, dest_ref, node_ref, out_ref):
    realiz, count = values_ref.shape
    slots = out_ref.shape[0]
    dest, node = dest_ref[...], node_ref[...]
    hit = lax.broadcasted_iota(jnp.int32, (slots // capacity, count), 0) == dest
    before = lax.broadcasted_iota(jnp.int32, (count, count), 0) < lax.broadcasted_iota(jnp.int32, (count, count), 1)
    hit = hit.astype(F32)
    earlier = jnp.dot(hit.astype(BF16), before.astype(F32).astype(BF16), preferred_element_type=F32)
    rank = jnp.sum(hit * earlier, axis=0, keepdims=True).astype(jnp.int32)
    slot = dest * capacity + rank
    high, low = (node // 64).astype(F32), lax.rem(node, 64).astype(F32)
    side = lax.broadcasted_iota(jnp.int32, (LANES - realiz, count), 0)
    codes = jnp.where(side == 0, high, jnp.where(side == 1, low, 0.0)).astype(BF16)
    full = jnp.concatenate([values_ref[...], codes], axis=0)
    choose = (lax.broadcasted_iota(jnp.int32, (slots, count), 0) == slot).astype(F32).astype(BF16)
    out = lax.dot_general(choose, full, (((1,), (1,)), ((), ())), preferred_element_type=F32)
    out_ref[...] = out.astype(BF16)


def coarse_matrices(cols, rows, inverse_ref, out_refs):
    devices = cols * rows
    i = lax.broadcasted_iota(jnp.int32, (8 * devices, 4 * devices), 0)
    j = lax.broadcasted_iota(jnp.int32, (8 * devices, 4 * devices), 1)
    slot, device = j // devices, j % devices
    col, row = device // rows, device % rows
    along_x = (slot == 0) | (slot == 2)
    near = slot < 2
    step_col = jnp.where(near, 1, -1) * (1 - 2 * (col % 2))
    step_row = jnp.where(near, 1, -1) * (1 - 2 * (row % 2))
    to_col = jnp.where(along_x, col + step_col, col)
    to_row = jnp.where(along_x, row, row + step_row)
    shared = (to_col >= 0) & (to_col < cols) & (to_row >= 0) & (to_row < rows)

    def index(col, row):
        odd_col, odd_row = col % 2, row % 2
        edge = jnp.where(slot == 0, 1 - odd_col, jnp.where(slot == 1, 3 - odd_row, jnp.where(slot == 2, odd_col, 2 + odd_row)))
        return (col * rows + row) * 8 + edge * 2

    own, other = index(col, row), index(to_col, to_row)
    place = Place()
    k = lax.broadcasted_iota(jnp.int32, (8, 8), 0)
    from_row = lax.broadcasted_iota(jnp.int32, (8, 8), 1)
    edge = place.edges[3]
    for s in range(3):
        edge = jnp.where(k // 2 == s, place.edges[s], edge)
    pick = (from_row == 2 * edge + k % 2).astype(F32)
    mine = jnp.dot(pick, inverse_ref[...], precision=HP, preferred_element_type=F32)
    for part, out_ref in enumerate(out_refs):
        table = jnp.where(shared & (i == other + part), 0.5, jnp.where(i == own + part, jnp.where(shared, 0.5, 1.0), 0.0))
        out_ref[...] = jnp.dot(mine, table, precision=HP, preferred_element_type=F32)


def load_kernel(realiz, got_ref, near_ref, far_ref, e0, e1, e2, e3, message_ref):
    place, slots, edge_len = Place(), got_ref.shape[0], e0.shape[1]
    got = got_ref[...]
    node = got[:, realiz : realiz + 1].astype(F32) * 64.0 + got[:, realiz + 1 : realiz + 2].astype(F32)
    node = node.astype(jnp.int32)
    halves = near_ref, far_ref
    for slot, edge_ref in enumerate((e0, e1, e2, e3)):
        for start in range(0, edge_len, CHUNK):
            first = place.edges[slot] * edge_len + start
            here = lax.broadcasted_iota(jnp.int32, (slots, CHUNK), 1) + first == node
            load = lax.dot_general(got, here.astype(F32).astype(BF16), (((0,), (0,)), ((), ())), preferred_element_type=F32)
            at = slot % 2 * edge_len + start
            halves[slot // 2][:, at : at + CHUNK] = load[:realiz]
            edge_ref[:realiz, start : start + CHUNK] = load[:realiz]
    write_message(message_ref, project(halves), ())


def product(place, slots, vec_ref, matrix_ref, slot, start):
    edge_len = vec_ref.shape[1] // len(slots)
    column = pl.multiple_of(place.edges[slot] * edge_len + start, CHUNK)
    total = None
    for i, source in enumerate(slots):
        row = pl.multiple_of(place.edges[source] * edge_len, edge_len)
        block = matrix_ref[pl.ds(row, edge_len), pl.ds(column, CHUNK)]
        part = jnp.dot(vec_ref[:, i * edge_len : (i + 1) * edge_len], block, preferred_element_type=F32)
        total = part if total is None else total + part
    return total


def image_far_kernel(part_ref, g3, g2, schur_ref, precon_ref, sum_ref, rounded):
    place, edge_len = Place(), g2.shape[1]
    for i, got in enumerate((g2, g3)):
        at = pl.ds(i * edge_len, edge_len)
        value = part_ref[:, at] + jnp.where(place.shared[2 + i], got[...].astype(F32), 0.0)
        precon_ref[:, at] = value
        rounded[:, at] = value.astype(BF16)
    for slot in range(4):
        for start in range(0, edge_len, CHUNK):
            sum_ref[:, pl.ds(slot * edge_len + start, CHUNK)] = product(place, (2, 3), rounded, schur_ref, slot, start)


def image_near_kernel(part_ref, g0, g1, far_ref, sum_ref, gamma_ref, schur_ref, *refs):
    precon_ref, image_near_ref, image_far_ref, e0, e1, e2, e3, message_ref, rounded = refs[-9:]
    place, edge_len = Place(), g0.shape[1]
    for i, got in enumerate((g0, g1)):
        at = pl.ds(i * edge_len, edge_len)
        value = part_ref[:, at] + got[...].astype(F32)
        precon_ref[:, at] = value
        rounded[:, at] = value.astype(BF16)
    halves, vectors = (image_near_ref, image_far_ref), (precon_ref, far_ref)
    delta = None
    for slot, edge_ref in enumerate((e0, e1, e2, e3)):
        for start in range(0, edge_len, CHUNK):
            image = sum_ref[:, pl.ds(slot * edge_len + start, CHUNK)] + product(place, (0, 1), rounded, schur_ref, slot, start)
            at = pl.ds(slot % 2 * edge_len + start, CHUNK)
            halves[slot // 2][:, at] = image
            edge_ref[: image.shape[0], pl.ds(start, CHUNK)] = image
            here = lane_parts(vectors[slot // 2][:, at] * image)
            delta = here if delta is None else delta + here
    gamma = jnp.sum(gamma_ref[...], axis=1, keepdims=True)
    delta = jnp.sum(delta, axis=1, keepdims=True)
    columns = project(halves) if message_ref.shape[2] > LANES else ()
    write_message(message_ref, columns, (gamma, delta))


def coarse_table(gathered_ref, full):
    devices = gathered_ref.shape[0]
    for slot in range(4):
        full[slot * devices : (slot + 1) * devices] = gathered_ref[:, 0, slot * LANES : (slot + 1) * LANES]


def scalars(mode, gathered_ref, state_in, state_ref, realiz):
    total = jnp.sum(gathered_ref[:, 0, gathered_ref.shape[2] - LANES :], axis=0, keepdims=True)
    lane = lax.broadcasted_iota(jnp.int32, (1, LANES), 1)
    swapped = pltpu.roll(total, LANES // 2, 1)
    gamma = jnp.where(lane < realiz, total, swapped)
    delta = jnp.where(lane < realiz, swapped, total)
    if mode == "init":
        alpha, beta = gamma / delta, jnp.zeros_like(gamma)
    else:
        beta = gamma / state_in[0:1]
        alpha = gamma / (delta - beta * gamma / state_in[1:2])
    if state_ref is not None:
        state_ref[0:1] = gamma
        state_ref[1:2] = alpha
    return alpha, beta


def turn(rows, realiz):
    count = sum(row.shape[0] for row in rows)
    return jnp.concatenate([*rows, jnp.zeros((LANES - count, LANES), F32)], axis=0).T[:realiz]


def in_slots(refs, order):
    return [refs[order.index(slot)] for slot in range(4)]


def new_residual(place, slot, mode, columns, image_ref, got_ref, old, at, start):
    got = got_ref[: image_ref.shape[0], pl.ds(start, STEP)]
    shared = place.shared[slot]
    applied = image_ref[:, at] + (got if shared is None else jnp.where(shared, got, 0.0))
    if mode == "load":
        return None, applied
    if mode == "next":
        applied = applied + columns[:, 1:2] * old[1][:, at]
    return applied, old[0][:, at] - columns[:, 0:1] * applied


def new_field(mode, columns, precon_ref, old, at):
    direction = precon_ref[:, at]
    if mode == "init":
        return direction, columns[:, 0:1] * direction
    direction = direction + columns[:, 1:2] * old[0][:, at]
    return direction, old[1][:, at] + columns[:, 0:1] * direction


def precondition(place, columns, scaled, inverse_ref, part_at, resid_refs, edge_refs, gamma):
    edge_len = scaled.shape[1] // 4
    for slot in part_at:
        flat, ramp_by = (columns[:, 8 + 2 * slot + i : 9 + 2 * slot + i] for i in range(2))
        for start in range(0, edge_len, CHUNK):
            level, ramp = basis_parts(edge_len, start, CHUNK)
            part = product(place, (0, 1, 2, 3), scaled, inverse_ref, slot, start)
            part = place.weight(slot) * (part + (flat * level + ramp_by * ramp))
            part_ref, first = part_at[slot]
            part_ref[:, pl.ds(first + start, CHUNK)] = part
            edge_refs[slot][:, pl.ds(start, CHUNK)] = part.astype(BF16)
            here = lane_parts(resid_refs[slot // 2][:, pl.ds(slot % 2 * edge_len + start, CHUNK)] * part)
            gamma = here if gamma is None else gamma + here
    return gamma


OLD = {"load": 0, "init": 1, "next": 2}


def step_kernel(mode, *refs):
    refs = list(refs)
    take = lambda n: [refs.pop(0) for _ in range(n)]
    place = Place()
    images, edges, (gathered_ref,) = take(2), in_slots(take(4), LOAD_ORDER if mode == "load" else ORDER), take(1)
    olds = [take(OLD[mode]) for _ in range(2)]
    state_in, = take(1) if mode == "next" else (None,)
    coarse_in, = take(1) if mode != "load" else (None,)
    applied_in, = take(1) if mode == "next" else (None,)
    level_mat_ref, ramp_mat_ref, inverse_ref = take(3)
    news = [take(1 if mode == "load" else 2) for _ in range(2)]
    columns_ref, coarse_ref = take(2)
    state_ref, applied_ref = take(2) if mode != "load" else (None, None)
    scaled, part_ref, e2, e3, gamma_ref = take(5)
    realiz, edge_len = images[0].shape[0], edges[0].shape[1]
    if mode == "load":
        coarse_table(gathered_ref, coarse_ref)
        coarse = coarse_ref[...]
        rows, columns = [jnp.zeros((8, LANES), F32)], None
    else:
        alpha, beta = scalars(mode, gathered_ref, state_in, state_ref, realiz)
        columns = turn([alpha, beta], realiz)
        coarse_table(gathered_ref, applied_ref)
        if mode == "next":
            applied_ref[...] = applied_ref[...] + beta * applied_in[...]
        coarse = coarse_in[...] - alpha * applied_ref[...]
        coarse_ref[...] = coarse
        rows = [alpha, beta, jnp.zeros((6, LANES), F32)]
    for slot in range(4):
        half = slot // 2
        for start in range(0, edge_len, STEP):
            at = pl.ds(slot % 2 * edge_len + start, STEP)
            applied, resid = new_residual(place, slot, mode, columns, images[half], edges[slot], olds[half], at, start)
            news[half][0][:, at] = resid
            if applied is not None:
                news[half][1][:, at] = applied
            scaled[:, pl.ds(slot * edge_len + start, STEP)] = (place.weight(slot) * resid).astype(BF16)
    level = jnp.dot(level_mat_ref[...], coarse, precision=HP, preferred_element_type=F32)
    ramp = jnp.dot(ramp_mat_ref[...], coarse, precision=HP, preferred_element_type=F32)
    rows.append(level + pltpu.roll(ramp, LANES // 2, 1))
    columns = turn(rows, realiz)
    columns_ref[...] = columns
    resids = [new[0] for new in news]
    part_at = {2: (part_ref, 0), 3: (part_ref, edge_len)}
    gamma_ref[...] = precondition(place, columns, scaled, inverse_ref, part_at, resids, {2: e2, 3: e3}, None)


def rest_kernel(columns_ref, scaled, near_ref, far_ref, gamma_in, inverse_ref, part_ref, e0, e1, gamma_ref):
    part_at = {0: (part_ref, 0), 1: (part_ref, scaled.shape[1] // 4)}
    gamma_ref[...] = precondition(
        Place(), columns_ref[...], scaled, inverse_ref, part_at, (near_ref, far_ref), {0: e0, 1: e1}, gamma_in[...]
    )


def field_kernel(mode, columns_ref, *refs):
    old = 0 if mode == "init" else 2
    columns = columns_ref[...]
    for half in range(2):
        precon_ref, *olds = refs[half * (1 + old) : (half + 1) * (1 + old)]
        direction_ref, field_ref = refs[2 * (1 + old) + 2 * half : 2 * (1 + old) + 2 * half + 2]
        for start in range(0, precon_ref.shape[1], STEP):
            at = pl.ds(start, STEP)
            direction_ref[:, at], field_ref[:, at] = new_field(mode, columns, precon_ref, olds, at)


def last_kernel(*refs):
    refs = list(refs)
    take = lambda n: [refs.pop(0) for _ in range(n)]
    place = Place()
    images, edges, (gathered_ref,) = take(2), in_slots(take(4), ORDER), take(1)
    olds, (state_in,), tracks = [take(2) for _ in range(2)], take(1), [take(3) for _ in range(2)]
    field_ref, resid_ref = refs
    realiz, edge_len = images[0].shape[0], edges[0].shape[1]
    columns = turn(scalars("next", gathered_ref, state_in, None, realiz), realiz)
    for slot in range(4):
        half = slot // 2
        for start in range(0, edge_len, STEP):
            at = pl.ds(slot % 2 * edge_len + start, STEP)
            to = pl.ds(pl.multiple_of(place.edges[slot] * edge_len + start, STEP), STEP)
            _, resid_ref[:, to] = new_residual(place, slot, "next", columns, images[half], edges[slot], olds[half], at, start)
            _, field_ref[:, to] = new_field("next", columns, tracks[half][0], tracks[half][1:], at)


def gather(message):
    return lax.all_to_all(message, AXES, split_axis=0, concat_axis=0, tiled=True)


def body(obs_values, obs_dest, obs_node, schur, local_inverse, coarse_inverse):
    size = schur.shape[-1]
    obs_count, realiz = obs_values.shape
    cols, rows = lax.axis_size("sx"), lax.axis_size("sy")
    devices = cols * rows
    capacity = max(2, 2 * obs_count // devices)
    edge = shape(realiz, size // 4, BF16)
    exact, padded = [shape(realiz, size // 4)] * 4, [shape(realiz + PAD, size // 4)] * 4
    half, whole = shape(realiz, size // 2), shape(realiz, size)
    first, message, last = (jax.ShapeDtypeStruct((devices, 1, rows_sent * LANES), F32) for rows_sent in (4, 5, 1))
    narrow, state_shape = shape(realiz, LANES), shape(8, LANES)
    coarse_state = shape(4 * devices, LANES)
    scratch_half = pltpu.VMEM((realiz, size // 2), BF16)
    flops = 2 * realiz * size * size
    schur_mat, inverse_mat = schur[0, 0], local_inverse[0, 0]

    packed, *coarse_mats = call(
        functools.partial(first_kernel, capacity, cols, rows),
        [shape(devices * capacity, LANES, BF16), *[shape(8, 4 * devices)] * 2],
        (obs_values.T, obs_dest.reshape(1, obs_count), obs_node.reshape(1, obs_count), coarse_inverse),
        [
            pltpu.VMEM((realiz, obs_count), BF16),
            *[pltpu.VMEM((1, obs_count), jnp.int32)] * 2,
            pltpu.VMEM(coarse_inverse.shape, F32),
            pltpu.SemaphoreType.DMA((4,)),
        ],
        COVER,
        pl.BlockSpec(memory_space=pltpu.HBM),
    )
    got = lax.all_to_all(packed.reshape(devices, capacity, LANES), AXES, split_axis=0, concat_axis=0, tiled=True)
    *image, e0, e1, e2, e3, sent = call(
        functools.partial(load_kernel, realiz),
        [half, half, *exact, first],
        (got.reshape(devices * capacity, LANES),),
        flops=COVER,
    )
    mode, olds, states = "load", ([], []), []
    for step in range(ITERS + 1):
        g, gathered = exchange((e0, e1, e2, e3)), gather(sent)
        ins = [*image, *[g[slot] for slot in (LOAD_ORDER if mode == "load" else ORDER)], gathered, *olds[0], *olds[1]]
        if step == ITERS:
            field, resid = call(last_kernel, [whole, whole], [*ins, states[0], z[0], *track[0], z[1], *track[1]])
            return field[None, None], resid[None, None]
        count, state_count = (1, 1) if mode == "load" else (2, 3)
        outs = call(
            functools.partial(step_kernel, mode),
            [*[half] * (2 * count), narrow, *[coarse_state, state_shape, coarse_state][:state_count], shape(realiz, size, BF16), half, edge, edge, narrow],
            [*ins, *states, *coarse_mats, inverse_mat],
            flops=flops // 2,
        )
        olds, (columns, coarse), outs = (outs[:count], outs[count : 2 * count]), outs[2 * count : 2 * count + 2], outs[2 * count + 2 :]
        states, outs = [*outs[:1], coarse, *outs[1:2]] if mode != "load" else [coarse], outs[state_count - 1 :]
        scaled, part_far, e2, e3, gamma = outs
        part_near, e0, e1, gamma = call(
            rest_kernel,
            [half, edge, edge, narrow],
            (columns, scaled, olds[0][0], olds[1][0], gamma, inverse_mat),
            flops=flops // 2,
        )
        g = exchange((e0, e1, e2, e3))
        if step == 0:
            track = (), ()
        else:
            outs = call(
                functools.partial(field_kernel, mode), [half] * 4, (columns, z[0], *track[0], z[1], *track[1]), flops=1
            )
            track = outs[:2], outs[2:]
        z_far, partial = call(
            image_far_kernel, [half, whole], (part_far, g[3], g[2], schur_mat), [scratch_half], flops // 2
        )
        z_near, *image, e0, e1, e2, e3, sent = call(
            image_near_kernel,
            [half, half, half, *([*exact, last] if step == ITERS - 1 else [*padded, message])],
            (part_near, g[0], g[1], z_far, partial, gamma, schur_mat, *track[0][:1]),
            [scratch_half],
            flops // 2,
        )
        z = z_near, z_far
        mode = "init" if step == 0 else "next"


def solution(mesh):
    placed = (
        P(AXES, None),
        P(AXES, None),
        P(AXES),
        P("sx", "sy", None, None),
        P("sx", "sy", None, None),
        P(AXES, None),
    )
    return jax.shard_map(
        body,
        mesh=mesh,
        in_specs=placed,
        out_specs=(P("sx", "sy", None, None), P("sx", "sy", None, None)),
        check_vma=False,
    )
```
